32 devices in a mesh: shard: 8 (over z, x), rep: 4 (over y, core).
Axes of the slice: x: 2, y: 2, z: 4, core: 2. Of those that a mesh axis runs over, the one named last changes fastest.
Arguments:
- tokens: bfloat16 [8, 1024, 1024], P('rep', 'shard'), may hold values from -6 to 6
- lengths: int32 [8], P('rep'), may hold values from 512 to 1024, as said below
- expert_ids: int32 [8, 1024, 2], P('rep', 'shard'), may hold values from 0 to 3, all different within a row
- buckets: int32 [2047], replicated, may hold values from 0 to 31
- norm1_gain: bfloat16 [1024], P('shard'), may hold values from 0.5 to 1.5
- w_query: bfloat16 [1024, 1024], P('shard'), may hold values from -0.1875 to 0.1875
- w_key: bfloat16 [1024, 1024], P('shard'), may hold values from -0.1875 to 0.1875
- w_value: bfloat16 [1024, 1024], P('shard'), may hold values from -0.1875 to 0.1875
- w_out: bfloat16 [1024, 1024], P('shard'), may hold values from -0.75 to 0.75
- rel_bias: bfloat16 [32, 16], P(None, 'shard'), may hold values from -4 to 4
- norm2_gain: bfloat16 [1024], P('shard'), may hold values from 0.5 to 1.5
- w_router: bfloat16 [1024, 4], P('shard'), may hold values from -0.125 to 0.125
- w_gate: bfloat16 [4, 2816, 1024], P(None, 'shard'), may hold values from -0.1875 to 0.1875
- w_up: bfloat16 [4, 2816, 1024], P(None, 'shard'), may hold values from -0.1875 to 0.1875
- w_down: bfloat16 [4, 2816, 1024], P(None, 'shard'), may hold values from -0.109375 to 0.109375
- cotangent: bfloat16 [8, 1024, 1024], P('rep', 'shard'), may hold values from -6 to 6
Outputs:
- block_out: bfloat16 [8, 1024, 1024], P('rep', 'shard')
- grad_tokens: float32 [8, 1024, 1024], P('rep', 'shard')
- grad_norm1_gain: float32 [1024], P('shard')
- grad_w_query: float32 [1024, 1024], P('shard')
- grad_w_key: float32 [1024, 1024], P('shard')
- grad_w_value: float32 [1024, 1024], P('shard')
- grad_w_out: float32 [1024, 1024], P('shard')
- grad_rel_bias: float32 [32, 16], P(None, 'shard')
- grad_norm2_gain: float32 [1024], P('shard')
- grad_w_router: float32 [1024, 4], P('shard')
- grad_w_gate: float32 [4, 2816, 1024], P(None, 'shard')
- grad_w_up: float32 [4, 2816, 1024], P(None, 'shard')
- grad_w_down: float32 [4, 2816, 1024], P(None, 'shard')
The draws below stay inside these ranges and needn't reach their ends.
Inputs may be any that keep to these rules, and one draw needn't show every extreme that they name: `lengths`: in every group of 2 consecutive sequences at least one has length 1024. `expert_ids`: the two experts of a position differ.
All inputs are finite; a program needn't handle non-finite values.
Results may differ from the reference program's by a relative error of at most 0.022.
Values may be sent and summed in bfloat16 or wider, within the bound.
No kernel may reach another device: no remote copies, remote signals or barrier semaphores. Data moves between devices by JAX's collectives and lax.ppermute only.
A program may use at most 320 MiB of HBM per device.

```python
import jax
import jax.numpy as jnp
from jax import lax

D = 1024
H = 16
DH = 64
FF = 2816
NB = 32
E = 4
SG = 2
LMAX = 1024
LB = 128
SEQS = 8
CAP = 160
N_SHARD = 8
N_REP = 4


def draw_lengths(key, part):
    pick_key, size_key = jax.random.split(key)
    group_count = SEQS // SG
    longest = jax.random.randint(pick_key, (group_count, 1), 0, SG)
    drawn_sizes = jax.random.randint(size_key, (group_count, SG), LMAX // 2, LMAX + 1)
    members = jnp.arange(SG)[None, :]
    return jnp.where(members == longest, LMAX, drawn_sizes).reshape(SEQS).astype(jnp.int32)


def draw_buckets(key, part):
    half_count = NB // 2
    exact_key, jitter_key = jax.random.split(key)
    exact_count = jax.random.randint(exact_key, (), 1, half_count)
    bucket_steps = jnp.arange(1, half_count, dtype=jnp.int32)
    base_bound = jnp.right_shift(jnp.int32(LMAX // 4), half_count - 1 - bucket_steps)
    jitter = jax.random.randint(jitter_key, (half_count - 1,), 0, base_bound // 2 + 1)
    bounds = jnp.where(bucket_steps <= exact_count, bucket_steps, jnp.maximum(base_bound + jitter, bucket_steps))
    bounds = lax.cummax(bounds, axis=0)
    offsets = jnp.arange(2 * LMAX - 1, dtype=jnp.int32) - (LMAX - 1)
    distance = jnp.abs(offsets)
    bucket_level = jnp.sum((distance[:, None] >= bounds[None, :]).astype(jnp.int32), axis=1)
    return (bucket_level + jnp.where(offsets > 0, half_count, 0)).astype(jnp.int32)


def block_levels(own_key, dims, pieces, least, top_value):
    def one(dim, blocks):
        heights = jax.random.uniform(jax.random.fold_in(jax.random.fold_in(own_key, 6), dim), (blocks,), jnp.float32, least / len(pieces), top_value / len(pieces))
        return jnp.repeat(jnp.exp(heights), dims[dim] // blocks).reshape((-1,) + (1,) * (len(dims) - dim - 1))

    loudness = one(*pieces[0])
    for cut in pieces[1:]:
        loudness = loudness * one(*cut)
    return loudness


def choose_distinct(rng, rows, amount, top, lift):
    ranking = jax.random.permutation(jax.random.fold_in(rng, 1), amount)
    favour = ranking
    for power in range(3):
        favour = favour * favour // amount
    favour = favour * lift // amount
    tickets = jax.random.randint(jax.random.fold_in(rng, 2), (rows, amount), 0, 4096) + favour
    fixed_rows = jax.random.permutation(jax.random.fold_in(rng, 3), rows)[jnp.arange(amount) % rows]
    tickets = jnp.where(jnp.arange(rows)[:, None] == fixed_rows[None, :], 1 << 14, tickets)
    score = tickets * amount + jnp.arange(amount)
    return lax.top_k(score.astype(jnp.int32), top)[1].astype(jnp.int32)


def gaussian(rng, shape, deviation, reach, cuts=(), held_as=jnp.bfloat16):
    values = jax.random.normal(rng, shape, jnp.float32) * deviation
    if len(cuts) > 0:
        values = block_levels(rng, shape, cuts, -0.22, 0.18) * values
    return jnp.clip(values, min=-reach, max=reach).astype(held_as)


def setup_inputs(seed: int = 0) -> dict:
    streams_of = jax.random.split(jax.random.key(seed), 17)
    return {
        "tokens": gaussian(streams_of[0], (SEQS, LMAX, D), 1.0, 6.0, ((0, 4), (1, 8))),
        "lengths": draw_lengths(jax.random.fold_in(streams_of[16], 71), 0),
        "expert_ids": choose_distinct(streams_of[2], SEQS * LMAX, E, 2, 4096).reshape((SEQS, LMAX, 2)),
        "buckets": draw_buckets(jax.random.fold_in(streams_of[16], 71), 0),
        "norm1_gain": jnp.clip(1.0 + 0.1 * jax.random.normal(streams_of[4], (D,), jnp.float32), 0.5, 1.5).astype(jnp.bfloat16),
        "w_query": gaussian(streams_of[5], (D, D), D ** -0.5, 0.1875, ((0, 8),)),
        "w_key": gaussian(streams_of[6], (D, D), D ** -0.5, 0.1875, ((0, 8),)),
        "w_value": gaussian(streams_of[7], (D, D), D ** -0.5, 0.1875, ((0, 8),)),
        "w_out": gaussian(streams_of[8], (D, D), (D // 16) ** -0.5, 0.75, ((0, 8),)),
        "rel_bias": gaussian(streams_of[9], (NB, H), 1.0, 4.0, ((1, 8),)),
        "norm2_gain": jnp.clip(1.0 + 0.1 * jax.random.normal(streams_of[10], (D,), jnp.float32), 0.5, 1.5).astype(jnp.bfloat16),
        "w_router": gaussian(streams_of[11], (D, E), (2 * D) ** -0.5, 0.125, ((0, 8),)),
        "w_gate": gaussian(streams_of[12], (E, FF, D), D ** -0.5, 0.1875, ((1, 8),)),
        "w_up": gaussian(streams_of[13], (E, FF, D), D ** -0.5, 0.1875, ((1, 8),)),
        "w_down": gaussian(streams_of[14], (E, FF, D), FF ** -0.5, 0.109375, ((1, 8),)),
        "cotangent": gaussian(streams_of[15], (SEQS, LMAX, D), 1.0, 6.0, ((0, 4), (1, 8))),
    }


highest = lax.Precision.HIGHEST
epsilon = 1e-06

@jax.custom_vjp
def low(v):
    return lax.optimization_barrier(v.astype(jnp.bfloat16)).astype(jnp.float32)

@jax.custom_vjp
def low_back(v):
    return v

def low_keep(v):
    return (low(v), None)

def low_pass(kept, grad):
    return (grad,)

def back_keep(v):
    return (v, None)

def back_low(kept, grad):
    return (low(grad),)
low.defvjp(low_keep, low_pass)
low_back.defvjp(back_keep, back_low)

def rms_norm(values, gain_vec):
    return values * lax.rsqrt(lax.optimization_barrier(jnp.mean(values * values, axis=-1, keepdims=True)) + epsilon) * gain_vec

def matmul(left_side, right_side):
    return jnp.dot(left_side, right_side, precision=highest)

def to_groups(stacked):
    shaped = stacked.reshape((N_REP, SG, N_SHARD, LB) + stacked.shape[1:])
    return jnp.swapaxes(shaped, 1, 2).reshape((N_REP * N_SHARD, SG * LB) + stacked.shape[1:])

def from_groups(stacked):
    shaped = stacked.reshape((N_REP, N_SHARD, SG, LB) + stacked.shape[2:])
    return jnp.swapaxes(shaped, 1, 2).reshape((N_REP * SG * LMAX,) + stacked.shape[2:])

def assign_slots(pair_ids, alive_pairs, expert_count, capacity):
    expert_range = jnp.arange(expert_count, dtype=jnp.int32)
    hit_table = (pair_ids[:, None] == expert_range[None, :]).astype(jnp.int32) * alive_pairs[:, None]
    earlier = jnp.cumsum(hit_table, axis=0, dtype=jnp.int32) - hit_table
    placing = lax.optimization_barrier(jnp.sum(earlier * hit_table, axis=1, dtype=jnp.int32))
    kept_mask = jnp.logical_and(alive_pairs > 0, placing < capacity)
    slot_index = jnp.where(kept_mask, pair_ids * capacity + placing, expert_count * capacity)
    return (slot_index.astype(jnp.int32), kept_mask)

def attend_sequence(seq_items, bias_vec):
    queries, keys_all, values_all, length = seq_items
    block_rows = min(512, LMAX)
    key_pos = jnp.arange(LMAX, dtype=jnp.int32)
    key_live = key_pos < length

    def one_block(block_index):
        first_row = block_index * block_rows
        query_rows = lax.dynamic_slice_in_dim(queries, first_row, block_rows, 0)
        product = jnp.einsum('qhd,khd->hqk', query_rows, keys_all, precision=highest) * DH ** (-0.5)
        product = low_back(product)
        row_pos = first_row + jnp.arange(block_rows, dtype=jnp.int32)
        offsets = key_pos[None, :] - row_pos[:, None] + (LMAX - 1)
        scores = product + jnp.take(bias_vec, offsets, axis=1)
        scores = jnp.where(key_live[None, None, :], scores, -1e+30)
        weights = low(jax.nn.softmax(scores, axis=-1))
        return jnp.einsum('hqk,khd->qhd', weights, values_all, precision=highest)
    blocks = lax.map(jax.checkpoint(one_block), jnp.arange(LMAX // block_rows, dtype=jnp.int32))
    return blocks.reshape(LMAX, H, DH)

def block_forward(tokens, norm1_gain, w_query, w_key, w_value, w_out, rel_bias, norm2_gain, w_router, w_gate, w_up, w_down, lengths, expert_ids, buckets):
    seq_count = tokens.shape[0]
    flat_count = seq_count * LMAX
    positions = jnp.arange(LMAX, dtype=jnp.int32)
    live_mask = (positions[None, :] < lengths[:, None]).reshape(flat_count)
    flat_tokens = tokens.reshape(flat_count, D)
    normed = low(rms_norm(flat_tokens, norm1_gain))

    def project(weight):
        return low(low_back(matmul(normed, weight))).reshape(seq_count, LMAX, H, DH)
    queries = project(w_query)
    keys_all = project(w_key)
    values_all = project(w_value)
    bias_vec = jnp.take(rel_bias, buckets, axis=0).T
    heads_out = lax.map(lambda seq_items: attend_sequence(seq_items, bias_vec), (queries, keys_all, values_all, lengths))
    context = low(low_back(heads_out.reshape(flat_count, D)))
    hidden_one = flat_tokens + low_back(matmul(context, w_out))
    mixed_norm = low(rms_norm(hidden_one, norm2_gain))
    router = jax.nn.softmax(low_back(matmul(mixed_norm, w_router)), axis=-1)
    flattened_indices = expert_ids.reshape(flat_count, 2)
    choose = (flattened_indices[:, :, None] == jnp.arange(E, dtype=jnp.int32)[None, None, :]).astype(jnp.float32)
    chosen = lax.optimization_barrier(jnp.sum(choose * router[:, None, :], axis=-1))
    gate_share = chosen / lax.optimization_barrier(jnp.sum(chosen, axis=-1, keepdims=True))

    def group_experts(group_items):
        group_rows, group_ids, group_gates, group_live = group_items
        tok_count = group_rows.shape[0]
        pair_ids = group_ids.reshape(-1)
        alive_pairs = jnp.repeat(group_live, 2)
        slot_index, kept_mask = assign_slots(pair_ids, alive_pairs, E, CAP)
        owners = jnp.zeros(E * CAP + 1, jnp.int32).at[slot_index].set(jnp.repeat(jnp.arange(tok_count, dtype=jnp.int32), 2))
        filled = jnp.zeros(E * CAP + 1, jnp.float32).at[slot_index].set(kept_mask.astype(jnp.float32))
        dispatched = jnp.take(group_rows, owners[:E * CAP], axis=0) * filled[:E * CAP, None]
        dispatched = dispatched.reshape(E, CAP, D)
        gate_in = low_back(jnp.einsum('ecd,efd->ecf', dispatched, w_gate, precision=highest))
        up_in = low_back(jnp.einsum('ecd,efd->ecf', dispatched, w_up, precision=highest))
        hidden_low = low(jax.nn.gelu(gate_in, approximate=True) * up_in)
        expert_out = low_back(jnp.einsum('ecf,efd->ecd', hidden_low, w_down, precision=highest))
        out_table = jnp.concatenate([expert_out.reshape(E * CAP, D), jnp.zeros((1, D), jnp.float32)], axis=0)
        picked = jnp.take(out_table, slot_index, axis=0).reshape(tok_count, 2, D)
        pair_scale = group_gates * kept_mask.reshape(tok_count, 2).astype(jnp.float32)
        return lax.optimization_barrier(jnp.sum(picked * pair_scale[:, :, None], axis=1))
    grouped = lax.map(jax.checkpoint(group_experts), (to_groups(mixed_norm), to_groups(flattened_indices), to_groups(gate_share), to_groups(live_mask.astype(jnp.int32))))
    expert_mix = from_groups(grouped)
    result = live_mask.astype(jnp.float32)[:, None] * (hidden_one + expert_mix)
    return result.reshape(seq_count, LMAX, D)

def reference(tokens, lengths, expert_ids, buckets, norm1_gain, w_query, w_key, w_value, w_out, rel_bias, norm2_gain, w_router, w_gate, w_up, w_down, cotangent):
    floats = [member.astype(jnp.float32) for member in (tokens, norm1_gain, w_query, w_key, w_value, w_out, rel_bias, norm2_gain, w_router, w_gate, w_up, w_down)]

    def forward(*members):
        return block_forward(*members, lengths, expert_ids, buckets)
    output, pull_back = jax.vjp(forward, *floats)
    gradients = pull_back(cotangent.astype(jnp.float32))
    return (output.astype(jnp.bfloat16), gradients[0], gradients[1], gradients[2], gradients[3], gradients[4], gradients[5], gradients[6], gradients[7], gradients[8], gradients[9], gradients[10], gradients[11])
```

```python
import functools

import jax
import jax.numpy as jnp
from jax import lax
from jax.experimental import pallas as pl
from jax.experimental.pallas import tpu as pltpu
from jax.sharding import PartitionSpec as P

epsilon = 1e-06
highest = lax.Precision.HIGHEST
bf16 = jnp.bfloat16
f32 = jnp.float32
vmem_limit = 58 * 1024 * 1024
whole_ref = pl.BlockSpec(memory_space=pltpu.VMEM)


def dot_nt(left, right):
    return lax.dot_general(left, right, (((1,), (1,)), ((), ())), preferred_element_type=f32)


def dot_tn(left, right):
    return lax.dot_general(left, right, (((0,), (0,)), ((), ())), preferred_element_type=f32)


def dot_nn(left, right):
    return lax.dot_general(left, right, (((1,), (0,)), ((), ())), preferred_element_type=f32)


def ring_index(place, count):
    return jnp.where(place < count // 2, 2 * place, 2 * count - 1 - 2 * place)


def ring_place(index, count):
    return jnp.where(index % 2 == 0, index // 2, count - 1 - index // 2)


def ring_send(value, step, count):
    order = [2 * i if i < count // 2 else 2 * count - 1 - 2 * i for i in range(count)]
    pairs = [(order[i], order[(i + step) % count]) for i in range(count)]
    return lax.ppermute(value, "shard", pairs)


def ring_gather(value, count):
    half = value.shape[0] // 2
    ahead = behind = value
    pieces = [(0, 0, value)]
    for step in range(1, count // 2):
        behind = ring_send(behind, 1, count)
        ahead = ring_send(ahead, -1, count)
        pieces += [(count - step, 0, behind), (step, 0, ahead)]
    far = count // 2
    pieces.append((far, 0, ring_send(behind[:half], 1, count)))
    pieces.append((far, half, ring_send(ahead[half:], -1, count)))
    return pieces


def pieces_in_order(pieces, count):
    out = [None] * count
    for distance, first, piece in pieces:
        if out[distance] is None:
            out[distance] = piece
        else:
            out[distance] = jnp.concatenate([out[distance], piece], axis=0)
    return out


def add_low(left, right):
    return (left.astype(f32) + right.astype(f32)).astype(bf16)


def ring_sum(chunk_of, count):
    far = chunk_of(count // 2)
    half = far.shape[0] // 2
    right = ring_send(far[:half], 1, count)
    left = ring_send(far[half:], -1, count)
    for step in range(count // 2 - 1, 0, -1):
        own_right, own_left = chunk_of(step), chunk_of(count - step)
        if right.shape[0] == half:
            right = jnp.concatenate([add_low(right, own_right[:half]), own_right[half:]], axis=0)
            left = jnp.concatenate([own_left[:half], add_low(left, own_left[half:])], axis=0)
        else:
            right = add_low(right, own_right)
            left = add_low(left, own_left)
        right = ring_send(right, 1, count)
        left = ring_send(left, -1, count)
    return right, left


def swap(value, axis, count, bit):
    return lax.ppermute(value, axis, [(i, i ^ bit) for i in range(count)])


def bits_of(count):
    return [1 << i for i in range(count.bit_length() - 1)]


def rep_scatter(value, count, me):
    for bit in bits_of(count):
        value = value.reshape((value.shape[0] // 2, 2) + value.shape[1:])
        side = (me // bit) % 2
        sent = lax.dynamic_index_in_dim(value, 1 - side, 1, keepdims=False)
        kept = lax.dynamic_index_in_dim(value, side, 1, keepdims=False)
        value = add_low(kept, swap(sent, "rep", count, bit))
    return value[0]


def rep_gather(value, count, me):
    value = value[None]
    for bit in bits_of(count)[::-1]:
        other = swap(value, "rep", count, bit)
        side = (me // bit) % 2
        low = jnp.where(side == 0, value, other)
        high = jnp.where(side == 0, other, value)
        value = jnp.stack([low, high], axis=1).reshape((2 * value.shape[0],) + value.shape[1:])
    return value


def rep_total(value, count, me):
    value = value.reshape((2, value.shape[0] // 2) + value.shape[1:])
    side = me % 2
    sent = lax.dynamic_index_in_dim(value, 1 - side, 0, keepdims=False)
    kept = lax.dynamic_index_in_dim(value, side, 0, keepdims=False)
    mine = add_low(kept, swap(sent, "rep", count, 1))
    for bit in bits_of(count)[1:]:
        mine = add_low(mine, swap(mine, "rep", count, bit))
    other = swap(mine, "rep", count, 1)
    low = jnp.where(side == 0, mine, other)
    high = jnp.where(side == 0, other, mine)
    return jnp.concatenate([low, high], axis=0).astype(f32)


def assign_slots(pair_ids, alive_pairs, expert_count, capacity):
    expert_range = jnp.arange(expert_count, dtype=jnp.int32)
    hit_table = (pair_ids[:, None] == expert_range[None, :]).astype(jnp.int32) * alive_pairs[
        :, None
    ]
    earlier = jnp.cumsum(hit_table, axis=0, dtype=jnp.int32) - hit_table
    placing = jnp.sum(earlier * hit_table, axis=1, dtype=jnp.int32)
    return jnp.logical_and(alive_pairs > 0, placing < capacity)


def toeplitz_rows(window, row_count, col_count):
    lead = window.shape[:-1]
    padded = jnp.concatenate([window, jnp.zeros(lead + (1,), window.dtype)], axis=-1)
    rolled = jnp.concatenate([padded[..., row_count - 1 :], padded[..., : row_count - 1]], axis=-1)
    period = row_count + col_count
    tiled = jnp.tile(rolled, (1,) * len(lead) + (row_count,))
    shaped = tiled[..., : row_count * (period - 1)].reshape(lead + (row_count, period - 1))
    return shaped[..., :col_count]


def diagonal_sums(table, row_count, col_count):
    lead = table.shape[:-2]
    period = row_count + col_count
    widened = jnp.concatenate(
        [table, jnp.zeros(lead + (row_count, row_count - 1), table.dtype)], axis=-1
    )
    flat = widened.reshape(lead + (row_count * (period - 1),))
    flat = jnp.concatenate(
        [
            jnp.zeros(lead + (row_count - 1,), table.dtype),
            flat,
            jnp.zeros(lead + (1,), table.dtype),
        ],
        axis=-1,
    )
    shaped = flat.reshape(lead + (row_count, period))
    return jnp.sum(shaped[..., : period - 1], axis=-2)


def attend_kernel(places, span, heads, head_size, meta, *refs):
    pieces, (weight, bias, tokens_out, qkv_out, context_out) = refs[: len(places)], refs[len(places) :]
    length = meta[0]
    seq_len = tokens_out.shape[0]
    blocks = seq_len // 128
    for (distance, first), piece in zip(places, pieces):
        rows = min(span - first, piece.shape[0])
        low = piece[0:rows, :]
        wide = low.astype(f32)
        factor = lax.rsqrt(jnp.mean(wide * wide, axis=-1, keepdims=True) + epsilon)
        made = dot_nn(low, weight[...]) * factor
        start = pl.multiple_of(meta[1 + distance] * span + first, 16)
        tokens_out[pl.ds(start, rows), :] = low
        for part in range(3 * heads):
            cut = made[:, part * head_size : (part + 1) * head_size]
            if part < heads:
                cut = cut.astype(bf16).astype(f32) * head_size ** (-0.5)
            qkv_out[part, pl.ds(start, rows), :] = cut.astype(bf16)
    for head in range(heads):
        keys = qkv_out[heads + head]
        values = qkv_out[2 * heads + head]
        for block in range(0, blocks, 2):
            queries = qkv_out[head, block * 128 : block * 128 + 256, :]
            scores = dot_nt(queries, keys)
            first_col = (blocks - 1 - block) * 128
            added = jnp.concatenate(
                [
                    bias[head, :, first_col : first_col + seq_len],
                    bias[head, :, first_col - 128 : first_col - 128 + seq_len],
                ],
                axis=0,
            )
            column = lax.broadcasted_iota(jnp.int32, scores.shape, 1)
            scores = jnp.where(column < length, scores + added, -1e30)
            top = jnp.max(scores, axis=-1, keepdims=True)
            weights = jnp.exp(scores - top)
            total = jnp.sum(weights, axis=-1, keepdims=True)
            mixed = dot_nn(weights.astype(bf16), values) / total
            context_out[
                block * 128 : block * 128 + 256, head * head_size : (head + 1) * head_size
            ] = mixed.astype(bf16)


def attend(meta, pieces, weight, bias, span, heads, head_size):
    width = weight.shape[0]
    seq_len = span * (meta.shape[0] - 2)
    places = [(distance, first) for distance, first, piece in pieces]
    return pl.pallas_call(
        functools.partial(attend_kernel, places, span, heads, head_size),
        out_shape=(
            jax.ShapeDtypeStruct((seq_len, width), bf16),
            jax.ShapeDtypeStruct((3 * heads, seq_len, head_size), bf16),
            jax.ShapeDtypeStruct((seq_len, heads * head_size), bf16),
        ),
        grid_spec=pltpu.PrefetchScalarGridSpec(
            num_scalar_prefetch=1,
            grid=(),
            in_specs=[whole_ref] * (len(pieces) + 2),
            out_specs=[whole_ref] * 3,
        ),
        compiler_params=pltpu.CompilerParams(vmem_limit_bytes=vmem_limit),
        cost_estimate=pl.CostEstimate(
            flops=20 * 10**9, bytes_accessed=8 * 10**6, transcendentals=heads * seq_len * seq_len
        ),
        name="attend",
    )(meta, *[piece for distance, first, piece in pieces], weight, bias)


def experts_kernel(count, span, expert_count, meta, tokens, *refs):
    context = refs[:count]
    (
        out_weight,
        gain,
        router_weight,
        codes,
        cotangent,
        gate_weight,
        up_weight,
        down_weight,
        context_out,
        normed_out,
        hidden_out,
        grad_gate_out,
        grad_up_out,
        mix_out,
        grad_out,
        heads_out,
        logits_out,
        gain_out,
    ) = refs[count:]
    rows, width = tokens.shape
    step = pl.program_id(0)
    length, me = meta[0], meta[meta.shape[0] - 1]
    row = step * rows + lax.broadcasted_iota(jnp.int32, (rows, 1), 0)
    own = jnp.logical_and(row >= me * span, row < (me + 1) * span)
    joined = jnp.concatenate([piece[...] for piece in context], axis=1)
    context_out[...] = joined
    hidden = tokens[...].astype(f32) + dot_nn(joined, out_weight[...])
    factor = lax.rsqrt(jnp.mean(hidden * hidden, axis=-1, keepdims=True) + epsilon)
    normed = (hidden * factor * gain[...]).astype(bf16)
    normed_out[...] = normed
    logits = dot_nn(normed, router_weight[...])
    lane = lax.broadcasted_iota(jnp.int32, logits.shape, 1)
    logits = jnp.where(lane < expert_count, logits, -1e30)
    router = jnp.exp(logits - jnp.max(logits, axis=-1, keepdims=True))
    router = router / jnp.sum(router, axis=-1, keepdims=True)
    code = codes[...]
    chosen = (code > 0.5).astype(f32)
    kept = (code > 1.5).astype(f32)
    pair_total = jnp.sum(router * chosen, axis=-1, keepdims=True)
    share = router * chosen / pair_total
    scale = share * kept
    upstream = jnp.where(row < length, cotangent[...].astype(f32), 0.0)
    upstream_low = upstream.astype(bf16)
    chunks, _, chunk = hidden_out.shape
    units = chunk * chunks // expert_count
    mix = jnp.zeros((rows, width), f32)
    grad = jnp.zeros((rows, width), f32)
    pair_grads = jnp.zeros(logits.shape, f32)
    column = lax.broadcasted_iota(jnp.int32, (rows, chunk), 1)
    root = 0.7978845608028654
    for part in range(chunks):
        cut = slice(part * chunk, (part + 1) * chunk)
        gate_in = dot_nt(normed, gate_weight[cut, :])
        up_in = dot_nt(normed, up_weight[cut, :])
        grad_hidden = dot_nt(upstream_low, down_weight[cut, :])
        square = gate_in * gate_in
        curve = jnp.tanh(root * gate_in * (1.0 + 0.044715 * square))
        rise = 0.5 + 0.5 * curve
        gelu = gate_in * rise
        slope = rise + 0.5 * gate_in * (1.0 - curve * curve) * (
            root + (3 * 0.044715 * root) * square
        )
        hidden_unit = gelu * up_in
        product = hidden_unit * grad_hidden
        per_chunk = chunk // units
        scales = scale[:, part * per_chunk : part * per_chunk + 1]
        for member in range(1, per_chunk):
            expert = part * per_chunk + member
            scales = jnp.where(column < member * units, scales, scale[:, expert : expert + 1])
        for member in range(per_chunk):
            expert = part * per_chunk + member
            inside = jnp.logical_and(column >= member * units, column < (member + 1) * units)
            pair_sum = jnp.sum(jnp.where(inside, product, 0.0), axis=-1, keepdims=True)
            pair_grads = jnp.where(lane == expert, pair_sum, pair_grads)
        scaled_grad = scales * grad_hidden
        hidden_low = (scales * hidden_unit).astype(bf16)
        grad_gate = (scaled_grad * up_in * slope).astype(bf16)
        grad_up = (scaled_grad * gelu).astype(bf16)
        hidden_out[part] = hidden_low
        grad_gate_out[part] = grad_gate
        grad_up_out[part] = grad_up
        mix = mix + dot_nn(hidden_low, down_weight[cut, :])
        grad = grad + dot_nn(grad_gate, gate_weight[cut, :])
        grad = grad + dot_nn(grad_up, up_weight[cut, :])
    mix_out[...] = (mix + jnp.where(own, hidden, 0.0)).astype(bf16)
    pair_grads = pair_grads * kept
    weighted = jnp.sum(pair_grads * share, axis=-1, keepdims=True)
    grad_router = chosen * (pair_grads - weighted) / pair_total
    grad_logits = router * (grad_router - jnp.sum(router * grad_router, axis=-1, keepdims=True))
    grad_logits = grad_logits.astype(bf16)
    logits_out[...] = grad_logits
    grad = grad + dot_nt(grad_logits, router_weight[...])
    spread = hidden * factor
    gain_part = jnp.sum(grad * spread, axis=0, keepdims=True)

    @pl.when(step == 0)
    def _():
        gain_out[...] = jnp.zeros_like(gain_out)

    gain_out[0:1, :] += gain_part
    grad = grad * gain[...]
    middle = jnp.mean(grad * hidden, axis=-1, keepdims=True) * (factor * factor)
    back = factor * grad - spread * middle + jnp.where(own, upstream, 0.0)
    back = back.astype(bf16)
    grad_out[...] = back
    grad_heads = dot_nt(back, out_weight[...]).astype(bf16)
    each = width // count
    for place in range(count):
        heads_out[place] = grad_heads[:, place * each : (place + 1) * each]


def experts(
    meta, tokens, context, out_weight, gain, router_weight, codes, cotangent, weights, span, expert_count
):
    seq_len, width = tokens.shape
    count = len(context)
    units = weights[0].shape[0]
    chunks = expert_count // 2
    chunk = units // chunks
    rows = 256
    by_row = lambda cols: pl.BlockSpec((rows, cols), lambda i, meta: (i, 0))
    fixed = lambda shape: pl.BlockSpec(
        shape, lambda i, meta: (0,) * len(shape), pipeline_mode=pl.Buffered(1)
    )
    by_chunk = pl.BlockSpec((chunks, rows, chunk), lambda i, meta: (0, i, 0))
    each = width // count
    low = lambda *shape: jax.ShapeDtypeStruct(shape, bf16)
    return pl.pallas_call(
        functools.partial(experts_kernel, count, span, expert_count),
        out_shape=(
            low(seq_len, width),
            low(seq_len, width),
            low(chunks, seq_len, chunk),
            low(chunks, seq_len, chunk),
            low(chunks, seq_len, chunk),
            low(seq_len, width),
            low(seq_len, width),
            low(count, seq_len, each),
            low(seq_len, 128),
            jax.ShapeDtypeStruct((8, width), f32),
        ),
        grid_spec=pltpu.PrefetchScalarGridSpec(
            num_scalar_prefetch=1,
            grid=(seq_len // rows,),
            in_specs=[by_row(width)]
            + [by_row(each)] * count
            + [
                fixed(out_weight.shape),
                fixed(gain.shape),
                fixed(router_weight.shape),
                by_row(128),
                by_row(width),
            ]
            + [fixed(weight.shape) for weight in weights],
            out_specs=(
                by_row(width),
                by_row(width),
                by_chunk,
                by_chunk,
                by_chunk,
                by_row(width),
                by_row(width),
                pl.BlockSpec((count, rows, each), lambda i, meta: (0, i, 0)),
                by_row(128),
                pl.BlockSpec((8, width), lambda i, meta: (0, 0)),
            ),
        ),
        compiler_params=pltpu.CompilerParams(vmem_limit_bytes=vmem_limit),
        cost_estimate=pl.CostEstimate(
            flops=2 * seq_len * width * (6 * units + 2 * width),
            bytes_accessed=40 * 10**6,
            transcendentals=seq_len * units,
        ),
        name="experts",
    )(meta, tokens, *context, out_weight, gain, router_weight, codes, cotangent, *weights)


def attend_back_kernel(
    heads,
    head_size,
    meta,
    tokens,
    qkv,
    grad_heads,
    weight,
    bias,
    grad_in,
    grad_out,
    parts_out,
    bias_out,
    gain_out,
    key_sum,
    value_sum,
    joined,
):
    length = meta[0]
    seq_len = tokens.shape[0]
    blocks = seq_len // 128
    width_heads = heads * head_size
    bias_out[...] = jnp.zeros_like(bias_out)
    for head in range(heads):
        keys = qkv[heads + head]
        values = qkv[2 * heads + head]
        lanes = slice(head * head_size, (head + 1) * head_size)
        for block in range(0, blocks, 2):
            span = slice(block * 128, block * 128 + 256)
            queries = qkv[head, span, :]
            grads = grad_heads[span, lanes]
            first_row = (blocks - 1 - block) * 128
            added = jnp.concatenate(
                [
                    bias[head, first_row : first_row + seq_len, :],
                    bias[head, first_row - 128 : first_row - 128 + seq_len, :],
                ],
                axis=1,
            )
            scores = dot_nt(keys, queries)
            row = lax.broadcasted_iota(jnp.int32, scores.shape, 0)
            scores = jnp.where(row < length, scores + added, -1e30)
            top = jnp.max(scores, axis=0, keepdims=True)
            probs = jnp.exp(scores - top)
            probs = probs * (1.0 / jnp.sum(probs, axis=0, keepdims=True))
            product = probs * dot_nt(values, grads)
            delta = jnp.sum(product, axis=0, keepdims=True)
            grad_scores = product - probs * delta
            bias_out[head, first_row : first_row + seq_len, :] += grad_scores[:, :128]
            bias_out[head, first_row - 128 : first_row - 128 + seq_len, :] += grad_scores[:, 128:]
            scores_low = grad_scores.astype(bf16)
            key_part = dot_nn(scores_low, queries)
            value_part = dot_nn(probs.astype(bf16), grads)
            if block == 0:
                key_sum[...] = key_part
                value_sum[...] = value_part
            else:
                key_sum[...] += key_part
                value_sum[...] += value_part
            query_grad = dot_tn(keys, scores_low) * head_size ** (-0.5)
            joined[span, lanes] = query_grad.T.astype(bf16)
        joined[:, width_heads + head * head_size : width_heads + (head + 1) * head_size] = key_sum[
            ...
        ].astype(bf16)
        joined[
            :, 2 * width_heads + head * head_size : 2 * width_heads + (head + 1) * head_size
        ] = value_sum[...].astype(bf16)
    gain_out[...] = jnp.zeros_like(gain_out)
    for block in range(0, seq_len, 256):
        span = slice(block, block + 256)
        low = joined[span, :]
        wide = tokens[span, :].astype(f32)
        factor = lax.rsqrt(jnp.mean(wide * wide, axis=-1, keepdims=True) + epsilon)
        upstream = dot_nt(low, weight[...])
        spread = wide * factor
        gain_out[0:1, :] += jnp.sum(upstream * spread, axis=0, keepdims=True)
        middle = jnp.mean(upstream * wide, axis=-1, keepdims=True) * (factor * factor)
        back = factor * upstream - spread * middle + grad_in[span, :].astype(f32)
        grad_out[span, :] = back.astype(bf16)
        parts_out[span, :] = (low.astype(f32) * factor).astype(bf16)


def attend_back(meta, tokens, qkv, grad_heads, weight, bias, grad_in, heads, head_size):
    seq_len, width = tokens.shape
    return pl.pallas_call(
        functools.partial(attend_back_kernel, heads, head_size),
        out_shape=(
            jax.ShapeDtypeStruct((seq_len, width), bf16),
            jax.ShapeDtypeStruct((seq_len, 3 * heads * head_size), bf16),
            jax.ShapeDtypeStruct(bias.shape, f32),
            jax.ShapeDtypeStruct((8, width), f32),
        ),
        grid_spec=pltpu.PrefetchScalarGridSpec(
            num_scalar_prefetch=1,
            grid=(),
            in_specs=[whole_ref] * 6,
            out_specs=[whole_ref] * 4,
            scratch_shapes=[
                pltpu.VMEM((seq_len, head_size), f32),
                pltpu.VMEM((seq_len, head_size), f32),
                pltpu.VMEM((seq_len, 3 * heads * head_size), bf16),
            ],
        ),
        compiler_params=pltpu.CompilerParams(vmem_limit_bytes=vmem_limit),
        cost_estimate=pl.CostEstimate(
            flops=30 * 10**9, bytes_accessed=12 * 10**6, transcendentals=heads * seq_len * seq_len
        ),
        name="attend_back",
    )(meta, tokens, qkv, grad_heads, weight, bias, grad_in)


def body(
    tokens,
    lengths,
    expert_ids,
    buckets,
    norm1_gain,
    w_query,
    w_key,
    w_value,
    w_out,
    rel_bias,
    norm2_gain,
    w_router,
    w_gate,
    w_up,
    w_down,
    cotangent,
):
    seqs, span, width = tokens.shape
    count = lax.axis_size("shard")
    reps = lax.axis_size("rep")
    me = lax.axis_index("shard")
    rep = lax.axis_index("rep")
    seq_len = span * count
    expert_count, unit_count, _ = w_gate.shape
    heads = rel_bias.shape[1]
    head_size = w_query.shape[1] // (count * heads)
    each = heads * head_size
    feats = w_query.shape[0]
    cut = feats // reps
    row_count = seqs * span
    capacity = 10 * row_count // (4 * expert_count)
    place = ring_place(me, count)
    distances = jnp.arange(count, dtype=jnp.int32)
    owners = ring_index((place + distances) % count, count)
    distance_of = (ring_place(distances, count) - place) % count
    metas = [
        jnp.concatenate([lengths[s : s + 1], owners, me[None]]).astype(jnp.int32)
        for s in range(seqs)
    ]

    token_pieces = [ring_gather(tokens[0], count)]
    gain_one = norm1_gain.astype(f32)
    own_qkv = jnp.stack([w_query, w_key, w_value], axis=1)
    own_cut = lax.dynamic_slice_in_dim(own_qkv, rep * cut, cut, 0).astype(f32)
    own_cut = own_cut * lax.dynamic_slice_in_dim(gain_one, rep * cut, cut, 0)[:, None, None]
    own_cut = own_cut.astype(bf16).reshape(cut, 3, count, each).transpose(2, 0, 1, 3)
    qkv_weight = lax.all_to_all(
        own_cut.reshape(count, cut, 3 * each), "shard", split_axis=0, concat_axis=0, tiled=True
    )
    qkv_weight = rep_gather(qkv_weight, reps, rep).transpose(1, 0, 2, 3).reshape(width, 3 * each)

    positions = me * span + jnp.arange(span, dtype=jnp.int32)
    live_mask = positions[None, :] < lengths[:, None]
    pair_ids = expert_ids.reshape(row_count, 2)
    kept = assign_slots(
        pair_ids.reshape(-1),
        jnp.repeat(live_mask.reshape(row_count).astype(jnp.int32), 2),
        expert_count,
        capacity,
    ).reshape(row_count, 2)
    choose = pair_ids[:, :, None] == jnp.arange(expert_count, dtype=jnp.int32)[None, None, :]
    code = jnp.sum(choose.astype(f32) * (1.0 + kept.astype(f32))[:, :, None], axis=1)

    def line(values):
        flat = values.reshape(-1).astype(bf16)
        return jnp.pad(flat, (0, width - flat.shape[0]))[None]

    extras = jnp.concatenate(
        [
            line(code),
            line(jnp.concatenate([norm2_gain, w_router.reshape(-1)])),
            jnp.zeros((14, width), bf16),
        ],
        axis=0,
    )
    out_cut = lax.dynamic_slice_in_dim(w_out, rep * cut, cut, 0)
    packed = jnp.concatenate([tokens[1], out_cut, extras], axis=0)
    packed_pieces = ring_gather(packed, count)
    packed_list = pieces_in_order(packed_pieces, count)
    token_pieces.append([(d, 0, piece) for d, piece in enumerate(packed_list)])
    out_parts = jnp.stack([piece[span : span + cut] for piece in packed_list])
    out_weight = rep_gather(out_parts, reps, rep).transpose(1, 0, 2, 3).reshape(width, width)
    small = jnp.stack([piece[span + cut : span + cut + 2] for piece in packed_list])
    small = jnp.take(small, distance_of, axis=0)
    codes = small[:, 0, : row_count * expert_count].astype(f32)
    codes = codes.reshape(count, seqs, span, expert_count).transpose(1, 0, 2, 3)
    codes = codes.reshape(seqs, seq_len, expert_count)
    codes = jnp.pad(codes, ((0, 0), (0, 0), (0, 128 - expert_count)))
    gain_two = small[:, 1, :feats].astype(f32).reshape(1, width)
    router_weight = small[:, 1, feats : feats * (1 + expert_count)].reshape(width, expert_count)
    router_weight = jnp.pad(router_weight, ((0, 0), (0, 128 - expert_count)))

    bucket_count = rel_bias.shape[0]
    bucket_hot = (
        buckets[:, None] == jnp.arange(bucket_count, dtype=jnp.int32)[None, :]
    ).astype(f32)
    bias_vec = jnp.einsum("rb,bh->hr", bucket_hot, rel_bias.astype(f32), precision=highest)
    bias_width = 2 * seq_len - 128
    bias = toeplitz_rows(bias_vec, 128, bias_width)
    bias_turned = jnp.swapaxes(bias, 1, 2)

    cot_all = []
    for s in range(seqs):
        pieces = pieces_in_order(ring_gather(cotangent[s], count), count)
        joined = jnp.take(jnp.stack(pieces), distance_of, axis=0)
        cot_all.append(joined.reshape(seq_len, width))
    expert_weights = [
        weight.reshape(expert_count * unit_count, width) for weight in (w_gate, w_up, w_down)
    ]
    token_all, qkv_all, context_all = [], [], []
    for s in range(seqs):
        token_rows, qkv, context = attend(
            metas[s], token_pieces[s], qkv_weight, bias, span, heads, head_size
        )
        token_all.append(token_rows)
        qkv_all.append(qkv)
        context_all.append(pieces_in_order(ring_gather(context, count), count))
    results = []
    for s in range(seqs):
        results.append(
            experts(
                metas[s],
                token_all[s],
                context_all[s],
                out_weight,
                gain_two,
                router_weight,
                codes[s],
                cot_all[s],
                expert_weights,
                span,
                expert_count,
            )
        )
    grad_head_all = []
    for s in range(seqs):
        heads_part = results[s][7]
        right, left = ring_sum(lambda d: heads_part[d], count)
        total = heads_part[0].astype(f32) + right.astype(f32) + left.astype(f32)
        grad_head_all.append(total.astype(bf16))
    mix_parts = [result[5] for result in results]

    def rows_of(parts, distance):
        start = owners[distance] * span
        return [lax.dynamic_slice_in_dim(part, start, span, 0) for part in parts]

    right, left = ring_sum(lambda d: jnp.concatenate(rows_of(mix_parts, d), axis=0), count)
    mix_own = jnp.concatenate(rows_of(mix_parts, 0), axis=0).astype(f32)
    mix_own = mix_own + right.astype(f32) + left.astype(f32)
    block_out = (live_mask.reshape(row_count, 1).astype(f32) * mix_own).astype(bf16)
    block_out = block_out.reshape(seqs, span, width)

    def weight_grad(spots, sides):
        total = sum(
            jnp.einsum("clf,ld->cfd", results[s][spots], sides[s], preferred_element_type=f32)
            for s in range(seqs)
        )
        total = total.astype(bf16).reshape(expert_count * unit_count, width)
        return rep_total(total, reps, rep).reshape(expert_count, unit_count, width)

    normed_all = [result[1] for result in results]
    total_down = weight_grad(2, cot_all)
    total_gate = weight_grad(3, normed_all)
    total_up = weight_grad(4, normed_all)

    out_grad = sum(
        jnp.einsum("lc,ld->cd", results[s][0], results[s][6], preferred_element_type=f32)
        for s in range(seqs)
    ).astype(bf16)
    out_grad = out_grad.reshape(count, reps, cut, width)
    out_grad = rep_scatter(out_grad.transpose(1, 0, 2, 3), reps, rep)
    right, left = ring_sum(lambda d: out_grad[d], count)
    out_grad = add_low(out_grad[0].astype(f32) + right.astype(f32), left)
    total_out = rep_gather(out_grad, reps, rep).reshape(feats, width).astype(f32)

    backs = [
        attend_back(
            metas[s],
            token_all[s],
            qkv_all[s],
            grad_head_all[s],
            qkv_weight,
            bias_turned,
            results[s][6],
            heads,
            head_size,
        )
        for s in range(seqs)
    ]
    grad_tokens = []
    for s in range(seqs):
        grads = backs[s][0]
        right, left = ring_sum(lambda d: rows_of([grads], d)[0], count)
        own = rows_of([grads], 0)[0].astype(f32)
        grad_tokens.append(own + right.astype(f32) + left.astype(f32))
    grad_tokens = jnp.stack(grad_tokens)

    qkv_grad = sum(
        jnp.einsum("ld,lc->dc", token_all[s], backs[s][1], preferred_element_type=f32)
        for s in range(seqs)
    ).astype(bf16)
    qkv_grad = qkv_grad.reshape(count, reps, cut, 3 * each).transpose(1, 0, 2, 3)
    qkv_grad = rep_scatter(qkv_grad, reps, rep)
    qkv_grad = lax.all_to_all(qkv_grad, "shard", split_axis=0, concat_axis=0, tiled=True)
    qkv_grad = rep_gather(qkv_grad, reps, rep)
    qkv_grad = qkv_grad.reshape(reps, count, cut, 3, each).transpose(3, 0, 2, 1, 4)
    qkv_grad = qkv_grad.reshape(3, feats, width).astype(f32) * gain_one[None, :, None]

    router_grad = sum(
        jnp.einsum("ld,le->de", normed_all[s], results[s][8], preferred_element_type=f32)
        for s in range(seqs)
    )[:, :expert_count]
    gain_two_grad = sum(result[9][0] for result in results)
    gain_one_grad = sum(back[3][0] for back in backs)
    table = jnp.swapaxes(sum(back[2] for back in backs), 1, 2)
    offset_sums = diagonal_sums(table, 128, bias_width)
    bias_grad = jnp.einsum("hr,rb->bh", offset_sums, bucket_hot, precision=highest)
    bias_size = bucket_count * heads
    flat = jnp.concatenate(
        [
            gain_one_grad.reshape(count, feats),
            gain_two_grad.reshape(count, feats),
            router_grad.reshape(count, feats * expert_count),
        ],
        axis=1,
    ).reshape(-1)
    flat = jnp.concatenate([flat, bias_grad.reshape(-1)])
    for bit in bits_of(reps):
        flat = flat + swap(flat, "rep", reps, bit)
    total_bias = flat[-bias_size:].reshape(bucket_count, heads)
    flat = flat[:-bias_size]
    for bit in bits_of(count):
        flat = flat + swap(flat, "shard", count, bit)
    flat = lax.dynamic_index_in_dim(flat.reshape(count, -1), me, 0, keepdims=False)
    total_gain_one = flat[:feats] / gain_one
    total_gain_two = flat[feats : 2 * feats]
    total_router = flat[2 * feats :].reshape(feats, expert_count)
    return (
        block_out,
        grad_tokens,
        total_gain_one,
        qkv_grad[0],
        qkv_grad[1],
        qkv_grad[2],
        total_out,
        total_bias,
        total_gain_two,
        total_router,
        total_gate,
        total_up,
        total_down,
    )


def solution(mesh):
    rows = P("rep", "shard", None)
    first = P("shard")
    weight = P("shard", None)
    expert = P(None, "shard", None)
    return jax.shard_map(
        body,
        mesh=mesh,
        in_specs=(rows, P("rep"), rows, P(), first, weight, weight, weight, weight)
        + (P(None, "shard"), first, weight, expert, expert, expert, rows),
        out_specs=(rows, rows, first, weight, weight, weight, weight)
        + (P(None, "shard"), first, weight, expert, expert, expert),
        check_vma=False,
    )
```

```python
import functools

import jax
import jax.numpy as jnp
from jax import lax
from jax.experimental import pallas as pl
from jax.experimental.pallas import tpu as pltpu
from jax.sharding import PartitionSpec as P

epsilon = 1e-06
highest = lax.Precision.HIGHEST
bf16 = jnp.bfloat16
f32 = jnp.float32
vmem_limit = 58 * 1024 * 1024
whole_ref = pl.BlockSpec(memory_space=pltpu.VMEM)


def dot_nt(left, right):
    return lax.dot_general(left, right, (((1,), (1,)), ((), ())), preferred_element_type=f32)


def dot_tn(left, right):
    return lax.dot_general(left, right, (((0,), (0,)), ((), ())), preferred_element_type=f32)


def dot_nn(left, right):
    return lax.dot_general(left, right, (((1,), (0,)), ((), ())), preferred_element_type=f32)


def ring_index(place, count):
    return jnp.where(place < count // 2, 2 * place, 2 * count - 1 - 2 * place)


def ring_place(index, count):
    return jnp.where(index % 2 == 0, index // 2, count - 1 - index // 2)


def ring_send(value, step, count):
    order = [2 * i if i < count // 2 else 2 * count - 1 - 2 * i for i in range(count)]
    pairs = [(order[i], order[(i + step) % count]) for i in range(count)]
    return lax.ppermute(value, "shard", pairs)


def after(value, *waits):
    if not jax.tree.leaves(waits):
        return value
    flat, tree = jax.tree.flatten(value)
    held = lax.optimization_barrier(tuple(flat) + tuple(jax.tree.leaves(waits)))
    return tree.unflatten(held[: len(flat)])


def halve(value):
    half = value.shape[0] // 2
    return value[:half], value[half:]


class Gather:
    def __init__(self, value, count, split=None):
        self.count, self.step, self.split = count, 1, split or halve
        self.ahead = self.behind = value
        self.pieces = [(0, None, value)]
        self.done = False

    def hop(self, *waits):
        behind, ahead = after((self.behind, self.ahead), *waits)
        far = self.count // 2
        if self.step < far:
            self.behind = ring_send(behind, 1, self.count)
            self.ahead = ring_send(ahead, -1, self.count)
            self.pieces += [(self.count - self.step, None, self.behind), (self.step, None, self.ahead)]
            self.step += 1
        else:
            self.behind = ring_send(self.split(behind)[0], 1, self.count)
            self.ahead = ring_send(self.split(ahead)[1], -1, self.count)
            self.pieces += [(far, 0, self.behind), (far, 1, self.ahead)]
            self.done = True

    def last(self):
        return (self.behind, self.ahead)


def add_low(left, right):
    return (left.astype(f32) + right.astype(f32)).astype(bf16)


class Sum:
    def __init__(self, chunk_of, count):
        self.chunk_of, self.count, self.step = chunk_of, count, count // 2
        self.right = self.left = None
        self.done = False

    def hop(self, *waits):
        if self.right is None:
            far = self.chunk_of(self.step)
            self.half = far.shape[0] // 2
            right, left = far[: self.half], far[self.half :]
        else:
            own_right, own_left = self.chunk_of(self.step), self.chunk_of(self.count - self.step)
            right, left = self.right, self.left
            half = self.half
            if right.shape[0] == half:
                right = jnp.concatenate([add_low(right, own_right[:half]), own_right[half:]], axis=0)
                left = jnp.concatenate([own_left[:half], add_low(left, own_left[half:])], axis=0)
            else:
                right = add_low(right, own_right)
                left = add_low(left, own_left)
        right, left = after((right, left), *waits)
        self.right = ring_send(right, 1, self.count)
        self.left = ring_send(left, -1, self.count)
        self.step -= 1
        self.done = self.step == 0

    def last(self):
        return (self.right, self.left)


def fire(rings, *waits):
    rings = [ring for ring in rings if not ring.done]
    waits = waits + tuple(ring.last() for ring in rings if ring.last()[0] is not None)
    for ring in rings:
        ring.hop(*waits)


def lasts(rings):
    return tuple(ring.last() for ring in rings)


def swap(value, axis, count, bit):
    return lax.ppermute(value, axis, [(i, i ^ bit) for i in range(count)])


def bits_of(count):
    return [1 << i for i in range(count.bit_length() - 1)]


def rep_scatter(value, count, me):
    for bit in bits_of(count):
        value = value.reshape((value.shape[0] // 2, 2) + value.shape[1:])
        side = (me // bit) % 2
        sent = lax.dynamic_index_in_dim(value, 1 - side, 1, keepdims=False)
        kept = lax.dynamic_index_in_dim(value, side, 1, keepdims=False)
        value = add_low(kept, swap(sent, "rep", count, bit))
    return value[0]


def rep_gather(value, count, me):
    value = value[None]
    for bit in bits_of(count)[::-1]:
        other = swap(value, "rep", count, bit)
        side = (me // bit) % 2
        low = jnp.where(side == 0, value, other)
        high = jnp.where(side == 0, other, value)
        value = jnp.stack([low, high], axis=1).reshape((2 * value.shape[0],) + value.shape[1:])
    return value


def widen_kernel(parts, meta, kept, got, kept_other, got_other, out, *scratch):
    held, wide, in_sems, out_sems = scratch
    half = kept.shape[0]
    rows = half // parts
    sources = (kept, got, kept_other, got_other)
    ins = [
        [
            pltpu.make_async_copy(
                source.at[pl.ds(part * rows, rows), :],
                held.at[number, pl.ds(part * rows, rows), :],
                in_sems.at[number * parts + part],
            )
            for number, source in enumerate(sources)
        ]
        for part in range(parts)
    ]
    for part in range(parts):
        for copy in ins[part]:
            copy.start()
    outs = []
    for part in range(parts):
        for copy in ins[part]:
            copy.wait()
        at = slice(part * rows, (part + 1) * rows)
        for pair in range(2):
            total = held[2 * pair, at, :].astype(f32) + held[2 * pair + 1, at, :].astype(f32)
            wide[pair, at, :] = total
            side = meta[0] if pair == 0 else 1 - meta[0]
            start = pl.multiple_of(side * half + part * rows, 8)
            outs.append(
                pltpu.make_async_copy(
                    wide.at[pair, pl.ds(part * rows, rows), :],
                    out.at[pl.ds(start, rows), :],
                    out_sems.at[pair * parts + part],
                )
            )
            outs[-1].start()
    for copy in outs:
        copy.wait()


def widen(side, kept, got, kept_other, got_other):
    half, width = kept.shape
    parts = 4 if half % 64 == 0 else 2 if half % 32 == 0 else 1
    anywhere = pl.BlockSpec(memory_space=pl.ANY)
    return pl.pallas_call(
        functools.partial(widen_kernel, parts),
        out_shape=jax.ShapeDtypeStruct((2 * half, width), f32),
        in_specs=[pl.BlockSpec(memory_space=pltpu.SMEM)] + [anywhere] * 4,
        out_specs=anywhere,
        scratch_shapes=[
            pltpu.VMEM((4, half, width), bf16),
            pltpu.VMEM((2, half, width), f32),
            pltpu.SemaphoreType.DMA((4 * parts,)),
            pltpu.SemaphoreType.DMA((2 * parts,)),
        ],
        compiler_params=pltpu.CompilerParams(vmem_limit_bytes=16 * 2**20),
        name="widen",
    )(side, kept, got, kept_other, got_other)


class RepTotal:
    def __init__(self, value, count, me):
        self.count, self.side = count, me % 2
        value = value.reshape((2, value.shape[0] // 2) + value.shape[1:])
        sent = lax.dynamic_index_in_dim(value, 1 - self.side, 0, keepdims=False)
        self.kept = lax.dynamic_index_in_dim(value, self.side, 0, keepdims=False)
        self.got = swap(sent, "rep", count, 1)

    def cross(self, *waits):
        kept = add_low(self.kept, self.got)
        for bit in bits_of(self.count)[1:-1]:
            kept = add_low(kept, swap(kept, "rep", self.count, bit))
        self.kept = after(kept, *waits)
        self.got = swap(self.kept, "rep", self.count, self.count // 2)
        self.kept_other = swap(self.kept, "rep", self.count, 1)

    def finish(self):
        got_other = swap(self.got, "rep", self.count, 1)
        side = self.side.reshape(1).astype(jnp.int32)
        return widen(side, self.kept, self.got, self.kept_other, got_other)


def bias_kernel(vec, table, turned):
    heads, _, width = table.shape
    for head in range(heads):
        line = jnp.broadcast_to(vec[head : head + 1, :], (128, vec.shape[1]))
        line = pltpu.roll(line, vec.shape[1] - 127, 1, stride=1, stride_axis=0)
        table[head] = line[:, :width]
        for first in range(0, width, 128):
            turned[head, first : first + 128, :] = line[:, first : first + 128].T


def bias_tables(vec):
    heads, length = vec.shape
    width = length - 128
    return pl.pallas_call(
        bias_kernel,
        out_shape=(
            jax.ShapeDtypeStruct((heads, 128, width), f32),
            jax.ShapeDtypeStruct((heads, width, 128), f32),
        ),
        in_specs=[whole_ref],
        out_specs=[whole_ref] * 2,
        compiler_params=pltpu.CompilerParams(vmem_limit_bytes=24 * 2**20),
        name="bias_tables",
    )(vec)


def attend_kernel(seq, seqs, places, heads, head_size, meta, *refs):
    pieces = refs[: len(places)]
    cotangent, weight, bias, tokens_out, qkv_out, mixed_out, sems = refs[len(places) :]
    length = meta[seq]
    span = cotangent.shape[0]
    seq_len = tokens_out.shape[0]
    each = heads * head_size
    blocks = seq_len // 128
    copies = []
    for number, ((distance, first), piece) in enumerate(zip(places, pieces)):
        start = pl.multiple_of(meta[seqs + distance] * span, 16)
        copies.append(
            pltpu.make_async_copy(
                piece.at[pl.ds(first, span), :],
                tokens_out.at[pl.ds(start, span), :],
                sems.at[number],
            )
        )
        copies[-1].start()
    mixed_out[0:span, :] = cotangent[...]
    for copy in copies:
        copy.wait()
    for first in range(0, seq_len, 256):
        rows = slice(first, first + 256)
        low = tokens_out[rows, :]
        wide = low.astype(f32)
        factor = lax.rsqrt(jnp.mean(wide * wide, axis=-1, keepdims=True) + epsilon)
        made = dot_nn(low, weight[...]) * factor
        for part in range(3 * heads):
            cut = made[:, part * head_size : (part + 1) * head_size]
            if part < heads:
                cut = cut.astype(bf16).astype(f32) * head_size ** (-0.5)
            qkv_out[part, rows, :] = cut.astype(bf16)
    for head in range(heads):
        keys = qkv_out[heads + head]
        values = qkv_out[2 * heads + head]
        for block in range(0, blocks, 2):
            queries = qkv_out[head, block * 128 : block * 128 + 256, :]
            scores = dot_nt(queries, keys)
            first_col = (blocks - 1 - block) * 128
            added = jnp.concatenate(
                [
                    bias[head, :, first_col : first_col + seq_len],
                    bias[head, :, first_col - 128 : first_col - 128 + seq_len],
                ],
                axis=0,
            )
            column = lax.broadcasted_iota(jnp.int32, scores.shape, 1)
            scores = jnp.where(column < length, scores + added, -1e30)
            top = jnp.max(scores, axis=-1, keepdims=True)
            weights = jnp.exp(scores - top)
            total = jnp.sum(weights, axis=-1, keepdims=True)
            mixed = dot_nn(weights.astype(bf16), values) / total
            mixed = mixed.astype(bf16)
            for part in range(256 // span):
                lane = (block * 128 // span + part) * each + head * head_size
                mixed_out[span : 2 * span, lane : lane + head_size] = mixed[
                    part * span : (part + 1) * span, :
                ]


def attend(meta, seq, seqs, pieces, cotangent, weight, bias, heads, head_size):
    width = weight.shape[0]
    span = cotangent.shape[0]
    pieces = [(d, half, piece) for d, half, piece in pieces if half is None or half == seq]
    places = [(d, seq * span if half is None else 0) for d, half, piece in pieces]
    seq_len = span * len(pieces)
    full = lambda *shape: pl.BlockSpec(shape, lambda i, meta: (0,) * len(shape))
    shapes = ((seq_len, width), (3 * heads, seq_len, head_size), (2 * span, width))
    return pl.pallas_call(
        functools.partial(attend_kernel, seq, seqs, places, heads, head_size),
        out_shape=tuple(jax.ShapeDtypeStruct(shape, bf16) for shape in shapes),
        grid_spec=pltpu.PrefetchScalarGridSpec(
            num_scalar_prefetch=1,
            grid=(1,),
            in_specs=[pl.BlockSpec(memory_space=pl.ANY)] * len(pieces)
            + [full(*cotangent.shape), full(*weight.shape), full(*bias.shape)],
            out_specs=[full(*shape) for shape in shapes],
            scratch_shapes=[pltpu.SemaphoreType.DMA((len(pieces),))],
        ),
        compiler_params=pltpu.CompilerParams(vmem_limit_bytes=28 * 2**20),
        cost_estimate=pl.CostEstimate(
            flops=8 * 10**9, bytes_accessed=8 * 10**6, transcendentals=heads * seq_len * seq_len
        ),
        name="attend",
    )(meta, *[piece for d, half, piece in pieces], cotangent, weight, bias)


def experts_kernel(static, meta, *refs):
    count, span, seqs, expert_count, capacity, seq, block, kinds, alias_count = static
    tokens_hbm, *pieces = refs[: 1 + len(kinds)]
    refs = refs[1 + len(kinds) :]
    gain, router_weight, ids, gain_in, out_weight, gate_weight, up_weight, down_weight = refs[:8]
    refs = refs[8 + alias_count :]
    buffers, sums_out, gain_out, refs = refs[:8], refs[8], refs[9], refs[10:]
    staged, refs = refs[:8], refs[8:]
    heads_out, mix_out, tokens, context, sems, in_sems = refs
    (
        context_out,
        normed_out,
        cotangent,
        hidden_out,
        grad_gate_out,
        grad_up_out,
        grad_out,
        logits_out,
    ) = staged
    rows, width = tokens.shape
    each = width // count
    seq_len = span * count
    at_row = seq * seq_len + block * rows
    members = rows // span
    length, me = meta[seq], meta[meta.shape[0] - 1]

    tokens_copy = pltpu.make_async_copy(
        tokens_hbm.at[pl.ds(block * rows, rows), :], tokens, in_sems.at[0]
    )
    tokens_copy.start()
    lanes = pl.ds(block * members * each, members * each)
    context_copies, cotangent_copies = [], []
    for number, ((distance, half), piece) in enumerate(zip(kinds, pieces)):
        if half != 0:
            first = span if half is None else 0
            context_copies.append(
                pltpu.make_async_copy(
                    piece.at[pl.ds(first, span), lanes],
                    context.at[distance],
                    in_sems.at[1 + 2 * number],
                )
            )
            context_copies[-1].start()
    for number, ((distance, half), piece) in enumerate(zip(kinds, pieces)):
        if half != 1:
            owner = meta[seqs + distance]
            inside = owner // members == block
            start = pl.multiple_of(
                jnp.where(inside, owner - block * members, 0) * span, 16
            )
            copy = pltpu.make_async_copy(
                piece.at[pl.ds(0, span), :],
                cotangent.at[pl.ds(start, span), :],
                in_sems.at[2 + 2 * number],
            )
            pl.when(inside)(copy.start)
            cotangent_copies.append((inside, copy))

    copies = [
        pltpu.make_async_copy(source, target.at[pl.ds(at_row, rows), :], sems.at[number])
        for number, (source, target) in enumerate(zip(staged, buffers))
    ]
    heads_copy = pltpu.make_async_copy(
        heads_out, sums_out.at[:, pl.ds(0, span), lanes], sems.at[8]
    )
    mix_copies = [
        pltpu.make_async_copy(
            mix_out.at[pl.ds(part * span, span), :],
            sums_out.at[meta[seqs + count + block * members + part], pl.ds(span, span), :],
            sems.at[9 + part],
        )
        for part in range(members)
    ]

    group = seqs * span
    before = (
        lax.broadcasted_iota(jnp.int32, (group, group), 0)
        < lax.broadcasted_iota(jnp.int32, (group, group), 1)
    ).astype(bf16)
    expert_row = lax.broadcasted_iota(jnp.int32, (8, group), 0).astype(f32)
    member_lane = lax.broadcasted_iota(jnp.int32, (1, group), 1)
    codes = []
    for part in range(members):
        owner = block * members + part
        line = ids[pl.ds(meta[seqs + count + owner], 1), :]
        alive = jnp.zeros((1, group), f32)
        for other in range(seqs):
            inside = jnp.logical_and(
                member_lane >= other * span, member_lane < (other + 1) * span
            )
            inside = jnp.logical_and(
                inside, member_lane - other * span + owner * span < meta[other]
            )
            alive = jnp.where(inside, 1.0, alive)
        taken = jnp.logical_or(
            line[:, :group] == expert_row, line[:, group : 2 * group] == expert_row
        ).astype(f32)
        earlier = dot_nn((taken * alive).astype(bf16), before)
        code = taken * (1.0 + jnp.where(earlier < capacity, alive, 0.0))
        code = code[:, seq * span : (seq + 1) * span]
        code = jnp.concatenate([code, jnp.zeros((120, span), f32)], axis=0)
        codes.append(code.T)
    code = jnp.concatenate(codes, axis=0)

    total_units = gate_weight.shape[0]
    units = total_units // expert_count
    cuts = [slice(i, min(i + 256, total_units)) for i in range(0, total_units, 256)]
    row = block * rows + lax.broadcasted_iota(jnp.int32, (rows, 1), 0)
    own = jnp.logical_and(row >= me * span, row < (me + 1) * span)
    for copy in context_copies:
        copy.wait()
    joined = jnp.concatenate(
        [
            jnp.concatenate(
                [context[d, :, part * each : (part + 1) * each] for d in range(count)], axis=1
            )
            for part in range(members)
        ],
        axis=0,
    )
    context_out[...] = joined
    copies[0].start()
    tokens_copy.wait()
    hidden = tokens[...].astype(f32) + dot_nn(joined, out_weight[...])
    factor = lax.rsqrt(jnp.mean(hidden * hidden, axis=-1, keepdims=True) + epsilon)
    normed = (hidden * factor * gain[...]).astype(bf16)
    normed_out[...] = normed
    copies[1].start()
    logits = dot_nn(normed, router_weight[...])
    lane = lax.broadcasted_iota(jnp.int32, logits.shape, 1)
    logits = jnp.where(lane < expert_count, logits, -1e30)
    router = jnp.exp(logits - jnp.max(logits, axis=-1, keepdims=True))
    router = router / jnp.sum(router, axis=-1, keepdims=True)
    chosen = (code > 0.5).astype(f32)
    kept = (code > 1.5).astype(f32)
    pair_total = jnp.sum(router * chosen, axis=-1, keepdims=True)
    share = router * chosen / pair_total
    scale = share * kept
    for inside, copy in cotangent_copies:
        pl.when(inside)(copy.wait)
    copies[2].start()
    upstream = jnp.where(row < length, cotangent[...].astype(f32), 0.0)
    upstream_low = upstream.astype(bf16)
    root = 0.7978845608028654
    pair_grads = jnp.zeros(logits.shape, f32)
    scale_of = [jnp.broadcast_to(scale[:, e : e + 1], (rows, 128)) for e in range(expert_count)]
    part_sums = [jnp.zeros((rows, 128), f32) for e in range(expert_count)]
    lanes = lax.broadcasted_iota(jnp.int32, (rows, 128), 1)

    def front(number):
        cut = cuts[number]
        return (
            dot_nt(normed, gate_weight[cut, :]),
            dot_nt(normed, up_weight[cut, :]),
            dot_nt(upstream_low, down_weight[cut, :]),
        )

    ready = front(0)
    for number, cut in enumerate(cuts):
        now = ready
        if number + 1 < len(cuts):
            ready = front(number + 1)
        for first in range(cut.start, cut.stop, 128):
            wide = min(128, cut.stop - first)
            inside = slice(first - cut.start, first - cut.start + wide)
            gate_in, up_in, grad_hidden = (value[:, inside] for value in now)
            square = gate_in * gate_in
            bent = gate_in * (root + (root * 0.044715) * square)
            rise = 0.5 + 0.5 * jnp.tanh(bent)
            gelu = gate_in * rise
            slope = rise + (rise - rise * rise) * (6.0 * bent - (4.0 * root) * gate_in)
            hidden_unit = gelu * up_in
            product = hidden_unit * grad_hidden
            low_expert, high_expert = first // units, (first + wide - 1) // units
            scales = scale_of[low_expert][:, :wide]
            if low_expert == high_expert:
                if wide < 128:
                    product = jnp.pad(product, ((0, 0), (0, 128 - wide)))
                part_sums[low_expert] = part_sums[low_expert] + product
            else:
                under = lanes[:, :wide] < high_expert * units - first
                scales = jnp.where(under, scales, scale_of[high_expert][:, :wide])
                part_sums[low_expert] = part_sums[low_expert] + jnp.where(under, product, 0.0)
                part_sums[high_expert] = part_sums[high_expert] + jnp.where(under, 0.0, product)
            scaled_grad = scales * grad_hidden
            at = slice(first, first + wide)
            hidden_out[:, at] = (scales * hidden_unit).astype(bf16)
            grad_gate_out[:, at] = (scaled_grad * up_in * slope).astype(bf16)
            grad_up_out[:, at] = (scaled_grad * gelu).astype(bf16)
    for expert in range(expert_count):
        pair_sum = jnp.sum(part_sums[expert], axis=-1, keepdims=True)
        pair_grads = jnp.where(lane == expert, pair_sum, pair_grads)
    for copy in copies[3:6]:
        copy.start()
    mix = dot_nn(hidden_out[...], down_weight[...])
    grad = dot_nn(grad_gate_out[...], gate_weight[...]) + dot_nn(grad_up_out[...], up_weight[...])
    mix_out[...] = (mix + jnp.where(own, hidden, 0.0)).astype(bf16)
    for copy in mix_copies:
        copy.start()
    pair_grads = pair_grads * kept
    weighted = jnp.sum(pair_grads * share, axis=-1, keepdims=True)
    grad_router = chosen * (pair_grads - weighted) / pair_total
    grad_logits = router * (grad_router - jnp.sum(router * grad_router, axis=-1, keepdims=True))
    grad_logits = grad_logits.astype(bf16)
    logits_out[...] = grad_logits
    copies[7].start()
    grad = grad + dot_nt(grad_logits, router_weight[...])
    spread = hidden * factor
    gain_part = jnp.sum(grad * spread, axis=0, keepdims=True)
    gain_out[...] = gain_in[...]
    gain_out[0:1, :] += gain_part
    grad = grad * gain[...]
    middle = jnp.mean(grad * hidden, axis=-1, keepdims=True) * (factor * factor)
    back = factor * grad - spread * middle + jnp.where(own, upstream, 0.0)
    back = back.astype(bf16)
    grad_out[...] = back
    copies[6].start()
    grad_heads = dot_nt(back, out_weight[...]).astype(bf16)
    for d in range(count):
        for part in range(members):
            heads_out[d, :, part * each : (part + 1) * each] = grad_heads[
                part * span : (part + 1) * span, d * each : (d + 1) * each
            ]
    heads_copy.start()
    for copy in [*copies, *mix_copies, heads_copy]:
        copy.wait()


def experts(
    meta,
    where,
    tokens,
    pieces,
    gain,
    router_weight,
    ids,
    gain_in,
    weights,
    buffers,
    sums,
    sizes,
):
    seq, block = where
    count, span, seqs, expert_count, capacity = sizes
    seq_len, width = tokens.shape
    units = weights[1].shape[0]
    rows = 256
    each = width // count
    members = rows // span
    kinds = [(d, half) for d, half, piece in pieces]
    anywhere = pl.BlockSpec(memory_space=pl.ANY)
    low = lambda *shape: jax.ShapeDtypeStruct(shape, bf16)
    columns = [width] * 3 + [units] * 3 + [width, 128]
    aliased = list(buffers or []) + ([sums] if sums is not None else [])
    first = 2 + len(pieces) + 8
    targets = ([*range(8)] if buffers else []) + ([8] if sums is not None else [])
    static = (count, span, seqs, expert_count, capacity, seq, block, kinds, len(aliased))
    return pl.pallas_call(
        functools.partial(experts_kernel, static),
        out_shape=[low(seqs * seq_len, cols) for cols in columns]
        + [low(count, 2 * span, width), jax.ShapeDtypeStruct((8, width), f32)],
        in_specs=[pl.BlockSpec(memory_space=pltpu.SMEM)]
        + [anywhere] * (1 + len(pieces))
        + [whole_ref] * 8
        + [anywhere] * len(aliased),
        out_specs=[anywhere] * 9 + [whole_ref],
        scratch_shapes=[pltpu.VMEM((rows, cols), bf16) for cols in columns]
        + [
            pltpu.VMEM((count, span, members * each), bf16),
            pltpu.VMEM((rows, width), bf16),
            pltpu.VMEM((rows, width), bf16),
            pltpu.VMEM((count, span, members * each), bf16),
            pltpu.SemaphoreType.DMA((9 + members,)),
            pltpu.SemaphoreType.DMA((1 + 2 * len(pieces),)),
        ],
        input_output_aliases={first + i: target for i, target in enumerate(targets)},
        compiler_params=pltpu.CompilerParams(vmem_limit_bytes=36 * 2**20),
        cost_estimate=pl.CostEstimate(
            flops=2 * rows * width * (6 * units + 2 * width),
            bytes_accessed=16 * 10**6,
            transcendentals=rows * units,
        ),
        name="experts",
    )(
        meta,
        tokens,
        *[piece for d, half, piece in pieces],
        gain,
        router_weight,
        ids,
        gain_in,
        *weights,
        *aliased,
    )


def attend_back_kernel(seq, head, heads, meta, queries_in, keys_in, values_in, *refs):
    own, right, left, bias, queries_out, keys_out, values_out, sums_out = refs[:8]
    table, key_sum, value_sum, summed = refs[8:]
    length = meta[seq]
    _, seq_len, head_size = keys_in.shape
    span = right.shape[0]
    each = heads * head_size
    blocks = seq_len // 128
    summed[...] = (own[0].astype(f32) + right[...].astype(f32) + left[...].astype(f32)).astype(bf16)
    table[...] = jnp.zeros_like(table)
    keys = keys_in[0]
    values = values_in[0]
    for block in range(0, blocks, 2):
        rows = slice(block * 128, block * 128 + 256)
        queries = queries_in[0, rows, :]
        firsts = [
            part * each + head * head_size
            for part in range(block * 128 // span, (block * 128 + 256) // span)
        ]
        grads = jnp.concatenate(
            [summed[:, lane : lane + head_size] for lane in firsts], axis=0
        )
        first_row = (blocks - 1 - block) * 128
        added = jnp.concatenate(
            [
                bias[0, first_row : first_row + seq_len, :],
                bias[0, first_row - 128 : first_row - 128 + seq_len, :],
            ],
            axis=1,
        )
        scores = dot_nt(keys, queries)
        row = lax.broadcasted_iota(jnp.int32, scores.shape, 0)
        scores = jnp.where(row < length, scores + added, -1e30)
        top = jnp.max(scores, axis=0, keepdims=True)
        probs = jnp.exp(scores - top)
        probs = probs * (1.0 / jnp.sum(probs, axis=0, keepdims=True))
        product = probs * dot_nt(values, grads)
        delta = jnp.sum(product, axis=0, keepdims=True)
        grad_scores = product - probs * delta
        table[first_row : first_row + seq_len, :] += grad_scores[:, :128]
        table[first_row - 128 : first_row - 128 + seq_len, :] += grad_scores[:, 128:]
        scores_low = grad_scores.astype(bf16)
        key_part = dot_nn(scores_low, queries)
        value_part = dot_nn(probs.astype(bf16), grads)
        if block == 0:
            key_sum[...] = key_part
            value_sum[...] = value_part
        else:
            key_sum[...] += key_part
            value_sum[...] += value_part
        query_grad = dot_tn(keys, scores_low) * head_size ** (-0.5)
        queries_out[rows, :] = query_grad.T.astype(bf16)
    keys_out[...] = key_sum[...].astype(bf16)
    values_out[...] = value_sum[...].astype(bf16)
    width = table.shape[0] + 128
    lines = jnp.concatenate(
        [table[first : first + 128, :].T for first in range(0, width - 128, 128)]
        + [jnp.zeros((128, 128), f32)],
        axis=1,
    )
    rows = 128
    while rows > 1:
        rows //= 2
        lines = lines[:rows] + pltpu.roll(lines[rows : 2 * rows], width - rows, 1)
    sums_out[...] = jnp.broadcast_to(pltpu.roll(lines, 127, 1), sums_out.shape)


def attend_back(meta, seq, head, heads, qkv, own, right, left, span, bias):
    _, seq_len, head_size = qkv.shape
    width = right.shape[1]
    part = lambda at: pl.BlockSpec((1, seq_len, head_size), lambda i, meta: (at, 0, 0))
    full = lambda *shape: pl.BlockSpec(shape, lambda i, meta: (0,) * len(shape))
    low = jax.ShapeDtypeStruct((seq_len, head_size), bf16)
    return pl.pallas_call(
        functools.partial(attend_back_kernel, seq, head, heads),
        out_shape=(low, low, low, jax.ShapeDtypeStruct((8, 2 * seq_len), f32)),
        grid_spec=pltpu.PrefetchScalarGridSpec(
            num_scalar_prefetch=1,
            grid=(1,),
            in_specs=[part(head), part(heads + head), part(2 * heads + head)]
            + [full(1, span, width), full(span, width), full(span, width)]
            + [pl.BlockSpec((1,) + bias.shape[1:], lambda i, meta: (head, 0, 0))],
            out_specs=[full(seq_len, head_size)] * 3 + [full(8, 2 * seq_len)],
            scratch_shapes=[
                pltpu.VMEM(bias.shape[1:], f32),
                pltpu.VMEM((seq_len, head_size), f32),
                pltpu.VMEM((seq_len, head_size), f32),
                pltpu.VMEM((span, width), bf16),
            ],
        ),
        compiler_params=pltpu.CompilerParams(vmem_limit_bytes=28 * 2**20),
        cost_estimate=pl.CostEstimate(
            flops=6 * 10**9, bytes_accessed=4 * 10**6, transcendentals=seq_len * seq_len
        ),
        name="attend_back",
    )(meta, qkv, qkv, qkv, own, right, left, bias)


def norm_back_kernel(heads, *refs):
    parts, (tokens, weight, grad_in, grad_out, parts_out, gain_out) = refs[: 3 * heads], refs[3 * heads :]

    @pl.when(pl.program_id(0) == 0)
    def _():
        gain_out[...] = jnp.zeros_like(gain_out)

    low = jnp.concatenate([part[...] for part in parts], axis=1)
    wide = tokens[...].astype(f32)
    factor = lax.rsqrt(jnp.mean(wide * wide, axis=-1, keepdims=True) + epsilon)
    upstream = dot_nt(low, weight[...])
    spread = wide * factor
    gain_out[0:1, :] += jnp.sum(upstream * spread, axis=0, keepdims=True)
    middle = jnp.mean(upstream * wide, axis=-1, keepdims=True) * (factor * factor)
    back = factor * upstream - spread * middle + grad_in[...].astype(f32)
    grad_out[...] = back.astype(bf16)
    parts_out[...] = (low.astype(f32) * factor).astype(bf16)


def norm_back(seq, parts, tokens, weight, grad_in):
    seq_len, width = tokens.shape
    head_size = parts[0].shape[1]
    rows = 256
    blocks = seq_len // rows
    by_row = lambda cols, at=0: pl.BlockSpec((rows, cols), lambda i: (at + i, 0))
    columns = head_size * len(parts)
    return pl.pallas_call(
        functools.partial(norm_back_kernel, len(parts) // 3),
        out_shape=(
            jax.ShapeDtypeStruct((seq_len, width), bf16),
            jax.ShapeDtypeStruct((seq_len, columns), bf16),
            jax.ShapeDtypeStruct((8, width), f32),
        ),
        grid=(blocks,),
        in_specs=[by_row(head_size)] * len(parts)
        + [by_row(width), pl.BlockSpec(weight.shape, lambda i: (0, 0)), by_row(width, seq * blocks)],
        out_specs=(by_row(width), by_row(columns), pl.BlockSpec((8, width), lambda i: (0, 0))),
        compiler_params=pltpu.CompilerParams(vmem_limit_bytes=28 * 2**20),
        cost_estimate=pl.CostEstimate(
            flops=2 * seq_len * width * columns, bytes_accessed=10 * 10**6, transcendentals=0
        ),
        name="norm_back",
    )(*parts, tokens, weight, grad_in)


def spread_kernel(parts, gain, *outs):
    reps, count, cut, columns = parts.shape
    each = columns // 3
    for rep in range(reps):
        rows = slice(rep * cut, (rep + 1) * cut)
        scale = gain[rows, :]
        for owner in range(count):
            block = parts[rep, owner].astype(f32) * scale
            for kind, out in enumerate(outs):
                out[rows, owner * each : (owner + 1) * each] = block[:, kind * each : (kind + 1) * each]


def spread(parts, gain):
    reps, count, cut, columns = parts.shape
    shape = jax.ShapeDtypeStruct((reps * cut, count * columns // 3), f32)
    return pl.pallas_call(
        spread_kernel,
        out_shape=(shape,) * 3,
        in_specs=[whole_ref] * 2,
        out_specs=[whole_ref] * 3,
        compiler_params=pltpu.CompilerParams(vmem_limit_bytes=12 * 2**20),
        name="spread",
    )(parts, gain.reshape(-1, 1))


def body(
    tokens,
    lengths,
    expert_ids,
    buckets,
    norm1_gain,
    w_query,
    w_key,
    w_value,
    w_out,
    rel_bias,
    norm2_gain,
    w_router,
    w_gate,
    w_up,
    w_down,
    cotangent,
):
    seqs, span, width = tokens.shape
    count = lax.axis_size("shard")
    reps = lax.axis_size("rep")
    me = lax.axis_index("shard")
    rep = lax.axis_index("rep")
    seq_len = span * count
    expert_count, unit_count, _ = w_gate.shape
    heads = rel_bias.shape[1]
    head_size = w_query.shape[1] // (count * heads)
    each = heads * head_size
    feats = w_query.shape[0]
    cut = feats // reps
    row_count = seqs * span
    capacity = 10 * row_count // (4 * expert_count)
    place = ring_place(me, count)
    distances = jnp.arange(count, dtype=jnp.int32)
    owners = ring_index((place + distances) % count, count)
    distance_of = (ring_place(distances, count) - place) % count
    meta = jnp.concatenate([lengths, owners, distance_of, me[None]]).astype(jnp.int32)

    def line(values):
        flat = values.reshape(-1).astype(bf16)
        return jnp.pad(flat, (0, width - flat.shape[0]))[None]

    packed = jnp.concatenate(
        [
            tokens.reshape(row_count, width),
            lax.dynamic_slice_in_dim(w_out, rep * cut, cut, 0),
            line(expert_ids.reshape(row_count, 2).T),
            line(jnp.concatenate([norm2_gain, w_router.reshape(-1)])),
            jnp.zeros((14, width), bf16),
        ],
        axis=0,
    )
    extra = row_count
    token_ring = Gather(
        packed,
        count,
        lambda value: (
            jnp.concatenate([value[:span], value[extra:]], axis=0),
            value[span:extra],
        ),
    )
    hops = []
    while not token_ring.done:
        fire([token_ring])
        hops.append(token_ring.last())

    gain_one = norm1_gain.astype(f32)
    own_qkv = jnp.stack([w_query, w_key, w_value], axis=1)
    own_cut = lax.dynamic_slice_in_dim(own_qkv, rep * cut, cut, 0).astype(f32)
    own_cut = own_cut * lax.dynamic_slice_in_dim(gain_one, rep * cut, cut, 0)[:, None, None]
    own_cut = own_cut.astype(bf16).reshape(cut, 3, count, each).transpose(2, 0, 1, 3)
    qkv_weight = lax.all_to_all(
        own_cut.reshape(count, cut, 3 * each), "shard", split_axis=0, concat_axis=0, tiled=True
    )
    qkv_weight = rep_gather(after(qkv_weight, hops[1]), reps, rep).transpose(1, 0, 2, 3).reshape(width, 3 * each)

    bucket_count = rel_bias.shape[0]
    bucket_hot = (
        buckets[:, None] == jnp.arange(bucket_count, dtype=jnp.int32)[None, :]
    ).astype(f32)
    bucket_hot = jnp.pad(bucket_hot, ((0, 1), (0, 0)))
    bias_vec = jnp.einsum("rb,bh->hr", bucket_hot, rel_bias.astype(f32), precision=highest)
    bias, bias_turned = bias_tables(bias_vec)

    riders = [None] * count
    for distance, half, piece in token_ring.pieces:
        if half != 1:
            riders[distance] = piece[extra:] if half is None else piece[span:]
    riders = jnp.stack(riders)
    out_weight = rep_gather(riders[:, :cut], reps, rep).transpose(1, 0, 2, 3).reshape(width, width)
    ids = riders[:, cut].astype(f32)
    small = jnp.take(riders[:, cut + 1], distance_of, axis=0)
    gain_two = small[:, :feats].astype(f32).reshape(1, width)
    router_weight = small[:, feats : feats * (1 + expert_count)].reshape(width, expert_count)
    router_weight = jnp.pad(router_weight, ((0, 0), (0, 128 - expert_count)))
    expert_weights = [out_weight] + [
        weight.reshape(expert_count * unit_count, width) for weight in (w_gate, w_up, w_down)
    ]

    def sent(rings):
        return tuple(ring.last() for ring in rings if ring.last()[0] is not None)

    attended, mixed_rings, rings = [], [], []
    waits = token_ring.last()
    for s in range(seqs):
        fire(rings, waits)
        attended.append(
            attend(
                after(meta, waits),
                s,
                seqs,
                token_ring.pieces,
                cotangent[s],
                qkv_weight,
                bias,
                heads,
                head_size,
            )
        )
        waits = (attended[s][2], sent(rings))
        mixed_rings.append(Gather(attended[s][2], count))
        rings = [mixed_rings[0]]
    while not rings[0].done:
        fire(rings, waits)
        waits = lasts(rings)

    sizes = (count, span, seqs, expert_count, capacity)
    buffers = None
    gain_part = jnp.zeros((8, width), f32)
    sums_all, sum_rings = [], []
    rings = [mixed_rings[1]]
    for s in range(seqs):
        if s > 0:
            while not rings[0].done:
                fire(rings, waits)
                waits = lasts(rings)
            sum_rings.append(Sum(lambda d, part=sums_all[s - 1]: part[d], count))
            rings = [sum_rings[s - 1]]
        sums = None
        for block in range(seq_len // 256):
            if not rings[0].done:
                fire(rings, waits)
            *buffers, sums, gain_part = experts(
                after(meta, waits),
                (s, block),
                attended[s][0],
                mixed_rings[s].pieces,
                gain_two,
                router_weight,
                ids,
                gain_part,
                expert_weights,
                buffers,
                sums,
                sizes,
            )
            waits = (gain_part, sent(rings))
        sums_all.append(sums)
    context_rows, normed, cot_rows, hidden, grad_gate, grad_up, grad_rows, grad_logits = buffers
    while not rings[0].done:
        fire(rings, waits)
        waits = lasts(rings)

    sum_rings.append(Sum(lambda d: sums_all[1][d, :span], count))
    rings = [sum_rings[1]]
    totals = []
    for left_side, right_side in ((hidden, cot_rows), (grad_gate, normed), (grad_up, normed)):
        if not rings[0].done:
            fire(rings, waits)
        grads = dot_tn(after(left_side, waits), right_side).astype(bf16)
        totals.append(RepTotal(grads, reps, rep))
        waits = (grads, sent(rings))
        if len(totals) > 1:
            totals[-2].cross()
            waits = waits + (totals[-2].kept,)
    while not rings[0].done:
        fire(rings, waits)
        waits = lasts(rings)
    totals[2].cross()
    waits = (totals[2].kept, lasts(rings))

    def rows_of(array, distance):
        return lax.dynamic_slice_in_dim(array, owners[distance] * span, span, 0)

    def back(s, rings, waits):
        parts = []
        for head in range(heads):
            live = [ring for ring in rings if not ring.done]
            if live:
                fire(live, waits)
            made = attend_back(
                after(meta, waits),
                s,
                head,
                heads,
                attended[s][1],
                sums_all[s],
                *sum_rings[s].last(),
                span,
                bias_turned,
            )
            parts.append(made[:3])
            offset_sums.append((head, made[3]))
            waits = (made[0], sent(rings))
        parts = [parts[head][kind] for kind in range(3) for head in range(heads)]
        return norm_back(s, after(parts, waits), attended[s][0], qkv_weight, grad_rows)

    offset_sums = []
    grads_first, scaled_first, gain_first = back(0, [], waits)
    waits = (grads_first,)
    mix_ring = Sum(
        lambda d: jnp.concatenate([sums_all[1][d, span:], rows_of(grads_first, d)], axis=0), count
    )
    out_grad = dot_tn(after(context_rows, waits), grad_rows).astype(bf16)
    router_grad = dot_tn(normed, grad_logits)[:, :expert_count]
    flat = jnp.concatenate(
        [gain_part[0].reshape(count, feats), router_grad.reshape(count, feats * expert_count)], axis=1
    ).astype(bf16)
    flat = jnp.take(flat, owners, axis=0)
    small_size = flat.shape[1] // 2
    flat = jnp.pad(flat.reshape(count, 2, 1, small_size), ((0, 0), (0, 0), (0, 15), (0, width - small_size)))
    out_grad = jnp.concatenate([out_grad.reshape(count, 2, each // 2, width), flat], axis=2)
    side = rep % 2
    out_kept = lax.dynamic_index_in_dim(out_grad, side, 1, keepdims=False)
    out_got = swap(lax.dynamic_index_in_dim(out_grad, 1 - side, 1, keepdims=False), "rep", reps, 1)
    out_grad = add_low(out_kept, out_got)

    grads_last, scaled_last, gain_last = back(1, [mix_ring], waits)
    last_ring = Sum(
        lambda d: jnp.concatenate([rows_of(grads_last, d), out_grad[d]], axis=0), count
    )
    rings = [mix_ring, last_ring]
    waits = (grads_last,)
    while not all(ring.done for ring in rings):
        fire(rings, waits)
        waits = lasts(rings)

    def total_of(ring):
        total = ring.chunk_of(0).astype(f32)
        for part in ring.last():
            total = total + part.astype(f32)
        return total

    mix_first = sums_all[0][0, span:].astype(f32)
    for part in sum_rings[0].last():
        mix_first = mix_first + part[span:].astype(f32)
    middle, final = total_of(mix_ring), total_of(last_ring)
    grad_tokens = jnp.stack([middle[span:], final[:span]])
    positions = me * span + jnp.arange(span, dtype=jnp.int32)
    live_mask = (positions[None, :] < lengths[:, None]).astype(f32)[:, :, None]
    block_out = (live_mask * jnp.stack([mix_first, middle[:span]])).astype(bf16)
    out_own = final[span:].astype(bf16)
    for bit in bits_of(reps)[1:]:
        out_own = add_low(out_own, swap(out_own, "rep", reps, bit))
    out_other = swap(out_own, "rep", reps, 1)
    out_both = jnp.where(
        side == 0, jnp.stack([out_own, out_other]), jnp.stack([out_other, out_own])
    ).astype(f32)
    total_out = out_both[:, : each // 2].reshape(feats, width)
    flat = out_both[:, each // 2, :small_size].reshape(-1)
    total_gain_two = flat[:feats]
    total_router = flat[feats:].reshape(feats, expert_count)
    parts_all = [scaled_first, scaled_last]
    gain_one_part = [gain_first, gain_last]

    qkv_grad = sum(dot_tn(attended[s][0], parts_all[s]) for s in range(seqs)).astype(bf16)
    offsets = jnp.stack(
        [sum(part[0] for h, part in offset_sums if h == head) for head in range(heads)]
    )
    bias_grad = jnp.einsum("hr,rb->hb", offsets, bucket_hot, precision=highest)
    gain_rows = sum(part[0] for part in gain_one_part).reshape(count, reps, 1, cut)
    bias_rows = jnp.broadcast_to(
        bias_grad.reshape(1, reps, 1, -1), (count, reps, 1, bias_grad.size // reps)
    )
    flat = jnp.concatenate([gain_rows, bias_rows], axis=3).astype(bf16)
    flat = jnp.pad(flat, ((0, 0), (0, 0), (0, 15), (0, 3 * each - flat.shape[3])))
    qkv_grad = jnp.concatenate([qkv_grad.reshape(count, reps, cut, 3 * each), flat], axis=2)
    qkv_grad = rep_scatter(qkv_grad.transpose(1, 0, 2, 3), reps, rep)
    qkv_grad = lax.all_to_all(qkv_grad, "shard", split_axis=0, concat_axis=0, tiled=True)
    gain_one_grad = jnp.sum(qkv_grad[:, cut, :cut].astype(f32), axis=0)
    bias_size = bias_grad.size // reps
    bias_own = lax.dynamic_index_in_dim(qkv_grad[:, cut, cut : cut + bias_size], me, 0, keepdims=False)
    tail = jnp.concatenate([gain_one_grad.astype(bf16), bias_own])
    tail = jnp.pad(tail, (0, width - tail.shape[0])).reshape(1, width)
    both = jnp.concatenate(
        [
            qkv_grad[:, :cut].reshape(count * cut * 3 * each // width, width),
            jnp.pad(tail, ((0, 15), (0, 0))),
        ],
        axis=0,
    )
    both = rep_gather(both, reps, rep)
    qkv_rows = 3 * cut
    qkv_grad = spread(both[:, :qkv_rows].reshape(reps, count, cut, 3 * each), gain_one)
    tail = both[:, qkv_rows].astype(f32)
    total_gain_one = tail[:, :cut].reshape(feats) / gain_one
    total_bias = tail[:, cut : cut + bias_size].reshape(heads, bucket_count).T

    total_down, total_gate, total_up = (
        total.finish().reshape(expert_count, unit_count, width) for total in totals
    )
    return (
        block_out,
        grad_tokens,
        total_gain_one,
        qkv_grad[0],
        qkv_grad[1],
        qkv_grad[2],
        total_out,
        total_bias,
        total_gain_two,
        total_router,
        total_gate,
        total_up,
        total_down,
    )


def solution(mesh):
    rows = P("rep", "shard", None)
    first = P("shard")
    weight = P("shard", None)
    expert = P(None, "shard", None)
    return jax.shard_map(
        body,
        mesh=mesh,
        in_specs=(rows, P("rep"), rows, P(), first, weight, weight, weight, weight)
        + (P(None, "shard"), first, weight, expert, expert, expert, rows),
        out_specs=(rows, rows, first, weight, weight, weight, weight)
        + (P(None, "shard"), first, weight, expert, expert, expert),
        check_vma=False,
    )
```

```python
import functools

import jax
import jax.numpy as jnp
from jax import lax
from jax.experimental import pallas as pl
from jax.experimental.pallas import tpu as pltpu
from jax.sharding import PartitionSpec as P

epsilon = 1e-06
highest = lax.Precision.HIGHEST
bf16 = jnp.bfloat16
f32 = jnp.float32
vmem_limit = 58 * 1024 * 1024
whole_ref = pl.BlockSpec(memory_space=pltpu.VMEM)


def dot_nt(left, right):
    return lax.dot_general(left, right, (((1,), (1,)), ((), ())), preferred_element_type=f32)


def dot_tn(left, right):
    return lax.dot_general(left, right, (((0,), (0,)), ((), ())), preferred_element_type=f32)


def dot_nn(left, right):
    return lax.dot_general(left, right, (((1,), (0,)), ((), ())), preferred_element_type=f32)


def ring_index(place, count):
    return jnp.where(place < count // 2, 2 * place, 2 * count - 1 - 2 * place)


def ring_place(index, count):
    return jnp.where(index % 2 == 0, index // 2, count - 1 - index // 2)


def ring_send(value, step, count):
    order = [2 * i if i < count // 2 else 2 * count - 1 - 2 * i for i in range(count)]
    pairs = [(order[i], order[(i + step) % count]) for i in range(count)]
    return lax.ppermute(value, "shard", pairs)


def after(value, *waits):
    if not jax.tree.leaves(waits):
        return value
    flat, tree = jax.tree.flatten(value)
    held = lax.optimization_barrier(tuple(flat) + tuple(jax.tree.leaves(waits)))
    return tree.unflatten(held[: len(flat)])


def halve(value):
    half = value.shape[0] // 2
    return value[:half], value[half:]


class Gather:
    def __init__(self, value, count, split=None):
        self.count, self.step, self.split = count, 1, split or halve
        self.ahead = self.behind = value
        self.pieces = [(0, None, value)]
        self.done = False

    def hop(self, *waits):
        behind, ahead = after((self.behind, self.ahead), *waits)
        far = self.count // 2
        if self.step < far:
            self.behind = ring_send(behind, 1, self.count)
            self.ahead = ring_send(ahead, -1, self.count)
            self.pieces += [(self.count - self.step, None, self.behind), (self.step, None, self.ahead)]
            self.step += 1
        else:
            self.behind = ring_send(self.split(behind)[0], 1, self.count)
            self.ahead = ring_send(self.split(ahead)[1], -1, self.count)
            self.pieces += [(far, 0, self.behind), (far, 1, self.ahead)]
            self.done = True

    def last(self):
        return (self.behind, self.ahead)


def add_low(left, right):
    return (left.astype(f32) + right.astype(f32)).astype(bf16)


def ring_add_kernel(half, firsts, right, left, *refs):
    count = len(firsts)
    owns = (refs[:count], refs[count : 2 * count])
    outs = refs[2 * count :]
    total = outs[0].shape[0]
    for come, own, out, begin in zip((right, left), owns, outs, (0, total - half)):
        for source, first in zip(own, firsts):
            last = first + source.shape[1]
            low, high = max(first, begin), min(last, begin + half)
            if low < high:
                summed = source[0, low - first : high - first, :].astype(f32)
                summed = summed + come[low - begin : high - begin, :].astype(f32)
                out[low:high, :] = summed.astype(bf16)
            if first < min(low, last):
                out[first : min(low, last), :] = source[0, : min(low, last) - first, :]
            if max(high, first) < last:
                out[max(high, first) : last, :] = source[0, max(high, first) - first :, :]


def ring_add(right, left, own_right, own_left, rows):
    width = right.shape[1]
    total = sum(rows)
    firsts = [sum(rows[:i]) for i in range(len(rows))]
    full = lambda *shape: pl.BlockSpec(shape, lambda i: (0,) * len(shape))
    part = lambda spot, count: pl.BlockSpec((1, count, width), lambda i: (spot[1], spot[2], 0))
    shape = jax.ShapeDtypeStruct((total, width), bf16)
    return pl.pallas_call(
        functools.partial(ring_add_kernel, right.shape[0], firsts),
        out_shape=(shape, shape),
        grid=(1,),
        in_specs=[full(*right.shape)] * 2
        + [part(spot, count) for spot, count in zip(own_right, rows)]
        + [part(spot, count) for spot, count in zip(own_left, rows)],
        out_specs=(full(total, width),) * 2,
        compiler_params=pltpu.CompilerParams(vmem_limit_bytes=14 * 2**20),
        cost_estimate=pl.CostEstimate(
            flops=2 * total * width, bytes_accessed=1000, transcendentals=0
        ),
        name="ring_add",
    )(right, left, *[spot[0] for spot in own_right], *[spot[0] for spot in own_left])


class Sum:
    def __init__(self, sources, count):
        self.sources, self.count, self.step = sources, count, count // 2
        self.rows = [rows for array, block, rows in sources]
        self.right = self.left = None
        self.done = False

    def chunk(self, distance):
        return jnp.concatenate(
            [array[distance, block * rows : (block + 1) * rows] for array, block, rows in self.sources],
            axis=0,
        )

    def hop(self, *waits):
        if self.right is None:
            right, left = halve(self.chunk(self.step))
        else:
            spots = [
                [(array, distance, block) for array, block, rows in self.sources]
                for distance in (self.step, self.count - self.step)
            ]
            right, left = ring_add(self.right, self.left, *spots, self.rows)
        right, left = after((right, left), *waits)
        self.right = ring_send(right, 1, self.count)
        self.left = ring_send(left, -1, self.count)
        self.step -= 1
        self.done = self.step == 0

    def last(self):
        return (self.right, self.left)

    def total(self):
        total = self.chunk(0).astype(f32)
        return total + self.right.astype(f32) + self.left.astype(f32)


def fire(rings, *waits):
    rings = [ring for ring in rings if not ring.done]
    waits = waits + tuple(ring.last() for ring in rings if ring.last()[0] is not None)
    for ring in rings:
        ring.hop(*waits)


def lasts(rings):
    return tuple(ring.last() for ring in rings)


def swap(value, axis, count, bit):
    return lax.ppermute(value, axis, [(i, i ^ bit) for i in range(count)])


def bits_of(count):
    return [1 << i for i in range(count.bit_length() - 1)]


def rep_scatter(value, count, me, *waits):
    for bit in bits_of(count):
        value = value.reshape((value.shape[0] // 2, 2) + value.shape[1:])
        side = (me // bit) % 2
        sent = lax.dynamic_index_in_dim(value, 1 - side, 1, keepdims=False)
        kept = lax.dynamic_index_in_dim(value, side, 1, keepdims=False)
        if bit > 1:
            sent = after(sent, *waits)
        value = add_low(kept, swap(sent, "rep", count, bit))
    return value[0]


def rep_parts(value, count, me):
    parts, tags = [value], [0]
    for bit in bits_of(count)[::-1]:
        parts = parts + [swap(part, "rep", count, bit) for part in parts]
        tags = tags + [tag ^ bit for tag in tags]
    return parts, (me ^ jnp.array(tags, jnp.int32))


def rep_order(count):
    tags = [0]
    for bit in bits_of(count)[::-1]:
        tags = tags + [tag ^ bit for tag in tags]
    return [tags.index(tag) for tag in range(count)]


def weave_kernel(count, spots, *refs):
    parts, out, sems = refs[:count], refs[count], refs[count + 1]
    copies = [
        pltpu.make_async_copy(part, out.at[:, spots[i]], sems.at[i])
        for i, part in enumerate(parts)
    ]
    for copy in copies:
        copy.start()
    for copy in copies:
        copy.wait()


def weave(parts, spots):
    first, rows, columns = parts[0].shape
    anywhere = pl.BlockSpec(memory_space=pl.ANY)
    out = pl.pallas_call(
        functools.partial(weave_kernel, len(parts)),
        out_shape=jax.ShapeDtypeStruct((first, len(parts), rows, columns), parts[0].dtype),
        in_specs=[pl.BlockSpec(memory_space=pltpu.SMEM)] + [anywhere] * len(parts),
        out_specs=anywhere,
        scratch_shapes=[pltpu.SemaphoreType.DMA((len(parts),))],
        compiler_params=pltpu.CompilerParams(vmem_limit_bytes=2**20),
        name="weave",
    )(spots, *parts)
    return out.reshape(first * len(parts) * rows, columns)


def widen_kernel(parts, meta, kept, got, kept_other, got_other, out, *scratch):
    held, wide, in_sems, out_sems = scratch
    half = kept.shape[0]
    rows = half // parts
    sources = (kept, got, kept_other, got_other)
    ins = [
        [
            pltpu.make_async_copy(
                source.at[pl.ds(part * rows, rows), :],
                held.at[number, pl.ds(part * rows, rows), :],
                in_sems.at[number * parts + part],
            )
            for number, source in enumerate(sources)
        ]
        for part in range(parts)
    ]
    for part in range(parts):
        for copy in ins[part]:
            copy.start()
    outs = []
    for part in range(parts):
        for copy in ins[part]:
            copy.wait()
        at = slice(part * rows, (part + 1) * rows)
        for pair in range(2):
            total = held[2 * pair, at, :].astype(f32) + held[2 * pair + 1, at, :].astype(f32)
            wide[pair, at, :] = total
            side = meta[0] if pair == 0 else 1 - meta[0]
            start = pl.multiple_of(side * half + part * rows, 8)
            outs.append(
                pltpu.make_async_copy(
                    wide.at[pair, pl.ds(part * rows, rows), :],
                    out.at[pl.ds(start, rows), :],
                    out_sems.at[pair * parts + part],
                )
            )
            outs[-1].start()
    for copy in outs:
        copy.wait()


def widen(side, kept, got, kept_other, got_other):
    half, width = kept.shape
    parts = 4 if half % 64 == 0 else 2 if half % 32 == 0 else 1
    anywhere = pl.BlockSpec(memory_space=pl.ANY)
    return pl.pallas_call(
        functools.partial(widen_kernel, parts),
        out_shape=jax.ShapeDtypeStruct((2 * half, width), f32),
        in_specs=[pl.BlockSpec(memory_space=pltpu.SMEM)] + [anywhere] * 4,
        out_specs=anywhere,
        scratch_shapes=[
            pltpu.VMEM((4, half, width), bf16),
            pltpu.VMEM((2, half, width), f32),
            pltpu.SemaphoreType.DMA((4 * parts,)),
            pltpu.SemaphoreType.DMA((2 * parts,)),
        ],
        compiler_params=pltpu.CompilerParams(vmem_limit_bytes=16 * 2**20),
        name="widen",
    )(side, kept, got, kept_other, got_other)


class RepTotal:
    def __init__(self, value, count, me):
        self.count, self.side = count, me % 2
        value = value.reshape((2, value.shape[0] // 2) + value.shape[1:])
        sent = lax.dynamic_index_in_dim(value, 1 - self.side, 0, keepdims=False)
        self.kept = lax.dynamic_index_in_dim(value, self.side, 0, keepdims=False)
        self.got = swap(sent, "rep", count, 1)

    def cross(self, *waits):
        kept = add_low(self.kept, self.got)
        for bit in bits_of(self.count)[1:-1]:
            kept = add_low(kept, swap(kept, "rep", self.count, bit))
        self.kept = after(kept, *waits)
        self.got = swap(self.kept, "rep", self.count, self.count // 2)
        self.kept_other = swap(self.kept, "rep", self.count, 1)

    def finish(self):
        got_other = swap(self.got, "rep", self.count, 1)
        side = self.side.reshape(1).astype(jnp.int32)
        return widen(side, self.kept, self.got, self.kept_other, got_other)


def bias_kernel(vec, table, turned):
    heads, _, width = table.shape
    for head in range(heads):
        line = jnp.broadcast_to(vec[head : head + 1, :], (128, vec.shape[1]))
        line = pltpu.roll(line, vec.shape[1] - 127, 1, stride=1, stride_axis=0)
        table[head] = line[:, :width]
        for first in range(0, width, 128):
            turned[head, first : first + 128, :] = line[:, first : first + 128].T


def bias_tables(vec):
    heads, length = vec.shape
    width = length - 128
    return pl.pallas_call(
        bias_kernel,
        out_shape=(
            jax.ShapeDtypeStruct((heads, 128, width), f32),
            jax.ShapeDtypeStruct((heads, width, 128), f32),
        ),
        in_specs=[whole_ref],
        out_specs=[whole_ref] * 2,
        compiler_params=pltpu.CompilerParams(vmem_limit_bytes=24 * 2**20),
        name="bias_tables",
    )(vec)


def attend_kernel(seq, seqs, places, heads, head_size, riders, meta, *refs):
    pieces = refs[: len(places)]
    cotangent, weight, bias, tokens_out, qkv_out, mixed_out, *more = refs[len(places) :]
    sems = more[-1]
    length = meta[seq]
    span = cotangent.shape[0]
    seq_len = tokens_out.shape[0]
    each = heads * head_size
    blocks = seq_len // 128
    copies = []
    for number, ((distance, first), piece) in enumerate(zip(places, pieces)):
        start = pl.multiple_of(meta[seqs + distance] * span, 16)
        copies.append(
            pltpu.make_async_copy(
                piece.at[pl.ds(first, span), :],
                tokens_out.at[pl.ds(start, span), :],
                sems.at[number],
            )
        )
        copies[-1].start()
    for number, (distance, first) in enumerate(riders):
        copies.append(
            pltpu.make_async_copy(
                pieces[number].at[pl.ds(first, more[0].shape[1]), :],
                more[0].at[distance],
                sems.at[len(places) + number],
            )
        )
        copies[-1].start()
    mixed_out[0:span, :] = cotangent[...]
    for copy in copies:
        copy.wait()
    for first in range(0, seq_len, 256):
        rows = slice(first, first + 256)
        low = tokens_out[rows, :]
        wide = low.astype(f32)
        factor = lax.rsqrt(jnp.mean(wide * wide, axis=-1, keepdims=True) + epsilon)
        made = dot_nn(low, weight[...]) * factor
        for part in range(3 * heads):
            cut = made[:, part * head_size : (part + 1) * head_size]
            if part < heads:
                cut = cut.astype(bf16).astype(f32) * head_size ** (-0.5)
            qkv_out[part, rows, :] = cut.astype(bf16)
    for head in range(heads):
        keys = qkv_out[heads + head]
        values = qkv_out[2 * heads + head]
        for block in range(0, blocks, 2):
            queries = qkv_out[head, block * 128 : block * 128 + 256, :]
            scores = dot_nt(queries, keys)
            first_col = (blocks - 1 - block) * 128
            added = jnp.concatenate(
                [
                    bias[head, :, first_col : first_col + seq_len],
                    bias[head, :, first_col - 128 : first_col - 128 + seq_len],
                ],
                axis=0,
            )
            column = lax.broadcasted_iota(jnp.int32, scores.shape, 1)
            scores = jnp.where(column < length, scores + added, -1e30)
            top = jnp.max(scores, axis=-1, keepdims=True)
            weights = jnp.exp(scores - top)
            total = jnp.sum(weights, axis=-1, keepdims=True)
            mixed = dot_nn(weights.astype(bf16), values) / total
            mixed = mixed.astype(bf16)
            for part in range(256 // span):
                lane = (block * 128 // span + part) * each + head * head_size
                mixed_out[span : 2 * span, lane : lane + head_size] = mixed[
                    part * span : (part + 1) * span, :
                ]


def attend(meta, seq, seqs, pieces, cotangent, weight, bias, heads, head_size):
    width = weight.shape[0]
    span = cotangent.shape[0]
    pieces = [(d, half, piece) for d, half, piece in pieces if half is None or half == seq]
    places = [(d, seq * span if half is None else 0) for d, half, piece in pieces]
    seq_len = span * len(pieces)
    full = lambda *shape: pl.BlockSpec(shape, lambda i, meta: (0,) * len(shape))
    shapes = [(seq_len, width), (3 * heads, seq_len, head_size), (2 * span, width)]
    riders = []
    if seq == 0:
        extra = pieces[0][2].shape[0] - seqs * span
        riders = [(d, seqs * span if half is None else span) for d, half, piece in pieces]
        shapes.append((len(pieces), extra, width))
    return pl.pallas_call(
        functools.partial(attend_kernel, seq, seqs, places, heads, head_size, riders),
        out_shape=tuple(jax.ShapeDtypeStruct(shape, bf16) for shape in shapes),
        grid_spec=pltpu.PrefetchScalarGridSpec(
            num_scalar_prefetch=1,
            grid=(1,),
            in_specs=[pl.BlockSpec(memory_space=pl.ANY)] * len(pieces)
            + [full(*cotangent.shape), full(*weight.shape), full(*bias.shape)],
            out_specs=[full(*shape) for shape in shapes],
            scratch_shapes=[pltpu.SemaphoreType.DMA((2 * len(pieces),))],
        ),
        compiler_params=pltpu.CompilerParams(vmem_limit_bytes=28 * 2**20),
        cost_estimate=pl.CostEstimate(
            flops=8 * 10**9, bytes_accessed=1000, transcendentals=heads * seq_len * seq_len
        ),
        name="attend",
    )(meta, *[piece for d, half, piece in pieces], cotangent, weight, bias)


def experts_kernel(static, meta, *refs):
    count, span, seqs, expert_count, capacity, seq, blocks, kinds, alias_count = static
    tokens_hbm, *pieces = refs[: 1 + len(kinds)]
    refs = refs[1 + len(kinds) :]
    gain, router_weight, ids, gain_in, out_weight, gate_weight, up_weight, down_weight = refs[:8]
    refs = refs[8 + alias_count :]
    buffers, sums_out, gain_out, refs = refs[:8], refs[8], refs[9], refs[10:]
    staged, refs = refs[:8], refs[8:]
    heads_all, mix_all, tokens_all, context_all, sems_all, in_sems_all = refs
    _, rows, width = tokens_all.shape
    each = width // count
    seq_len = span * count
    members = rows // span
    length, me = meta[seq], meta[meta.shape[0] - 1]


    def bring(number_of_block, block):
        tokens, context = tokens_all.at[number_of_block], context_all.at[number_of_block]
        cotangent, in_sems = staged[2].at[number_of_block], in_sems_all.at[number_of_block]
        tokens_copy = pltpu.make_async_copy(
            tokens_hbm.at[pl.ds(block * rows, rows), :], tokens, in_sems.at[0]
        )
        tokens_copy.start()
        lanes = pl.ds(block * members * each, members * each)
        context_copies, cotangent_copies = [], []
        for number, ((distance, half), piece) in enumerate(zip(kinds, pieces)):
            if half != 0:
                first = span if half is None else 0
                context_copies.append(
                    pltpu.make_async_copy(
                        piece.at[pl.ds(first, span), lanes],
                        context.at[distance],
                        in_sems.at[1 + 2 * number],
                    )
                )
                context_copies[-1].start()
        for number, ((distance, half), piece) in enumerate(zip(kinds, pieces)):
            if half != 1:
                owner = meta[seqs + distance]
                inside = owner // members == block
                start = pl.multiple_of(
                    jnp.where(inside, owner - block * members, 0) * span, 16
                )
                copy = pltpu.make_async_copy(
                    piece.at[pl.ds(0, span), :],
                    cotangent.at[pl.ds(start, span), :],
                    in_sems.at[2 + 2 * number],
                )
                pl.when(inside)(copy.start)
                cotangent_copies.append((inside, copy))
        return tokens_copy, context_copies, cotangent_copies

    def work(number_of_block, block, brought, staged):
        tokens_copy, context_copies, cotangent_copies = brought
        staged = [ref.at[number_of_block] for ref in staged]
        heads_out, mix_out, tokens, context = (
            ref.at[number_of_block] for ref in (heads_all, mix_all, tokens_all, context_all)
        )
        sems = sems_all.at[number_of_block]
        at_row = seq * seq_len + block * rows
        lanes = pl.ds(block * members * each, members * each)
        (
            context_out,
            normed_out,
            cotangent,
            hidden_out,
            grad_gate_out,
            grad_up_out,
            grad_out,
            logits_out,
        ) = staged
        copies = [
            pltpu.make_async_copy(source, target.at[pl.ds(at_row, rows), :], sems.at[number])
            for number, (source, target) in enumerate(zip(staged, buffers))
        ]
        heads_copy = pltpu.make_async_copy(
            heads_out, sums_out.at[:, pl.ds(0, span), lanes], sems.at[8]
        )
        mix_copies = [
            pltpu.make_async_copy(
                mix_out.at[pl.ds(part * span, span), :],
                sums_out.at[meta[seqs + count + block * members + part], pl.ds(span, span), :],
                sems.at[9 + part],
            )
            for part in range(members)
        ]

        group = seqs * span
        before = (
            lax.broadcasted_iota(jnp.int32, (group, group), 0)
            < lax.broadcasted_iota(jnp.int32, (group, group), 1)
        ).astype(bf16)
        expert_row = lax.broadcasted_iota(jnp.int32, (8, group), 0).astype(f32)
        member_lane = lax.broadcasted_iota(jnp.int32, (1, group), 1)
        codes = []
        for part in range(members):
            owner = block * members + part
            line = ids[pl.ds(meta[seqs + count + owner], 1), :]
            alive = jnp.zeros((1, group), f32)
            for other in range(seqs):
                inside = jnp.logical_and(
                    member_lane >= other * span, member_lane < (other + 1) * span
                )
                inside = jnp.logical_and(
                    inside, member_lane - other * span + owner * span < meta[other]
                )
                alive = jnp.where(inside, 1.0, alive)
            taken = jnp.logical_or(
                line[:, :group] == expert_row, line[:, group : 2 * group] == expert_row
            ).astype(f32)
            earlier = dot_nn((taken * alive).astype(bf16), before)
            code = taken * (1.0 + jnp.where(earlier < capacity, alive, 0.0))
            code = code[:, seq * span : (seq + 1) * span]
            code = jnp.concatenate([code, jnp.zeros((120, span), f32)], axis=0)
            codes.append(code.T)
        code = jnp.concatenate(codes, axis=0)

        total_units = gate_weight.shape[0]
        units = total_units // expert_count
        cuts = [slice(i, min(i + 256, total_units)) for i in range(0, total_units, 256)]
        row = block * rows + lax.broadcasted_iota(jnp.int32, (rows, 1), 0)
        own = jnp.logical_and(row >= me * span, row < (me + 1) * span)
        for copy in context_copies:
            copy.wait()
        joined = jnp.concatenate(
            [
                jnp.concatenate(
                    [context[d, :, part * each : (part + 1) * each] for d in range(count)], axis=1
                )
                for part in range(members)
            ],
            axis=0,
        )
        context_out[...] = joined
        copies[0].start()
        tokens_copy.wait()
        hidden = tokens[...].astype(f32) + dot_nn(joined, out_weight[...])
        factor = lax.rsqrt(jnp.mean(hidden * hidden, axis=-1, keepdims=True) + epsilon)
        normed = (hidden * factor * gain[...]).astype(bf16)
        normed_out[...] = normed
        copies[1].start()
        logits = dot_nn(normed, router_weight[...])
        lane = lax.broadcasted_iota(jnp.int32, logits.shape, 1)
        logits = jnp.where(lane < expert_count, logits, -1e30)
        router = jnp.exp(logits - jnp.max(logits, axis=-1, keepdims=True))
        router = router / jnp.sum(router, axis=-1, keepdims=True)
        chosen = (code > 0.5).astype(f32)
        kept = (code > 1.5).astype(f32)
        pair_total = jnp.sum(router * chosen, axis=-1, keepdims=True)
        share = router * chosen / pair_total
        scale = share * kept
        for inside, copy in cotangent_copies:
            pl.when(inside)(copy.wait)
        copies[2].start()
        upstream = jnp.where(row < length, cotangent[...].astype(f32), 0.0)
        upstream_low = upstream.astype(bf16)
        root = 0.7978845608028654
        pair_grads = jnp.zeros(logits.shape, f32)
        scale_of = [jnp.broadcast_to(scale[:, e : e + 1], (rows, 128)) for e in range(expert_count)]
        part_sums = [jnp.zeros((rows, 128), f32) for e in range(expert_count)]
        lanes = lax.broadcasted_iota(jnp.int32, (rows, 128), 1)

        def front(number):
            cut = cuts[number]
            return (
                dot_nt(normed, gate_weight[cut, :]),
                dot_nt(normed, up_weight[cut, :]),
                dot_nt(upstream_low, down_weight[cut, :]),
            )

        ready = front(0)
        for number, cut in enumerate(cuts):
            now = ready
            if number + 1 < len(cuts):
                ready = front(number + 1)
            for first in range(cut.start, cut.stop, 128):
                wide = min(128, cut.stop - first)
                inside = slice(first - cut.start, first - cut.start + wide)
                gate_in, up_in, grad_hidden = (value[:, inside] for value in now)
                square = gate_in * gate_in
                bent = gate_in * (root + (root * 0.044715) * square)
                rise = 0.5 + 0.5 * jnp.tanh(bent)
                gelu = gate_in * rise
                slope = rise + (rise - rise * rise) * (6.0 * bent - (4.0 * root) * gate_in)
                hidden_unit = gelu * up_in
                product = hidden_unit * grad_hidden
                low_expert, high_expert = first // units, (first + wide - 1) // units
                scales = scale_of[low_expert][:, :wide]
                if low_expert == high_expert:
                    if wide < 128:
                        product = jnp.pad(product, ((0, 0), (0, 128 - wide)))
                    part_sums[low_expert] = part_sums[low_expert] + product
                else:
                    under = lanes[:, :wide] < high_expert * units - first
                    scales = jnp.where(under, scales, scale_of[high_expert][:, :wide])
                    part_sums[low_expert] = part_sums[low_expert] + jnp.where(under, product, 0.0)
                    part_sums[high_expert] = part_sums[high_expert] + jnp.where(under, 0.0, product)
                scaled_grad = scales * grad_hidden
                at = slice(first, first + wide)
                hidden_out[:, at] = (scales * hidden_unit).astype(bf16)
                grad_gate_out[:, at] = (scaled_grad * up_in * slope).astype(bf16)
                grad_up_out[:, at] = (scaled_grad * gelu).astype(bf16)
        for expert in range(expert_count):
            pair_sum = jnp.sum(part_sums[expert], axis=-1, keepdims=True)
            pair_grads = jnp.where(lane == expert, pair_sum, pair_grads)
        for copy in copies[3:6]:
            copy.start()
        mix = dot_nn(hidden_out[...], down_weight[...])
        grad = dot_nn(grad_gate_out[...], gate_weight[...]) + dot_nn(grad_up_out[...], up_weight[...])
        mix_out[...] = (mix + jnp.where(own, hidden, 0.0)).astype(bf16)
        for copy in mix_copies:
            copy.start()
        pair_grads = pair_grads * kept
        weighted = jnp.sum(pair_grads * share, axis=-1, keepdims=True)
        grad_router = chosen * (pair_grads - weighted) / pair_total
        grad_logits = router * (grad_router - jnp.sum(router * grad_router, axis=-1, keepdims=True))
        grad_logits = grad_logits.astype(bf16)
        logits_out[...] = grad_logits
        copies[7].start()
        grad = grad + dot_nt(grad_logits, router_weight[...])
        spread = hidden * factor
        gain_part = jnp.sum(grad * spread, axis=0, keepdims=True)
        if number_of_block == 0:
            gain_out[...] = gain_in[...]
        gain_out[0:1, :] += gain_part
        grad = grad * gain[...]
        middle = jnp.mean(grad * hidden, axis=-1, keepdims=True) * (factor * factor)
        back = factor * grad - spread * middle + jnp.where(own, upstream, 0.0)
        back = back.astype(bf16)
        grad_out[...] = back
        copies[6].start()
        grad_heads = dot_nt(back, out_weight[...]).astype(bf16)
        for d in range(count):
            for part in range(members):
                heads_out[d, :, part * each : (part + 1) * each] = grad_heads[
                    part * span : (part + 1) * span, d * each : (d + 1) * each
                ]
        heads_copy.start()
        return [*copies, *mix_copies, heads_copy]

    brought = [bring(number, block) for number, block in enumerate(blocks)]
    started = []
    for number, block in enumerate(blocks):
        started += work(number, block, brought[number], staged)
    for copy in started:
        copy.wait()


def experts(
    meta,
    where,
    tokens,
    pieces,
    gain,
    router_weight,
    ids,
    gain_in,
    weights,
    buffers,
    sums,
    sizes,
):
    seq, blocks = where
    count, span, seqs, expert_count, capacity = sizes
    seq_len, width = tokens.shape
    units = weights[1].shape[0]
    rows = 256
    each = width // count
    members = rows // span
    many = len(blocks)
    kinds = [(d, half) for d, half, piece in pieces]
    anywhere = pl.BlockSpec(memory_space=pl.ANY)
    low = lambda *shape: jax.ShapeDtypeStruct(shape, bf16)
    columns = [width] * 3 + [units] * 3 + [width, 128]
    aliased = list(buffers or []) + ([sums] if sums is not None else [])
    first = 2 + len(pieces) + 8
    targets = ([*range(8)] if buffers else []) + ([8] if sums is not None else [])
    static = (count, span, seqs, expert_count, capacity, seq, blocks, kinds, len(aliased))
    return pl.pallas_call(
        functools.partial(experts_kernel, static),
        out_shape=[low(seqs * seq_len, cols) for cols in columns]
        + [low(count, 2 * span, width), jax.ShapeDtypeStruct((8, width), f32)],
        in_specs=[pl.BlockSpec(memory_space=pltpu.SMEM)]
        + [anywhere] * (1 + len(pieces))
        + [whole_ref] * 8
        + [anywhere] * len(aliased),
        out_specs=[anywhere] * 9 + [whole_ref],
        scratch_shapes=[pltpu.VMEM((many, rows, cols), bf16) for cols in columns]
        + [
            pltpu.VMEM((many, count, span, members * each), bf16),
            pltpu.VMEM((many, rows, width), bf16),
            pltpu.VMEM((many, rows, width), bf16),
            pltpu.VMEM((many, count, span, members * each), bf16),
            pltpu.SemaphoreType.DMA((many, 9 + members)),
            pltpu.SemaphoreType.DMA((many, 1 + 2 * len(pieces))),
        ],
        input_output_aliases={first + i: target for i, target in enumerate(targets)},
        compiler_params=pltpu.CompilerParams(vmem_limit_bytes=36 * 2**20),
        cost_estimate=pl.CostEstimate(
            flops=2 * many * rows * width * (6 * units + 2 * width),
            bytes_accessed=1000,
            transcendentals=many * rows * units,
        ),
        name="experts",
    )(
        meta,
        tokens,
        *[piece for d, half, piece in pieces],
        gain,
        router_weight,
        ids,
        gain_in,
        *weights,
        *aliased,
    )


def block_sets(blocks, seq):
    step = 1 if seq == 0 else 2
    return [list(range(i, min(i + step, blocks))) for i in range(0, blocks, step)]


def attend_back_kernel(seq, head, heads, meta, queries_in, keys_in, values_in, *refs):
    own, right, left, bias, parts_out, sums_out = refs[:6]
    table, key_sum, value_sum, summed = refs[6:]
    length = meta[seq]
    _, seq_len, head_size = keys_in.shape
    span = right.shape[0]
    each = heads * head_size
    blocks = seq_len // 128
    summed[...] = (own[0].astype(f32) + right[...].astype(f32) + left[...].astype(f32)).astype(bf16)
    table[...] = jnp.zeros_like(table)
    keys = keys_in[0]
    values = values_in[0]
    for block in range(0, blocks, 2):
        rows = slice(block * 128, block * 128 + 256)
        queries = queries_in[0, rows, :]
        firsts = [
            part * each + head * head_size
            for part in range(block * 128 // span, (block * 128 + 256) // span)
        ]
        grads = jnp.concatenate(
            [summed[:, lane : lane + head_size] for lane in firsts], axis=0
        )
        first_row = (blocks - 1 - block) * 128
        added = jnp.concatenate(
            [
                bias[0, first_row : first_row + seq_len, :],
                bias[0, first_row - 128 : first_row - 128 + seq_len, :],
            ],
            axis=1,
        )
        scores = dot_nt(keys, queries)
        row = lax.broadcasted_iota(jnp.int32, scores.shape, 0)
        scores = jnp.where(row < length, scores + added, -1e30)
        top = jnp.max(scores, axis=0, keepdims=True)
        probs = jnp.exp(scores - top)
        probs = probs * (1.0 / jnp.sum(probs, axis=0, keepdims=True))
        product = probs * dot_nt(values, grads)
        delta = jnp.sum(product, axis=0, keepdims=True)
        grad_scores = product - probs * delta
        table[first_row : first_row + seq_len, :] += grad_scores[:, :128]
        table[first_row - 128 : first_row - 128 + seq_len, :] += grad_scores[:, 128:]
        scores_low = grad_scores.astype(bf16)
        key_part = dot_nn(scores_low, queries)
        value_part = dot_nn(probs.astype(bf16), grads)
        if block == 0:
            key_sum[...] = key_part
            value_sum[...] = value_part
        else:
            key_sum[...] += key_part
            value_sum[...] += value_part
        query_grad = dot_tn(keys, scores_low) * head_size ** (-0.5)
        parts_out[0, rows, :] = query_grad.T.astype(bf16)
    parts_out[1] = key_sum[...].astype(bf16)
    parts_out[2] = value_sum[...].astype(bf16)
    width = table.shape[0] + 128
    lines = jnp.concatenate(
        [table[first : first + 128, :].T for first in range(0, width - 128, 128)]
        + [jnp.zeros((128, 128), f32)],
        axis=1,
    )
    rows = 128
    while rows > 1:
        rows //= 2
        lines = lines[:rows] + pltpu.roll(lines[rows : 2 * rows], width - rows, 1)
    sums_out[...] = jnp.broadcast_to(pltpu.roll(lines, 127, 1), sums_out.shape)


def attend_back(meta, seq, head, heads, qkv, own, right, left, span, bias):
    _, seq_len, head_size = qkv.shape
    width = right.shape[1]
    part = lambda at: pl.BlockSpec((1, seq_len, head_size), lambda i, meta: (at, 0, 0))
    full = lambda *shape: pl.BlockSpec(shape, lambda i, meta: (0,) * len(shape))
    low = jax.ShapeDtypeStruct((3, seq_len, head_size), bf16)
    return pl.pallas_call(
        functools.partial(attend_back_kernel, seq, head, heads),
        out_shape=(low, jax.ShapeDtypeStruct((8, 2 * seq_len), f32)),
        grid_spec=pltpu.PrefetchScalarGridSpec(
            num_scalar_prefetch=1,
            grid=(1,),
            in_specs=[part(head), part(heads + head), part(2 * heads + head)]
            + [full(1, span, width), full(span, width), full(span, width)]
            + [pl.BlockSpec((1,) + bias.shape[1:], lambda i, meta: (head, 0, 0))],
            out_specs=[full(3, seq_len, head_size), full(8, 2 * seq_len)],
            scratch_shapes=[
                pltpu.VMEM(bias.shape[1:], f32),
                pltpu.VMEM((seq_len, head_size), f32),
                pltpu.VMEM((seq_len, head_size), f32),
                pltpu.VMEM((span, width), bf16),
            ],
        ),
        compiler_params=pltpu.CompilerParams(vmem_limit_bytes=28 * 2**20),
        cost_estimate=pl.CostEstimate(
            flops=6 * 10**9, bytes_accessed=1000, transcendentals=seq_len * seq_len
        ),
        name="attend_back",
    )(meta, qkv, qkv, qkv, own, right, left, bias)


def norm_back_kernel(heads, first, meta, *refs):
    parts, (tokens, weight, grad_in, grad_out, parts_out, gain_out) = refs[:heads], refs[heads:]

    @pl.when(pl.program_id(0) == 0)
    def _():
        gain_out[...] = jnp.zeros_like(gain_out)

    low = jnp.concatenate([part[kind] for kind in range(3) for part in parts], axis=1)
    wide = tokens[...].astype(f32)
    factor = lax.rsqrt(jnp.mean(wide * wide, axis=-1, keepdims=True) + epsilon)
    upstream = dot_nt(low, weight[...])
    spread = wide * factor
    gain_out[0:1, :] += jnp.sum(upstream * spread, axis=0, keepdims=True)
    middle = jnp.mean(upstream * wide, axis=-1, keepdims=True) * (factor * factor)
    back = factor * upstream - spread * middle + grad_in[...].astype(f32)
    back = back.astype(bf16)
    span = grad_out.shape[1]
    members = back.shape[0] // span
    for part in range(members):
        distance = meta[first + pl.program_id(0) * members + part]
        grad_out[distance] = back[part * span : (part + 1) * span, :]
    parts_out[...] = (low.astype(f32) * factor).astype(bf16)


def norm_back(meta, seq, seqs, parts, tokens, weight, grad_in, count):
    seq_len, width = tokens.shape
    head_size = parts[0].shape[2]
    rows, span = 256, seq_len // count
    by_row = lambda cols, at=0: pl.BlockSpec((rows, cols), lambda i, meta: (at + i, 0))
    columns = 3 * head_size * len(parts)
    return pl.pallas_call(
        functools.partial(norm_back_kernel, len(parts), seqs + count),
        out_shape=(
            jax.ShapeDtypeStruct((count, span, width), bf16),
            jax.ShapeDtypeStruct((seq_len, columns), bf16),
            jax.ShapeDtypeStruct((8, width), f32),
        ),
        grid_spec=pltpu.PrefetchScalarGridSpec(
            num_scalar_prefetch=1,
            grid=(seq_len // rows,),
            in_specs=[pl.BlockSpec((3, rows, head_size), lambda i, meta: (0, i, 0))] * len(parts)
            + [
                by_row(width),
                pl.BlockSpec(weight.shape, lambda i, meta: (0, 0)),
                by_row(width, seq * (seq_len // rows)),
            ],
            out_specs=(
                pl.BlockSpec((count, span, width), lambda i, meta: (0, 0, 0)),
                by_row(columns),
                pl.BlockSpec((8, width), lambda i, meta: (0, 0)),
            ),
        ),
        compiler_params=pltpu.CompilerParams(vmem_limit_bytes=24 * 2**20),
        cost_estimate=pl.CostEstimate(
            flops=2 * seq_len * width * columns, bytes_accessed=1000, transcendentals=0
        ),
        name="norm_back",
    )(meta, *parts, tokens, weight, grad_in)


def spread_kernel(reps, spots, *refs):
    parts, gain, outs = refs[:reps], refs[reps], refs[reps + 1 :]
    count, _, columns = parts[0].shape
    cut = gain.shape[0] // reps
    each = columns // 3
    for number, part in enumerate(parts):
        rows = pl.ds(pl.multiple_of(spots[number] * cut, cut), cut)
        scale = gain[rows, :]
        for owner in range(count):
            block = part[owner, :cut, :].astype(f32) * scale
            for kind, out in enumerate(outs):
                out[rows, owner * each : (owner + 1) * each] = block[:, kind * each : (kind + 1) * each]


def spread(parts, spots, found, gain):
    count, _, columns = parts[0].shape
    cut, each = gain.shape[0] // len(parts), columns // 3
    if cut % 8:
        whole = jnp.take(jnp.stack(parts), found, axis=0)[:, :, :cut].astype(f32)
        whole = whole.reshape(len(parts), count, cut, 3, each).transpose(3, 0, 2, 1, 4)
        whole = whole.reshape(3, gain.shape[0], count * each) * gain[None, :, None]
        return whole[0], whole[1], whole[2]
    shape = jax.ShapeDtypeStruct((gain.shape[0], count * each), f32)
    return pl.pallas_call(
        functools.partial(spread_kernel, len(parts)),
        out_shape=(shape,) * 3,
        in_specs=[pl.BlockSpec(memory_space=pltpu.SMEM)] + [whole_ref] * (len(parts) + 1),
        out_specs=[whole_ref] * 3,
        compiler_params=pltpu.CompilerParams(vmem_limit_bytes=12 * 2**20),
        name="spread",
    )(spots, *parts, gain.reshape(-1, 1))


def body(
    tokens,
    lengths,
    expert_ids,
    buckets,
    norm1_gain,
    w_query,
    w_key,
    w_value,
    w_out,
    rel_bias,
    norm2_gain,
    w_router,
    w_gate,
    w_up,
    w_down,
    cotangent,
):
    seqs, span, width = tokens.shape
    count = lax.axis_size("shard")
    reps = lax.axis_size("rep")
    me = lax.axis_index("shard")
    rep = lax.axis_index("rep")
    seq_len = span * count
    expert_count, unit_count, _ = w_gate.shape
    heads = rel_bias.shape[1]
    head_size = w_query.shape[1] // (count * heads)
    each = heads * head_size
    feats = w_query.shape[0]
    cut = feats // reps
    row_count = seqs * span
    capacity = 10 * row_count // (4 * expert_count)
    place = ring_place(me, count)
    distances = jnp.arange(count, dtype=jnp.int32)
    owners = ring_index((place + distances) % count, count)
    distance_of = (ring_place(distances, count) - place) % count
    meta = jnp.concatenate([lengths, owners, distance_of, me[None]]).astype(jnp.int32)

    def line(values):
        flat = values.reshape(-1).astype(bf16)
        return jnp.pad(flat, (0, width - flat.shape[0]))[None]

    packed = jnp.concatenate(
        [
            tokens.reshape(row_count, width),
            lax.dynamic_slice_in_dim(w_out, rep * cut, cut, 0),
            line(expert_ids.reshape(row_count, 2).T),
            line(jnp.concatenate([norm2_gain, w_router.reshape(-1)])),
            jnp.zeros((14, width), bf16),
        ],
        axis=0,
    )
    extra = row_count
    token_ring = Gather(
        packed,
        count,
        lambda value: (
            jnp.concatenate([value[:span], value[extra:]], axis=0),
            value[span:extra],
        ),
    )
    hops = []
    while not token_ring.done:
        fire([token_ring])
        hops.append(token_ring.last())

    gain_one = norm1_gain.astype(f32)
    own_qkv = jnp.stack([w_query, w_key, w_value], axis=1)
    own_cut = lax.dynamic_slice_in_dim(own_qkv, rep * cut, cut, 0).astype(f32)
    own_cut = own_cut * lax.dynamic_slice_in_dim(gain_one, rep * cut, cut, 0)[:, None, None]
    own_cut = own_cut.astype(bf16).reshape(cut, 3, count, each).transpose(2, 0, 1, 3)
    qkv_weight = lax.all_to_all(
        own_cut.reshape(count, cut, 3 * each), "shard", split_axis=0, concat_axis=0, tiled=True
    )
    qkv_weight = weave(*rep_parts(after(qkv_weight, hops[1]), reps, rep))

    bucket_count = rel_bias.shape[0]
    bucket_hot = (
        buckets[:, None] == jnp.arange(bucket_count, dtype=jnp.int32)[None, :]
    ).astype(f32)
    bucket_hot = jnp.pad(bucket_hot, ((0, 1), (0, 0)))
    bias_vec = jnp.einsum("rb,bh->hr", bucket_hot, rel_bias.astype(f32), precision=highest)
    bias, bias_turned = bias_tables(bias_vec)

    def sent(rings):
        return tuple(ring.last() for ring in rings if ring.last()[0] is not None)

    attended, mixed_rings, rings = [], [], []
    waits = token_ring.last()
    for s in range(seqs):
        fire(rings, waits)
        attended.append(
            attend(
                after(meta, waits),
                s,
                seqs,
                token_ring.pieces,
                cotangent[s],
                qkv_weight,
                bias,
                heads,
                head_size,
            )
        )
        waits = (attended[s][2], sent(rings))
        if s == 0:
            riders = attended[s][3]
            out_parts = rep_parts(riders[:, :cut], reps, rep)
        mixed_rings.append(Gather(attended[s][2], count))
        rings = [mixed_rings[0]]
    while not rings[0].done:
        fire(rings, waits)
        waits = lasts(rings)

    out_weight = weave(*out_parts)
    ids = riders[:, cut].astype(f32)
    small = jnp.take(riders[:, cut + 1], distance_of, axis=0)
    gain_two = small[:, :feats].astype(f32).reshape(1, width)
    router_weight = small[:, feats : feats * (1 + expert_count)].reshape(width, expert_count)
    router_weight = jnp.pad(router_weight, ((0, 0), (0, 128 - expert_count)))
    expert_weights = [out_weight] + [
        weight.reshape(expert_count * unit_count, width) for weight in (w_gate, w_up, w_down)
    ]

    sizes = (count, span, seqs, expert_count, capacity)
    buffers = None
    gain_part = jnp.zeros((8, width), f32)
    sums_all, sum_rings = [], []
    rings = [mixed_rings[1]]
    for s in range(seqs):
        if s > 0:
            while not rings[0].done:
                fire(rings, waits)
                waits = lasts(rings)
            sum_rings.append(Sum([(sums_all[s - 1], 0, 2 * span)], count))
            rings = [sum_rings[s - 1]]
        sums = None
        for blocks in block_sets(seq_len // 256, s):
            if not rings[0].done:
                fire(rings, waits)
            *buffers, sums, gain_part = experts(
                after(meta, waits),
                (s, blocks),
                attended[s][0],
                mixed_rings[s].pieces,
                gain_two,
                router_weight,
                ids,
                gain_part,
                expert_weights,
                buffers,
                sums,
                sizes,
            )
            waits = (gain_part, sent(rings))
        sums_all.append(sums)
    context_rows, normed, cot_rows, hidden, grad_gate, grad_up, grad_rows, grad_logits = buffers

    offset_sums, totals, finished, scaled_all, gain_one_part = [], [], [], [], []

    def total_grad(left_side, right_side, waits):
        grads = dot_tn(after(left_side, waits), right_side).astype(bf16)
        totals.append(RepTotal(grads, reps, rep))
        return grads

    def step(rings, waits):
        live = [ring for ring in rings if not ring.done]
        if live:
            fire(live, waits)

    def back_head(s, head, waits):
        made = attend_back(
            after(meta, waits),
            s,
            head,
            heads,
            attended[s][1],
            sums_all[s],
            *sum_rings[s].last(),
            span,
            bias_turned,
        )
        offset_sums.append((head, made[1]))
        return made[0]

    def back_norm(s, parts, waits):
        grads, scaled, gain_rows = norm_back(
            after(meta, waits), s, seqs, parts, attended[s][0], qkv_weight, grad_rows, count
        )
        scaled_all.append(scaled)
        gain_one_part.append(gain_rows)
        return grads

    sum_rings.append(Sum([(sums_all[1], 0, 2 * span)], count))
    first, second = sum_rings
    rings = [first]
    step(rings, waits)
    done = total_grad(hidden, cot_rows, waits)
    rings = [first, second]
    waits = (done, sent(rings))
    step(rings, waits)
    out_grad = dot_tn(after(context_rows, waits), grad_rows).astype(bf16)
    router_grad = dot_tn(normed, grad_logits)[:, :expert_count]
    flat = jnp.concatenate(
        [gain_part[0].reshape(count, feats), router_grad.reshape(count, feats * expert_count)], axis=1
    ).astype(bf16)
    flat = jnp.take(flat, owners, axis=0)
    small_size = flat.shape[1] // 2
    flat = jnp.pad(flat.reshape(count, 2, 1, small_size), ((0, 0), (0, 0), (0, 15), (0, width - small_size)))
    out_whole = jnp.concatenate([out_grad.reshape(count, 2, each // 2, width), flat], axis=2)
    side = rep % 2
    out_kept = lax.dynamic_index_in_dim(out_whole, side, 1, keepdims=False)
    out_got = swap(lax.dynamic_index_in_dim(out_whole, 1 - side, 1, keepdims=False), "rep", reps, 1)
    done = total_grad(grad_gate, normed, (waits, out_grad))
    waits = (done, sent(rings))
    while not first.done:
        step(rings, waits)
        waits = lasts(rings)
    rings = [second]
    parts = []
    for head in range(heads):
        step(rings, waits)
        parts.append(back_head(0, head, waits))
        waits = (parts[-1], sent(rings))
        if head == 0:
            totals[0].cross()
            out_grad = add_low(out_kept, out_got)
            waits = waits + (totals[0].kept, out_grad)
    totals[1].cross()
    waits = waits + (totals[1].kept,)
    grads_first = back_norm(0, parts, waits)
    waits = (grads_first, waits)
    final = [Sum([(grads_first, 0, span), (out_grad, 0, out_grad.shape[1])], count)]
    rings = [second, final[0]]
    step(rings, waits)
    done = total_grad(grad_up, normed, (waits, totals[0].got))
    waits = (done, sent(rings))
    while not second.done:
        step(rings, waits)
        waits = lasts(rings)
    rings = [final[0]]
    parts = []
    for head in range(heads):
        step(rings, waits)
        parts.append(back_head(1, head, waits))
        waits = (parts[-1], sent(rings))
        if head == 0:
            totals[2].cross()
            waits = waits + (totals[2].kept, totals[1].got)
    step(rings, waits)
    grads_last = back_norm(1, parts, waits)
    final.append(Sum([(grads_last, 0, span)], count))
    waits = (grads_last, sent(rings))
    rings = final
    while not all(ring.done for ring in rings):
        step(rings, waits)
        waits = lasts(rings)

    mix_first, mix_last, final_first, final_last = (
        ring.total() for ring in (*sum_rings, *final)
    )
    grad_tokens = jnp.stack([final_first[:span], final_last])
    positions = me * span + jnp.arange(span, dtype=jnp.int32)
    live_mask = (positions[None, :] < lengths[:, None]).astype(f32)[:, :, None]
    block_out = (live_mask * jnp.stack([mix_first[span:], mix_last[span:]])).astype(bf16)
    out_own = final_first[span:].astype(bf16)
    for bit in bits_of(reps)[1:]:
        out_own = add_low(out_own, swap(out_own, "rep", reps, bit))
    out_other = swap(out_own, "rep", reps, 1)
    out_both = jnp.where(
        side == 0, jnp.stack([out_own, out_other]), jnp.stack([out_other, out_own])
    ).astype(f32)
    total_out = out_both[:, : each // 2].reshape(feats, width)
    flat = out_both[:, each // 2, :small_size].reshape(-1)
    total_gain_two = flat[:feats]
    total_router = flat[feats:].reshape(feats, expert_count)

    qkv_grad = sum(dot_tn(attended[s][0], scaled_all[s]) for s in range(seqs)).astype(bf16)
    offsets = jnp.stack(
        [sum(part[0] for h, part in offset_sums if h == head) for head in range(heads)]
    )
    bias_grad = jnp.einsum("hr,rb->hb", offsets, bucket_hot, precision=highest)
    gain_rows = sum(part[0] for part in gain_one_part).reshape(count, reps, 1, cut)
    bias_rows = jnp.broadcast_to(
        bias_grad.reshape(1, reps, 1, -1), (count, reps, 1, bias_grad.size // reps)
    )
    flat = jnp.concatenate([gain_rows, bias_rows], axis=3).astype(bf16)
    flat = jnp.pad(flat, ((0, 0), (0, 0), (0, 15), (0, 3 * each - flat.shape[3])))
    qkv_grad = jnp.concatenate([qkv_grad.reshape(count, reps, cut, 3 * each), flat], axis=2)
    qkv_grad = rep_scatter(qkv_grad.transpose(1, 0, 2, 3), reps, rep, totals[2].got)
    qkv_grad = lax.all_to_all(qkv_grad, "shard", split_axis=0, concat_axis=0, tiled=True)
    bias_size = bias_grad.size // reps
    parts, spots = rep_parts(qkv_grad, reps, rep)
    found = jnp.take(jnp.array(rep_order(reps), jnp.int32), rep ^ jnp.arange(reps))
    qkv_grad = spread(parts, spots, found, gain_one)
    tail = jnp.take(jnp.stack([part[:, cut] for part in parts]), found, axis=0).astype(f32)
    total_gain_one = jnp.sum(tail[:, :, :cut], axis=1).reshape(feats) / gain_one
    total_bias = lax.dynamic_index_in_dim(tail, me, 1, keepdims=False)[:, cut : cut + bias_size]
    total_bias = total_bias.reshape(heads, bucket_count).T

    total_down, total_gate, total_up = (
        total.finish().reshape(expert_count, unit_count, width) for total in totals
    )
    return (
        block_out,
        grad_tokens,
        total_gain_one,
        qkv_grad[0],
        qkv_grad[1],
        qkv_grad[2],
        total_out,
        total_bias,
        total_gain_two,
        total_router,
        total_gate,
        total_up,
        total_down,
    )


def solution(mesh):
    rows = P("rep", "shard", None)
    first = P("shard")
    weight = P("shard", None)
    expert = P(None, "shard", None)
    return jax.shard_map(
        body,
        mesh=mesh,
        in_specs=(rows, P("rep"), rows, P(), first, weight, weight, weight, weight)
        + (P(None, "shard"), first, weight, expert, expert, expert, rows),
        out_specs=(rows, rows, first, weight, weight, weight, weight)
        + (P(None, "shard"), first, weight, expert, expert, expert),
        check_vma=False,
    )
```

```python
import functools

import jax
import jax.numpy as jnp
from jax import lax
from jax.experimental import pallas as pl
from jax.experimental.pallas import tpu as pltpu
from jax.sharding import PartitionSpec as P

epsilon = 1e-06
highest = lax.Precision.HIGHEST
bf16 = jnp.bfloat16
f32 = jnp.float32
vmem_limit = 58 * 1024 * 1024
whole_ref = pl.BlockSpec(memory_space=pltpu.VMEM)


def dot_nt(left, right):
    return lax.dot_general(left, right, (((1,), (1,)), ((), ())), preferred_element_type=f32)


def dot_tn(left, right):
    return lax.dot_general(left, right, (((0,), (0,)), ((), ())), preferred_element_type=f32)


def dot_nn(left, right):
    return lax.dot_general(left, right, (((1,), (0,)), ((), ())), preferred_element_type=f32)


def ring_index(place, count):
    return jnp.where(place < count // 2, 2 * place, 2 * count - 1 - 2 * place)


def ring_place(index, count):
    return jnp.where(index % 2 == 0, index // 2, count - 1 - index // 2)


def ring_send(value, step, count):
    order = [2 * i if i < count // 2 else 2 * count - 1 - 2 * i for i in range(count)]
    pairs = [(order[i], order[(i + step) % count]) for i in range(count)]
    return lax.ppermute(value, "shard", pairs)


def after(value, *waits):
    if not jax.tree.leaves(waits):
        return value
    flat, tree = jax.tree.flatten(value)
    held = lax.optimization_barrier(tuple(flat) + tuple(jax.tree.leaves(waits)))
    return tree.unflatten(held[: len(flat)])


def halve(value):
    half = value.shape[0] // 2
    return value[:half], value[half:]


class Gather:
    def __init__(self, value, count, split=None):
        self.count, self.step, self.split = count, 1, split or halve
        self.ahead = self.behind = value
        self.pieces = [(0, None, value)]
        self.done = False

    def hop(self, *waits):
        behind, ahead = after((self.behind, self.ahead), *waits)
        far = self.count // 2
        if self.step < far:
            self.behind = ring_send(behind, 1, self.count)
            self.ahead = ring_send(ahead, -1, self.count)
            self.pieces += [(self.count - self.step, None, self.behind), (self.step, None, self.ahead)]
            self.step += 1
        else:
            self.behind = ring_send(self.split(behind)[0], 1, self.count)
            self.ahead = ring_send(self.split(ahead)[1], -1, self.count)
            self.pieces += [(far, 0, self.behind), (far, 1, self.ahead)]
            self.done = True

    def last(self):
        return (self.behind, self.ahead)


def add_low(left, right):
    return (left.astype(f32) + right.astype(f32)).astype(bf16)


def ring_add_kernel(half, firsts, right, left, *refs):
    count = len(firsts)
    owns = (refs[:count], refs[count : 2 * count])
    outs = refs[2 * count :]
    total = outs[0].shape[0]
    for come, own, out, begin in zip((right, left), owns, outs, (0, total - half)):
        for source, first in zip(own, firsts):
            last = first + source.shape[1]
            low, high = max(first, begin), min(last, begin + half)
            if low < high:
                summed = source[0, low - first : high - first, :].astype(f32)
                summed = summed + come[low - begin : high - begin, :].astype(f32)
                out[low:high, :] = summed.astype(bf16)
            if first < min(low, last):
                out[first : min(low, last), :] = source[0, : min(low, last) - first, :]
            if max(high, first) < last:
                out[max(high, first) : last, :] = source[0, max(high, first) - first :, :]


def ring_add(right, left, own_right, own_left, rows):
    width = right.shape[1]
    total = sum(rows)
    firsts = [sum(rows[:i]) for i in range(len(rows))]
    full = lambda *shape: pl.BlockSpec(shape, lambda i: (0,) * len(shape))
    part = lambda spot, count: pl.BlockSpec((1, count, width), lambda i: (spot[1], spot[2], 0))
    shape = jax.ShapeDtypeStruct((total, width), bf16)
    return pl.pallas_call(
        functools.partial(ring_add_kernel, right.shape[0], firsts),
        out_shape=(shape, shape),
        grid=(1,),
        in_specs=[full(*right.shape)] * 2
        + [part(spot, count) for spot, count in zip(own_right, rows)]
        + [part(spot, count) for spot, count in zip(own_left, rows)],
        out_specs=(full(total, width),) * 2,
        compiler_params=pltpu.CompilerParams(vmem_limit_bytes=14 * 2**20),
        cost_estimate=pl.CostEstimate(
            flops=2 * total * width, bytes_accessed=1000, transcendentals=0
        ),
        name="ring_add",
    )(right, left, *[spot[0] for spot in own_right], *[spot[0] for spot in own_left])


class Sum:
    def __init__(self, sources, count):
        self.sources, self.count, self.step = sources, count, count // 2
        self.rows = [rows for array, block, rows in sources]
        self.right = self.left = None
        self.done = False

    def chunk(self, distance):
        return jnp.concatenate(
            [array[distance, block * rows : (block + 1) * rows] for array, block, rows in self.sources],
            axis=0,
        )

    def hop(self, *waits):
        if self.right is None:
            right, left = halve(self.chunk(self.step))
        else:
            spots = [
                [(array, distance, block) for array, block, rows in self.sources]
                for distance in (self.step, self.count - self.step)
            ]
            right, left = ring_add(self.right, self.left, *spots, self.rows)
        right, left = after((right, left), *waits)
        self.right = ring_send(right, 1, self.count)
        self.left = ring_send(left, -1, self.count)
        self.step -= 1
        self.done = self.step == 0

    def last(self):
        return (self.right, self.left)


def total_of(ring):
    total = ring.chunk(0).astype(f32)
    return total + ring.right.astype(f32) + ring.left.astype(f32)


def fire(rings, *waits):
    rings = [ring for ring in rings if not ring.done]
    waits = waits + tuple(ring.last() for ring in rings if ring.last()[0] is not None)
    for ring in rings:
        ring.hop(*waits)


def lasts(rings):
    return tuple(ring.last() for ring in rings)


def swap(value, axis, count, bit):
    return lax.ppermute(value, axis, [(i, i ^ bit) for i in range(count)])


def bits_of(count):
    return [1 << i for i in range(count.bit_length() - 1)]


def rep_scatter(value, count, me, *waits):
    for bit in bits_of(count):
        value = value.reshape((value.shape[0] // 2, 2) + value.shape[1:])
        side = (me // bit) % 2
        sent = lax.dynamic_index_in_dim(value, 1 - side, 1, keepdims=False)
        kept = lax.dynamic_index_in_dim(value, side, 1, keepdims=False)
        if bit > 1:
            sent = after(sent, *waits)
        value = add_low(kept, swap(sent, "rep", count, bit))
    return value[0]


def rep_parts(value, count, me):
    parts, tags = [value], [0]
    for bit in bits_of(count)[::-1]:
        parts = parts + [swap(part, "rep", count, bit) for part in parts]
        tags = tags + [tag ^ bit for tag in tags]
    return parts, (me ^ jnp.array(tags, jnp.int32))


def rep_order(count):
    tags = [0]
    for bit in bits_of(count)[::-1]:
        tags = tags + [tag ^ bit for tag in tags]
    return [tags.index(tag) for tag in range(count)]


def weave_kernel(count, spots, *refs):
    parts, out, sems = refs[:count], refs[count], refs[count + 1]
    copies = [
        pltpu.make_async_copy(part, out.at[:, spots[i]], sems.at[i])
        for i, part in enumerate(parts)
    ]
    for copy in copies:
        copy.start()
    for copy in copies:
        copy.wait()


def weave(parts, spots):
    first, rows, columns = parts[0].shape
    anywhere = pl.BlockSpec(memory_space=pl.ANY)
    out = pl.pallas_call(
        functools.partial(weave_kernel, len(parts)),
        out_shape=jax.ShapeDtypeStruct((first, len(parts), rows, columns), parts[0].dtype),
        in_specs=[pl.BlockSpec(memory_space=pltpu.SMEM)] + [anywhere] * len(parts),
        out_specs=anywhere,
        scratch_shapes=[pltpu.SemaphoreType.DMA((len(parts),))],
        compiler_params=pltpu.CompilerParams(vmem_limit_bytes=2**20),
        name="weave",
    )(spots, *parts)
    return out.reshape(first * len(parts) * rows, columns)


def widen_kernel(parts, meta, kept, got, kept_other, got_other, out, *scratch):
    held, wide, in_sems, out_sems = scratch
    half = kept.shape[0]
    rows = half // parts
    sources = (kept, got, kept_other, got_other)
    ins = [
        [
            pltpu.make_async_copy(
                source.at[pl.ds(part * rows, rows), :],
                held.at[number, pl.ds(part * rows, rows), :],
                in_sems.at[number * parts + part],
            )
            for number, source in enumerate(sources)
        ]
        for part in range(parts)
    ]
    for part in range(parts):
        for copy in ins[part]:
            copy.start()
    outs = []
    for part in range(parts):
        for copy in ins[part]:
            copy.wait()
        at = slice(part * rows, (part + 1) * rows)
        for pair in range(2):
            total = held[2 * pair, at, :].astype(f32) + held[2 * pair + 1, at, :].astype(f32)
            wide[pair, at, :] = total
            side = meta[0] if pair == 0 else 1 - meta[0]
            start = pl.multiple_of(side * half + part * rows, 8)
            outs.append(
                pltpu.make_async_copy(
                    wide.at[pair, pl.ds(part * rows, rows), :],
                    out.at[pl.ds(start, rows), :],
                    out_sems.at[pair * parts + part],
                )
            )
            outs[-1].start()
    for copy in outs:
        copy.wait()


def widen(side, kept, got, kept_other, got_other):
    half, width = kept.shape
    parts = 4 if half % 64 == 0 else 2 if half % 32 == 0 else 1
    anywhere = pl.BlockSpec(memory_space=pl.ANY)
    return pl.pallas_call(
        functools.partial(widen_kernel, parts),
        out_shape=jax.ShapeDtypeStruct((2 * half, width), f32),
        in_specs=[pl.BlockSpec(memory_space=pltpu.SMEM)] + [anywhere] * 4,
        out_specs=anywhere,
        scratch_shapes=[
            pltpu.VMEM((4, half, width), bf16),
            pltpu.VMEM((2, half, width), f32),
            pltpu.SemaphoreType.DMA((4 * parts,)),
            pltpu.SemaphoreType.DMA((2 * parts,)),
        ],
        compiler_params=pltpu.CompilerParams(vmem_limit_bytes=16 * 2**20),
        name="widen",
    )(side, kept, got, kept_other, got_other)


class RepTotal:
    def __init__(self, value, count, me):
        self.count, self.side = count, me % 2
        value = value.reshape((2, value.shape[0] // 2) + value.shape[1:])
        sent = lax.dynamic_index_in_dim(value, 1 - self.side, 0, keepdims=False)
        self.kept = lax.dynamic_index_in_dim(value, self.side, 0, keepdims=False)
        self.got = swap(sent, "rep", count, 1)

    def cross(self, *waits):
        kept = add_low(self.kept, self.got)
        for bit in bits_of(self.count)[1:-1]:
            kept = add_low(kept, swap(kept, "rep", self.count, bit))
        self.kept = after(kept, *waits)
        self.got = swap(self.kept, "rep", self.count, self.count // 2)
        self.kept_other = swap(self.kept, "rep", self.count, 1)

    def finish(self):
        got_other = swap(self.got, "rep", self.count, 1)
        side = self.side.reshape(1).astype(jnp.int32)
        return widen(side, self.kept, self.got, self.kept_other, got_other)


def bias_kernel(vec, table, turned):
    heads, _, width = table.shape
    for head in range(heads):
        line = jnp.broadcast_to(vec[head : head + 1, :], (128, vec.shape[1]))
        line = pltpu.roll(line, vec.shape[1] - 127, 1, stride=1, stride_axis=0)
        table[head] = line[:, :width]
        for first in range(0, width, 128):
            turned[head, first : first + 128, :] = line[:, first : first + 128].T


def bias_tables(vec):
    heads, length = vec.shape
    width = length - 128
    return pl.pallas_call(
        bias_kernel,
        out_shape=(
            jax.ShapeDtypeStruct((heads, 128, width), f32),
            jax.ShapeDtypeStruct((heads, width, 128), f32),
        ),
        in_specs=[whole_ref],
        out_specs=[whole_ref] * 2,
        compiler_params=pltpu.CompilerParams(vmem_limit_bytes=24 * 2**20),
        name="bias_tables",
    )(vec)


def attend_kernel(seq, seqs, places, heads, head_size, riders, meta, *refs):
    pieces = refs[: len(places)]
    cotangent, weight, bias, tokens_out, qkv_out, mixed_out, *more = refs[len(places) :]
    sems = more[-1]
    length = meta[seq]
    span = cotangent.shape[0]
    seq_len = tokens_out.shape[0]
    each = heads * head_size
    blocks = seq_len // 128
    copies = []
    for number, ((distance, first), piece) in enumerate(zip(places, pieces)):
        start = pl.multiple_of(meta[seqs + distance] * span, 16)
        copies.append(
            pltpu.make_async_copy(
                piece.at[pl.ds(first, span), :],
                tokens_out.at[pl.ds(start, span), :],
                sems.at[number],
            )
        )
        copies[-1].start()
    for number, (distance, first) in enumerate(riders):
        copies.append(
            pltpu.make_async_copy(
                pieces[number].at[pl.ds(first, more[0].shape[1]), :],
                more[0].at[distance],
                sems.at[len(places) + number],
            )
        )
        copies[-1].start()
    mixed_out[0:span, :] = cotangent[...]
    for copy in copies:
        copy.wait()
    for first in range(0, seq_len, 256):
        rows = slice(first, first + 256)
        low = tokens_out[rows, :]
        wide = low.astype(f32)
        factor = lax.rsqrt(jnp.mean(wide * wide, axis=-1, keepdims=True) + epsilon)
        made = dot_nn(low, weight[...]) * factor
        for part in range(3 * heads):
            cut = made[:, part * head_size : (part + 1) * head_size]
            if part < heads:
                cut = cut.astype(bf16).astype(f32) * head_size ** (-0.5)
            qkv_out[part, rows, :] = cut.astype(bf16)
    for head in range(heads):
        keys = qkv_out[heads + head]
        values = qkv_out[2 * heads + head]
        for block in range(0, blocks, 2):
            queries = qkv_out[head, block * 128 : block * 128 + 256, :]
            scores = dot_nt(queries, keys)
            first_col = (blocks - 1 - block) * 128
            added = jnp.concatenate(
                [
                    bias[head, :, first_col : first_col + seq_len],
                    bias[head, :, first_col - 128 : first_col - 128 + seq_len],
                ],
                axis=0,
            )
            column = lax.broadcasted_iota(jnp.int32, scores.shape, 1)
            scores = jnp.where(column < length, scores + added, -1e30)
            top = jnp.max(scores, axis=-1, keepdims=True)
            weights = jnp.exp(scores - top)
            total = jnp.sum(weights, axis=-1, keepdims=True)
            mixed = dot_nn(weights.astype(bf16), values) / total
            mixed = mixed.astype(bf16)
            for part in range(256 // span):
                lane = (block * 128 // span + part) * each + head * head_size
                mixed_out[span : 2 * span, lane : lane + head_size] = mixed[
                    part * span : (part + 1) * span, :
                ]


def attend(meta, seq, seqs, pieces, cotangent, weight, bias, heads, head_size):
    width = weight.shape[0]
    span = cotangent.shape[0]
    pieces = [(d, half, piece) for d, half, piece in pieces if half is None or half == seq]
    places = [(d, seq * span if half is None else 0) for d, half, piece in pieces]
    seq_len = span * len(pieces)
    full = lambda *shape: pl.BlockSpec(shape, lambda i, meta: (0,) * len(shape))
    shapes = [(seq_len, width), (3 * heads, seq_len, head_size), (2 * span, width)]
    riders = []
    if seq == 0:
        extra = pieces[0][2].shape[0] - seqs * span
        riders = [(d, seqs * span if half is None else span) for d, half, piece in pieces]
        shapes.append((len(pieces), extra, width))
    return pl.pallas_call(
        functools.partial(attend_kernel, seq, seqs, places, heads, head_size, riders),
        out_shape=tuple(jax.ShapeDtypeStruct(shape, bf16) for shape in shapes),
        grid_spec=pltpu.PrefetchScalarGridSpec(
            num_scalar_prefetch=1,
            grid=(1,),
            in_specs=[pl.BlockSpec(memory_space=pl.ANY)] * len(pieces)
            + [full(*cotangent.shape), full(*weight.shape), full(*bias.shape)],
            out_specs=[full(*shape) for shape in shapes],
            scratch_shapes=[pltpu.SemaphoreType.DMA((2 * len(pieces),))],
        ),
        compiler_params=pltpu.CompilerParams(vmem_limit_bytes=28 * 2**20),
        cost_estimate=pl.CostEstimate(
            flops=8 * 10**9, bytes_accessed=1000, transcendentals=heads * seq_len * seq_len
        ),
        name="attend",
    )(meta, *[piece for d, half, piece in pieces], cotangent, weight, bias)


def experts_kernel(static, meta, *refs):
    count, span, seqs, expert_count, capacity, seq, blocks, kinds, alias_count = static
    tokens_hbm, *pieces = refs[: 1 + len(kinds)]
    refs = refs[1 + len(kinds) :]
    gain, router_weight, ids, gain_in, out_weight, gate_weight, up_weight, down_weight = refs[:8]
    refs = refs[8 + alias_count :]
    buffers, sums_out, gain_out, refs = refs[:8], refs[8], refs[9], refs[10:]
    staged, refs = refs[:8], refs[8:]
    heads_all, mix_all, tokens_all, context_all, sems_all, in_sems_all = refs
    _, rows, width = tokens_all.shape
    each = width // count
    seq_len = span * count
    members = rows // span
    length, me = meta[seq], meta[meta.shape[0] - 1]


    def bring(number_of_block, block):
        tokens, context = tokens_all.at[number_of_block], context_all.at[number_of_block]
        cotangent, in_sems = staged[2].at[number_of_block], in_sems_all.at[number_of_block]
        tokens_copy = pltpu.make_async_copy(
            tokens_hbm.at[pl.ds(block * rows, rows), :], tokens, in_sems.at[0]
        )
        tokens_copy.start()
        lanes = pl.ds(block * members * each, members * each)
        context_copies, cotangent_copies = [], []
        for number, ((distance, half), piece) in enumerate(zip(kinds, pieces)):
            if half != 0:
                first = span if half is None else 0
                context_copies.append(
                    pltpu.make_async_copy(
                        piece.at[pl.ds(first, span), lanes],
                        context.at[distance],
                        in_sems.at[1 + 2 * number],
                    )
                )
                context_copies[-1].start()
        for number, ((distance, half), piece) in enumerate(zip(kinds, pieces)):
            if half != 1:
                owner = meta[seqs + distance]
                inside = owner // members == block
                start = pl.multiple_of(
                    jnp.where(inside, owner - block * members, 0) * span, 16
                )
                copy = pltpu.make_async_copy(
                    piece.at[pl.ds(0, span), :],
                    cotangent.at[pl.ds(start, span), :],
                    in_sems.at[2 + 2 * number],
                )
                pl.when(inside)(copy.start)
                cotangent_copies.append((inside, copy))
        return tokens_copy, context_copies, cotangent_copies

    def work(number_of_block, block, brought, staged):
        tokens_copy, context_copies, cotangent_copies = brought
        staged = [ref.at[number_of_block] for ref in staged]
        heads_out, mix_out, tokens, context = (
            ref.at[number_of_block] for ref in (heads_all, mix_all, tokens_all, context_all)
        )
        sems = sems_all.at[number_of_block]
        at_row = seq * seq_len + block * rows
        lanes = pl.ds(block * members * each, members * each)
        (
            context_out,
            normed_out,
            cotangent,
            hidden_out,
            grad_gate_out,
            grad_up_out,
            grad_out,
            logits_out,
        ) = staged
        copies = [
            pltpu.make_async_copy(source, target.at[pl.ds(at_row, rows), :], sems.at[number])
            for number, (source, target) in enumerate(zip(staged, buffers))
        ]
        heads_copy = pltpu.make_async_copy(
            heads_out, sums_out.at[:, pl.ds(0, span), lanes], sems.at[8]
        )
        mix_copies = [
            pltpu.make_async_copy(
                mix_out.at[pl.ds(part * span, span), :],
                sums_out.at[meta[seqs + count + block * members + part], pl.ds(span, span), :],
                sems.at[9 + part],
            )
            for part in range(members)
        ]

        group = seqs * span
        before = (
            lax.broadcasted_iota(jnp.int32, (group, group), 0)
            < lax.broadcasted_iota(jnp.int32, (group, group), 1)
        ).astype(bf16)
        expert_row = lax.broadcasted_iota(jnp.int32, (8, group), 0).astype(f32)
        member_lane = lax.broadcasted_iota(jnp.int32, (1, group), 1)
        codes = []
        for part in range(members):
            owner = block * members + part
            line = ids[pl.ds(meta[seqs + count + owner], 1), :]
            alive = jnp.zeros((1, group), f32)
            for other in range(seqs):
                inside = jnp.logical_and(
                    member_lane >= other * span, member_lane < (other + 1) * span
                )
                inside = jnp.logical_and(
                    inside, member_lane - other * span + owner * span < meta[other]
                )
                alive = jnp.where(inside, 1.0, alive)
            taken = jnp.logical_or(
                line[:, :group] == expert_row, line[:, group : 2 * group] == expert_row
            ).astype(f32)
            earlier = dot_nn((taken * alive).astype(bf16), before)
            code = taken * (1.0 + jnp.where(earlier < capacity, alive, 0.0))
            code = code[:, seq * span : (seq + 1) * span]
            code = jnp.concatenate([code, jnp.zeros((120, span), f32)], axis=0)
            codes.append(code.T)
        code = jnp.concatenate(codes, axis=0)

        total_units = gate_weight.shape[0]
        units = total_units // expert_count
        cuts = [slice(i, min(i + 256, total_units)) for i in range(0, total_units, 256)]
        row = block * rows + lax.broadcasted_iota(jnp.int32, (rows, 1), 0)
        own = jnp.logical_and(row >= me * span, row < (me + 1) * span)
        for copy in context_copies:
            copy.wait()
        joined = jnp.concatenate(
            [
                jnp.concatenate(
                    [context[d, :, part * each : (part + 1) * each] for d in range(count)], axis=1
                )
                for part in range(members)
            ],
            axis=0,
        )
        context_out[...] = joined
        copies[0].start()
        tokens_copy.wait()
        hidden = tokens[...].astype(f32) + dot_nn(joined, out_weight[...])
        factor = lax.rsqrt(jnp.mean(hidden * hidden, axis=-1, keepdims=True) + epsilon)
        normed = (hidden * factor * gain[...]).astype(bf16)
        normed_out[...] = normed
        copies[1].start()
        logits = dot_nn(normed, router_weight[...])
        lane = lax.broadcasted_iota(jnp.int32, logits.shape, 1)
        logits = jnp.where(lane < expert_count, logits, -1e30)
        router = jnp.exp(logits - jnp.max(logits, axis=-1, keepdims=True))
        router = router / jnp.sum(router, axis=-1, keepdims=True)
        chosen = (code > 0.5).astype(f32)
        kept = (code > 1.5).astype(f32)
        pair_total = jnp.sum(router * chosen, axis=-1, keepdims=True)
        share = router * chosen / pair_total
        scale = share * kept
        for inside, copy in cotangent_copies:
            pl.when(inside)(copy.wait)
        copies[2].start()
        upstream = jnp.where(row < length, cotangent[...].astype(f32), 0.0)
        upstream_low = upstream.astype(bf16)
        root = 0.7978845608028654
        pair_grads = jnp.zeros(logits.shape, f32)
        scale_of = [jnp.broadcast_to(scale[:, e : e + 1], (rows, 128)) for e in range(expert_count)]
        part_sums = [jnp.zeros((rows, 128), f32) for e in range(expert_count)]
        lanes = lax.broadcasted_iota(jnp.int32, (rows, 128), 1)

        def front(number):
            cut = cuts[number]
            return (
                dot_nt(normed, gate_weight[cut, :]),
                dot_nt(normed, up_weight[cut, :]),
                dot_nt(upstream_low, down_weight[cut, :]),
            )

        ready = front(0)
        for number, cut in enumerate(cuts):
            now = ready
            if number + 1 < len(cuts):
                ready = front(number + 1)
            for first in range(cut.start, cut.stop, 128):
                wide = min(128, cut.stop - first)
                inside = slice(first - cut.start, first - cut.start + wide)
                gate_in, up_in, grad_hidden = (value[:, inside] for value in now)
                square = gate_in * gate_in
                bent = gate_in * (root + (root * 0.044715) * square)
                rise = 0.5 + 0.5 * jnp.tanh(bent)
                gelu = gate_in * rise
                slope = rise + (rise - rise * rise) * (6.0 * bent - (4.0 * root) * gate_in)
                hidden_unit = gelu * up_in
                product = hidden_unit * grad_hidden
                low_expert, high_expert = first // units, (first + wide - 1) // units
                scales = scale_of[low_expert][:, :wide]
                if low_expert == high_expert:
                    if wide < 128:
                        product = jnp.pad(product, ((0, 0), (0, 128 - wide)))
                    part_sums[low_expert] = part_sums[low_expert] + product
                else:
                    under = lanes[:, :wide] < high_expert * units - first
                    scales = jnp.where(under, scales, scale_of[high_expert][:, :wide])
                    part_sums[low_expert] = part_sums[low_expert] + jnp.where(under, product, 0.0)
                    part_sums[high_expert] = part_sums[high_expert] + jnp.where(under, 0.0, product)
                scaled_grad = scales * grad_hidden
                at = slice(first, first + wide)
                hidden_out[:, at] = (scales * hidden_unit).astype(bf16)
                grad_gate_out[:, at] = (scaled_grad * up_in * slope).astype(bf16)
                grad_up_out[:, at] = (scaled_grad * gelu).astype(bf16)
        for expert in range(expert_count):
            pair_sum = jnp.sum(part_sums[expert], axis=-1, keepdims=True)
            pair_grads = jnp.where(lane == expert, pair_sum, pair_grads)
        for copy in copies[3:6]:
            copy.start()
        mix = dot_nn(hidden_out[...], down_weight[...])
        grad = dot_nn(grad_gate_out[...], gate_weight[...]) + dot_nn(grad_up_out[...], up_weight[...])
        mix_out[...] = (mix + jnp.where(own, hidden, 0.0)).astype(bf16)
        for copy in mix_copies:
            copy.start()
        pair_grads = pair_grads * kept
        weighted = jnp.sum(pair_grads * share, axis=-1, keepdims=True)
        grad_router = chosen * (pair_grads - weighted) / pair_total
        grad_logits = router * (grad_router - jnp.sum(router * grad_router, axis=-1, keepdims=True))
        grad_logits = grad_logits.astype(bf16)
        logits_out[...] = grad_logits
        copies[7].start()
        grad = grad + dot_nt(grad_logits, router_weight[...])
        spread = hidden * factor
        gain_part = jnp.sum(grad * spread, axis=0, keepdims=True)
        if number_of_block == 0:
            gain_out[...] = gain_in[...]
        gain_out[0:1, :] += gain_part
        grad = grad * gain[...]
        middle = jnp.mean(grad * hidden, axis=-1, keepdims=True) * (factor * factor)
        back = factor * grad - spread * middle + jnp.where(own, upstream, 0.0)
        back = back.astype(bf16)
        grad_out[...] = back
        copies[6].start()
        grad_heads = dot_nt(back, out_weight[...]).astype(bf16)
        for d in range(count):
            for part in range(members):
                heads_out[d, :, part * each : (part + 1) * each] = grad_heads[
                    part * span : (part + 1) * span, d * each : (d + 1) * each
                ]
        heads_copy.start()
        return [*copies, *mix_copies, heads_copy]

    brought = [bring(number, block) for number, block in enumerate(blocks)]
    started = []
    for number, block in enumerate(blocks):
        started += work(number, block, brought[number], staged)
    for copy in started:
        copy.wait()


def experts(
    meta,
    where,
    tokens,
    pieces,
    gain,
    router_weight,
    ids,
    gain_in,
    weights,
    buffers,
    sums,
    sizes,
):
    seq, blocks = where
    count, span, seqs, expert_count, capacity = sizes
    seq_len, width = tokens.shape
    units = weights[1].shape[0]
    rows = 256
    each = width // count
    members = rows // span
    many = len(blocks)
    kinds = [(d, half) for d, half, piece in pieces]
    anywhere = pl.BlockSpec(memory_space=pl.ANY)
    low = lambda *shape: jax.ShapeDtypeStruct(shape, bf16)
    columns = [width] * 3 + [units] * 3 + [width, 128]
    aliased = list(buffers or []) + ([sums] if sums is not None else [])
    first = 2 + len(pieces) + 8
    targets = ([*range(8)] if buffers else []) + ([8] if sums is not None else [])
    static = (count, span, seqs, expert_count, capacity, seq, blocks, kinds, len(aliased))
    return pl.pallas_call(
        functools.partial(experts_kernel, static),
        out_shape=[low(seqs * seq_len, cols) for cols in columns]
        + [low(count, 2 * span, width), jax.ShapeDtypeStruct((8, width), f32)],
        in_specs=[pl.BlockSpec(memory_space=pltpu.SMEM)]
        + [anywhere] * (1 + len(pieces))
        + [whole_ref] * 8
        + [anywhere] * len(aliased),
        out_specs=[anywhere] * 9 + [whole_ref],
        scratch_shapes=[pltpu.VMEM((many, rows, cols), bf16) for cols in columns]
        + [
            pltpu.VMEM((many, count, span, members * each), bf16),
            pltpu.VMEM((many, rows, width), bf16),
            pltpu.VMEM((many, rows, width), bf16),
            pltpu.VMEM((many, count, span, members * each), bf16),
            pltpu.SemaphoreType.DMA((many, 9 + members)),
            pltpu.SemaphoreType.DMA((many, 1 + 2 * len(pieces))),
        ],
        input_output_aliases={first + i: target for i, target in enumerate(targets)},
        compiler_params=pltpu.CompilerParams(vmem_limit_bytes=36 * 2**20),
        cost_estimate=pl.CostEstimate(
            flops=2 * many * rows * width * (6 * units + 2 * width),
            bytes_accessed=1000,
            transcendentals=many * rows * units,
        ),
        name="experts",
    )(
        meta,
        tokens,
        *[piece for d, half, piece in pieces],
        gain,
        router_weight,
        ids,
        gain_in,
        *weights,
        *aliased,
    )


def block_sets(blocks, seq):
    step = 1 if seq == 0 else 2
    return [list(range(i, min(i + step, blocks))) for i in range(0, blocks, step)]


def attend_back_kernel(seq, head, heads, meta, queries_in, keys_in, values_in, *refs):
    own, right, left, bias, parts_out, sums_out = refs[:6]
    table, key_sum, value_sum, summed = refs[6:]
    length = meta[seq]
    _, seq_len, head_size = keys_in.shape
    span = right.shape[0]
    each = heads * head_size
    blocks = seq_len // 128
    summed[...] = (own[0].astype(f32) + right[...].astype(f32) + left[...].astype(f32)).astype(bf16)
    table[...] = jnp.zeros_like(table)
    keys = keys_in[0]
    values = values_in[0]
    for block in range(0, blocks, 2):
        rows = slice(block * 128, block * 128 + 256)
        queries = queries_in[0, rows, :]
        firsts = [
            part * each + head * head_size
            for part in range(block * 128 // span, (block * 128 + 256) // span)
        ]
        grads = jnp.concatenate(
            [summed[:, lane : lane + head_size] for lane in firsts], axis=0
        )
        first_row = (blocks - 1 - block) * 128
        added = jnp.concatenate(
            [
                bias[0, first_row : first_row + seq_len, :],
                bias[0, first_row - 128 : first_row - 128 + seq_len, :],
            ],
            axis=1,
        )
        scores = dot_nt(keys, queries)
        row = lax.broadcasted_iota(jnp.int32, scores.shape, 0)
        scores = jnp.where(row < length, scores + added, -1e30)
        top = jnp.max(scores, axis=0, keepdims=True)
        probs = jnp.exp(scores - top)
        probs = probs * (1.0 / jnp.sum(probs, axis=0, keepdims=True))
        product = probs * dot_nt(values, grads)
        delta = jnp.sum(product, axis=0, keepdims=True)
        grad_scores = product - probs * delta
        table[first_row : first_row + seq_len, :] += grad_scores[:, :128]
        table[first_row - 128 : first_row - 128 + seq_len, :] += grad_scores[:, 128:]
        scores_low = grad_scores.astype(bf16)
        key_part = dot_nn(scores_low, queries)
        value_part = dot_nn(probs.astype(bf16), grads)
        if block == 0:
            key_sum[...] = key_part
            value_sum[...] = value_part
        else:
            key_sum[...] += key_part
            value_sum[...] += value_part
        query_grad = dot_tn(keys, scores_low) * head_size ** (-0.5)
        parts_out[0, rows, :] = query_grad.T.astype(bf16)
    parts_out[1] = key_sum[...].astype(bf16)
    parts_out[2] = value_sum[...].astype(bf16)
    width = table.shape[0] + 128
    lines = jnp.concatenate(
        [table[first : first + 128, :].T for first in range(0, width - 128, 128)]
        + [jnp.zeros((128, 128), f32)],
        axis=1,
    )
    rows = 128
    while rows > 1:
        rows //= 2
        lines = lines[:rows] + pltpu.roll(lines[rows : 2 * rows], width - rows, 1)
    sums_out[...] = jnp.broadcast_to(pltpu.roll(lines, 127, 1), sums_out.shape)


def attend_back(meta, seq, head, heads, qkv, own, right, left, span, bias):
    _, seq_len, head_size = qkv.shape
    width = right.shape[1]
    part = lambda at: pl.BlockSpec((1, seq_len, head_size), lambda i, meta: (at, 0, 0))
    full = lambda *shape: pl.BlockSpec(shape, lambda i, meta: (0,) * len(shape))
    low = jax.ShapeDtypeStruct((3, seq_len, head_size), bf16)
    return pl.pallas_call(
        functools.partial(attend_back_kernel, seq, head, heads),
        out_shape=(low, jax.ShapeDtypeStruct((8, 2 * seq_len), f32)),
        grid_spec=pltpu.PrefetchScalarGridSpec(
            num_scalar_prefetch=1,
            grid=(1,),
            in_specs=[part(head), part(heads + head), part(2 * heads + head)]
            + [full(1, span, width), full(span, width), full(span, width)]
            + [pl.BlockSpec((1,) + bias.shape[1:], lambda i, meta: (head, 0, 0))],
            out_specs=[full(3, seq_len, head_size), full(8, 2 * seq_len)],
            scratch_shapes=[
                pltpu.VMEM(bias.shape[1:], f32),
                pltpu.VMEM((seq_len, head_size), f32),
                pltpu.VMEM((seq_len, head_size), f32),
                pltpu.VMEM((span, width), bf16),
            ],
        ),
        compiler_params=pltpu.CompilerParams(vmem_limit_bytes=28 * 2**20),
        cost_estimate=pl.CostEstimate(
            flops=6 * 10**9, bytes_accessed=1000, transcendentals=seq_len * seq_len
        ),
        name="attend_back",
    )(meta, qkv, qkv, qkv, own, right, left, bias)


def norm_back_kernel(heads, first, meta, *refs):
    parts, (tokens, weight, grad_in, grad_out, parts_out, gain_out) = refs[:heads], refs[heads:]

    @pl.when(pl.program_id(0) == 0)
    def _():
        gain_out[...] = jnp.zeros_like(gain_out)

    low = jnp.concatenate([part[kind] for kind in range(3) for part in parts], axis=1)
    wide = tokens[...].astype(f32)
    factor = lax.rsqrt(jnp.mean(wide * wide, axis=-1, keepdims=True) + epsilon)
    upstream = dot_nt(low, weight[...])
    spread = wide * factor
    gain_out[0:1, :] += jnp.sum(upstream * spread, axis=0, keepdims=True)
    middle = jnp.mean(upstream * wide, axis=-1, keepdims=True) * (factor * factor)
    back = factor * upstream - spread * middle + grad_in[...].astype(f32)
    back = back.astype(bf16)
    span = grad_out.shape[1]
    members = back.shape[0] // span
    for part in range(members):
        distance = meta[first + pl.program_id(0) * members + part]
        grad_out[distance] = back[part * span : (part + 1) * span, :]
    parts_out[...] = (low.astype(f32) * factor).astype(bf16)


def norm_back(meta, seq, seqs, parts, tokens, weight, grad_in, count):
    seq_len, width = tokens.shape
    head_size = parts[0].shape[2]
    rows, span = 256, seq_len // count
    by_row = lambda cols, at=0: pl.BlockSpec((rows, cols), lambda i, meta: (at + i, 0))
    columns = 3 * head_size * len(parts)
    return pl.pallas_call(
        functools.partial(norm_back_kernel, len(parts), seqs + count),
        out_shape=(
            jax.ShapeDtypeStruct((count, span, width), bf16),
            jax.ShapeDtypeStruct((seq_len, columns), bf16),
            jax.ShapeDtypeStruct((8, width), f32),
        ),
        grid_spec=pltpu.PrefetchScalarGridSpec(
            num_scalar_prefetch=1,
            grid=(seq_len // rows,),
            in_specs=[pl.BlockSpec((3, rows, head_size), lambda i, meta: (0, i, 0))] * len(parts)
            + [
                by_row(width),
                pl.BlockSpec(weight.shape, lambda i, meta: (0, 0)),
                by_row(width, seq * (seq_len // rows)),
            ],
            out_specs=(
                pl.BlockSpec((count, span, width), lambda i, meta: (0, 0, 0)),
                by_row(columns),
                pl.BlockSpec((8, width), lambda i, meta: (0, 0)),
            ),
        ),
        compiler_params=pltpu.CompilerParams(vmem_limit_bytes=24 * 2**20),
        cost_estimate=pl.CostEstimate(
            flops=2 * seq_len * width * columns, bytes_accessed=1000, transcendentals=0
        ),
        name="norm_back",
    )(meta, *parts, tokens, weight, grad_in)


def spread_kernel(reps, spots, *refs):
    parts, gain, outs = refs[:reps], refs[reps], refs[reps + 1 :]
    count, _, columns = parts[0].shape
    cut = gain.shape[0] // reps
    each = columns // 3
    for number, part in enumerate(parts):
        rows = pl.ds(pl.multiple_of(spots[number] * cut, cut), cut)
        scale = gain[rows, :]
        for owner in range(count):
            block = part[owner, :cut, :].astype(f32) * scale
            for kind, out in enumerate(outs):
                out[rows, owner * each : (owner + 1) * each] = block[:, kind * each : (kind + 1) * each]


def spread(parts, spots, found, gain):
    count, _, columns = parts[0].shape
    cut, each = gain.shape[0] // len(parts), columns // 3
    if cut % 8:
        whole = jnp.take(jnp.stack(parts), found, axis=0)[:, :, :cut].astype(f32)
        whole = whole.reshape(len(parts), count, cut, 3, each).transpose(3, 0, 2, 1, 4)
        whole = whole.reshape(3, gain.shape[0], count * each) * gain[None, :, None]
        return whole[0], whole[1], whole[2]
    shape = jax.ShapeDtypeStruct((gain.shape[0], count * each), f32)
    return pl.pallas_call(
        functools.partial(spread_kernel, len(parts)),
        out_shape=(shape,) * 3,
        in_specs=[pl.BlockSpec(memory_space=pltpu.SMEM)] + [whole_ref] * (len(parts) + 1),
        out_specs=[whole_ref] * 3,
        compiler_params=pltpu.CompilerParams(vmem_limit_bytes=12 * 2**20),
        name="spread",
    )(spots, *parts, gain.reshape(-1, 1))


def body(
    tokens,
    lengths,
    expert_ids,
    buckets,
    norm1_gain,
    w_query,
    w_key,
    w_value,
    w_out,
    rel_bias,
    norm2_gain,
    w_router,
    w_gate,
    w_up,
    w_down,
    cotangent,
):
    seqs, span, width = tokens.shape
    count = lax.axis_size("shard")
    reps = lax.axis_size("rep")
    me = lax.axis_index("shard")
    rep = lax.axis_index("rep")
    seq_len = span * count
    expert_count, unit_count, _ = w_gate.shape
    heads = rel_bias.shape[1]
    head_size = w_query.shape[1] // (count * heads)
    each = heads * head_size
    feats = w_query.shape[0]
    cut = feats // reps
    row_count = seqs * span
    capacity = 10 * row_count // (4 * expert_count)
    place = ring_place(me, count)
    distances = jnp.arange(count, dtype=jnp.int32)
    owners = ring_index((place + distances) % count, count)
    distance_of = (ring_place(distances, count) - place) % count
    meta = jnp.concatenate([lengths, owners, distance_of, me[None]]).astype(jnp.int32)

    def line(values):
        flat = values.reshape(-1).astype(bf16)
        return jnp.pad(flat, (0, width - flat.shape[0]))[None]

    packed = jnp.concatenate(
        [
            tokens.reshape(row_count, width),
            lax.dynamic_slice_in_dim(w_out, rep * cut, cut, 0),
            line(expert_ids.reshape(row_count, 2).T),
            line(jnp.concatenate([norm2_gain, w_router.reshape(-1)])),
            jnp.zeros((14, width), bf16),
        ],
        axis=0,
    )
    extra = row_count
    token_ring = Gather(
        packed,
        count,
        lambda value: (
            jnp.concatenate([value[:span], value[extra:]], axis=0),
            value[span:extra],
        ),
    )
    hops = []
    while not token_ring.done:
        fire([token_ring])
        hops.append(token_ring.last())

    gain_one = norm1_gain.astype(f32)
    own_qkv = jnp.stack([w_query, w_key, w_value], axis=1)
    own_cut = lax.dynamic_slice_in_dim(own_qkv, rep * cut, cut, 0).astype(f32)
    own_cut = own_cut * lax.dynamic_slice_in_dim(gain_one, rep * cut, cut, 0)[:, None, None]
    own_cut = own_cut.astype(bf16).reshape(cut, 3, count, each).transpose(2, 0, 1, 3)
    qkv_weight = lax.all_to_all(
        own_cut.reshape(count, cut, 3 * each), "shard", split_axis=0, concat_axis=0, tiled=True
    )
    qkv_weight = weave(*rep_parts(after(qkv_weight, hops[1]), reps, rep))

    bucket_count = rel_bias.shape[0]
    bucket_hot = (
        buckets[:, None] == jnp.arange(bucket_count, dtype=jnp.int32)[None, :]
    ).astype(f32)
    bucket_hot = jnp.pad(bucket_hot, ((0, 1), (0, 0)))
    bias_vec = jnp.einsum("rb,bh->hr", bucket_hot, rel_bias.astype(f32), precision=highest)
    bias, bias_turned = bias_tables(bias_vec)

    def sent(rings):
        return tuple(ring.last() for ring in rings if ring.last()[0] is not None)

    attended, mixed_rings, rings = [], [], []
    waits = token_ring.last()
    for s in range(seqs):
        fire(rings, waits)
        attended.append(
            attend(
                after(meta, waits),
                s,
                seqs,
                token_ring.pieces,
                cotangent[s],
                qkv_weight,
                bias,
                heads,
                head_size,
            )
        )
        waits = (attended[s][2], sent(rings))
        if s == 0:
            riders = attended[s][3]
            out_parts = rep_parts(riders[:, :cut], reps, rep)
        mixed_rings.append(Gather(attended[s][2], count))
        rings = [mixed_rings[0]]
    while not rings[0].done:
        fire(rings, waits)
        waits = lasts(rings)

    out_weight = weave(*out_parts)
    ids = riders[:, cut].astype(f32)
    small = jnp.take(riders[:, cut + 1], distance_of, axis=0)
    gain_two = small[:, :feats].astype(f32).reshape(1, width)
    router_weight = small[:, feats : feats * (1 + expert_count)].reshape(width, expert_count)
    router_weight = jnp.pad(router_weight, ((0, 0), (0, 128 - expert_count)))
    expert_weights = [out_weight] + [
        weight.reshape(expert_count * unit_count, width) for weight in (w_gate, w_up, w_down)
    ]

    sizes = (count, span, seqs, expert_count, capacity)
    buffers = None
    gain_part = jnp.zeros((8, width), f32)
    sums_all, sum_rings = [], []
    rings = [mixed_rings[1]]
    for s in range(seqs):
        if s > 0:
            while not rings[0].done:
                fire(rings, waits)
                waits = lasts(rings)
            sum_rings.append(Sum([(sums_all[s - 1], 0, 2 * span)], count))
            rings = [sum_rings[s - 1]]
        sums = None
        for blocks in block_sets(seq_len // 256, s):
            if not rings[0].done:
                fire(rings, waits)
            *buffers, sums, gain_part = experts(
                after(meta, waits),
                (s, blocks),
                attended[s][0],
                mixed_rings[s].pieces,
                gain_two,
                router_weight,
                ids,
                gain_part,
                expert_weights,
                buffers,
                sums,
                sizes,
            )
            waits = (gain_part, sent(rings))
        sums_all.append(sums)
    context_rows, normed, cot_rows, hidden, grad_gate, grad_up, grad_rows, grad_logits = buffers

    offset_sums, totals, finished, scaled_all, gain_one_part = [], [], [], [], []

    def total_grad(left_side, right_side, waits):
        grads = dot_tn(after(left_side, waits), right_side).astype(bf16)
        totals.append(RepTotal(grads, reps, rep))
        return grads

    def step(rings, waits):
        live = [ring for ring in rings if not ring.done]
        if live:
            fire(live, waits)

    def back_head(s, head, waits):
        made = attend_back(
            after(meta, waits),
            s,
            head,
            heads,
            attended[s][1],
            sums_all[s],
            *sum_rings[s].last(),
            span,
            bias_turned,
        )
        offset_sums.append((head, made[1]))
        return made[0]

    def back_norm(s, parts, waits):
        grads, scaled, gain_rows = norm_back(
            after(meta, waits), s, seqs, parts, attended[s][0], qkv_weight, grad_rows, count
        )
        scaled_all.append(scaled)
        gain_one_part.append(gain_rows)
        return grads

    sum_rings.append(Sum([(sums_all[1], 0, 2 * span)], count))
    first, second = sum_rings
    rings = [first]
    step(rings, waits)
    done = total_grad(hidden, cot_rows, waits)
    rings = [first, second]
    waits = (done, sent(rings))
    step(rings, waits)
    out_grad = dot_tn(after(context_rows, waits), grad_rows).astype(bf16)
    router_grad = dot_tn(normed, grad_logits)[:, :expert_count]
    flat = jnp.concatenate(
        [gain_part[0].reshape(count, feats), router_grad.reshape(count, feats * expert_count)], axis=1
    ).astype(bf16)
    flat = jnp.take(flat, owners, axis=0)
    small_size = flat.shape[1] // 2
    flat = jnp.pad(flat.reshape(count, 2, 1, small_size), ((0, 0), (0, 0), (0, 15), (0, width - small_size)))
    out_whole = jnp.concatenate([out_grad.reshape(count, 2, each // 2, width), flat], axis=2)
    side = rep % 2
    out_kept = lax.dynamic_index_in_dim(out_whole, side, 1, keepdims=False)
    out_got = swap(lax.dynamic_index_in_dim(out_whole, 1 - side, 1, keepdims=False), "rep", reps, 1)
    done = total_grad(grad_gate, normed, (waits, out_grad))
    waits = (done, sent(rings))
    while not first.done:
        step(rings, waits)
        waits = lasts(rings)
    rings = [second]
    parts = []
    for head in range(heads):
        step(rings, waits)
        parts.append(back_head(0, head, waits))
        waits = (parts[-1], sent(rings))
        if head == 0:
            totals[0].cross()
            out_grad = add_low(out_kept, out_got)
            waits = waits + (totals[0].kept, out_grad)
    totals[1].cross()
    waits = waits + (totals[1].kept,)
    grads_first = back_norm(0, parts, waits)
    waits = (grads_first, waits)
    final = [Sum([(grads_first, 0, span), (out_grad, 0, out_grad.shape[1])], count)]
    rings = [second, final[0]]
    step(rings, waits)
    done = total_grad(grad_up, normed, (waits, totals[0].got))
    wide = totals[0].finish()
    waits = (done, wide, sent(rings))
    while not second.done:
        step(rings, waits)
        waits = lasts(rings)
    rings = [final[0]]
    parts = []
    for head in range(heads):
        step(rings, waits)
        parts.append(back_head(1, head, waits))
        waits = (parts[-1], sent(rings))
        if head == 0:
            totals[2].cross()
            waits = waits + (totals[2].kept,)
    step(rings, waits)
    grads_last = back_norm(1, parts, (waits, totals[1].got))
    final.append(Sum([(grads_last, 0, span)], count))
    waits = (grads_last, sent(rings))
    rings = final
    while not all(ring.done for ring in rings):
        step(rings, waits)
        waits = lasts(rings)

    mix_first, mix_last, final_first, final_last = (
        total_of(ring) for ring in (*sum_rings, *final)
    )
    grad_tokens = jnp.stack([final_first[:span], final_last])
    positions = me * span + jnp.arange(span, dtype=jnp.int32)
    live_mask = (positions[None, :] < lengths[:, None]).astype(f32)[:, :, None]
    block_out = (live_mask * jnp.stack([mix_first[span:], mix_last[span:]])).astype(bf16)
    out_own = final_first[span:].astype(bf16)
    for bit in bits_of(reps)[1:]:
        out_own = add_low(out_own, swap(out_own, "rep", reps, bit))
    out_other = swap(out_own, "rep", reps, 1)
    out_both = jnp.where(
        side == 0, jnp.stack([out_own, out_other]), jnp.stack([out_other, out_own])
    ).astype(f32)
    total_out = out_both[:, : each // 2].reshape(feats, width)
    flat = out_both[:, each // 2, :small_size].reshape(-1)
    total_gain_two = flat[:feats]
    total_router = flat[feats:].reshape(feats, expert_count)

    qkv_grad = sum(dot_tn(attended[s][0], scaled_all[s]) for s in range(seqs)).astype(bf16)
    offsets = jnp.stack(
        [sum(part[0] for h, part in offset_sums if h == head) for head in range(heads)]
    )
    bias_grad = jnp.einsum("hr,rb->hb", offsets, bucket_hot, precision=highest)
    gain_rows = sum(part[0] for part in gain_one_part).reshape(count, reps, 1, cut)
    bias_rows = jnp.broadcast_to(
        bias_grad.reshape(1, reps, 1, -1), (count, reps, 1, bias_grad.size // reps)
    )
    flat = jnp.concatenate([gain_rows, bias_rows], axis=3).astype(bf16)
    flat = jnp.pad(flat, ((0, 0), (0, 0), (0, 15), (0, 3 * each - flat.shape[3])))
    qkv_grad = jnp.concatenate([qkv_grad.reshape(count, reps, cut, 3 * each), flat], axis=2)
    qkv_grad = rep_scatter(qkv_grad.transpose(1, 0, 2, 3), reps, rep, totals[2].got)
    qkv_grad = lax.all_to_all(qkv_grad, "shard", split_axis=0, concat_axis=0, tiled=True)
    bias_size = bias_grad.size // reps
    parts, spots = rep_parts(qkv_grad, reps, rep)
    found = jnp.take(jnp.array(rep_order(reps), jnp.int32), rep ^ jnp.arange(reps))
    qkv_grad = spread(parts, spots, found, gain_one)
    tail = jnp.take(jnp.stack([part[:, cut] for part in parts]), found, axis=0).astype(f32)
    total_gain_one = jnp.sum(tail[:, :, :cut], axis=1).reshape(feats) / gain_one
    total_bias = lax.dynamic_index_in_dim(tail, me, 1, keepdims=False)[:, cut : cut + bias_size]
    total_bias = total_bias.reshape(heads, bucket_count).T

    total_down, total_gate, total_up = (
        total.reshape(expert_count, unit_count, width)
        for total in (wide, totals[1].finish(), totals[2].finish())
    )
    return (
        block_out,
        grad_tokens,
        total_gain_one,
        qkv_grad[0],
        qkv_grad[1],
        qkv_grad[2],
        total_out,
        total_bias,
        total_gain_two,
        total_router,
        total_gate,
        total_up,
        total_down,
    )


def solution(mesh):
    rows = P("rep", "shard", None)
    first = P("shard")
    weight = P("shard", None)
    expert = P(None, "shard", None)
    return jax.shard_map(
        body,
        mesh=mesh,
        in_specs=(rows, P("rep"), rows, P(), first, weight, weight, weight, weight)
        + (P(None, "shard"), first, weight, expert, expert, expert, rows),
        out_specs=(rows, rows, first, weight, weight, weight, weight)
        + (P(None, "shard"), first, weight, expert, expert, expert),
        check_vma=False,
    )
```

```python
import functools

import jax
import jax.numpy as jnp
from jax import lax
from jax.experimental import pallas as pl
from jax.experimental.pallas import tpu as pltpu
from jax.sharding import PartitionSpec as P

epsilon = 1e-06
highest = lax.Precision.HIGHEST
bf16 = jnp.bfloat16
f32 = jnp.float32
vmem_limit = 58 * 1024 * 1024
whole_ref = pl.BlockSpec(memory_space=pltpu.VMEM)


def dot_nt(left, right):
    return lax.dot_general(left, right, (((1,), (1,)), ((), ())), preferred_element_type=f32)


def dot_tn(left, right):
    return lax.dot_general(left, right, (((0,), (0,)), ((), ())), preferred_element_type=f32)


def dot_nn(left, right):
    return lax.dot_general(left, right, (((1,), (0,)), ((), ())), preferred_element_type=f32)


def ring_index(place, count):
    return jnp.where(place < count // 2, 2 * place, 2 * count - 1 - 2 * place)


def ring_place(index, count):
    return jnp.where(index % 2 == 0, index // 2, count - 1 - index // 2)


def ring_send(value, step, count):
    order = [2 * i if i < count // 2 else 2 * count - 1 - 2 * i for i in range(count)]
    pairs = [(order[i], order[(i + step) % count]) for i in range(count)]
    return lax.ppermute(value, "shard", pairs)


def after(value, *waits):
    if not jax.tree.leaves(waits):
        return value
    flat, tree = jax.tree.flatten(value)
    held = lax.optimization_barrier(tuple(flat) + tuple(jax.tree.leaves(waits)))
    return tree.unflatten(held[: len(flat)])


def halve(value):
    half = value.shape[0] // 2
    return value[:half], value[half:]


class Gather:
    def __init__(self, value, count, split=None):
        self.count, self.step, self.split = count, 1, split or halve
        self.ahead = self.behind = value
        self.pieces = [(0, None, value)]
        self.done = False

    def hop(self, *waits):
        behind, ahead = after((self.behind, self.ahead), *waits)
        far = self.count // 2
        if self.step < far:
            self.behind = ring_send(behind, 1, self.count)
            self.ahead = ring_send(ahead, -1, self.count)
            self.pieces += [(self.count - self.step, None, self.behind), (self.step, None, self.ahead)]
            self.step += 1
        else:
            self.behind = ring_send(self.split(behind)[0], 1, self.count)
            self.ahead = ring_send(self.split(ahead)[1], -1, self.count)
            self.pieces += [(far, 0, self.behind), (far, 1, self.ahead)]
            self.done = True

    def last(self):
        return (self.behind, self.ahead)


def add_low(left, right):
    return (left.astype(f32) + right.astype(f32)).astype(bf16)


def ring_add_kernel(half, firsts, right, left, *refs):
    count = len(firsts)
    owns = (refs[:count], refs[count : 2 * count])
    outs = refs[2 * count :]
    total = outs[0].shape[0]
    for come, own, out, begin in zip((right, left), owns, outs, (0, total - half)):
        for source, first in zip(own, firsts):
            last = first + source.shape[1]
            low, high = max(first, begin), min(last, begin + half)
            if low < high:
                summed = source[0, low - first : high - first, :].astype(f32)
                summed = summed + come[low - begin : high - begin, :].astype(f32)
                out[low:high, :] = summed.astype(bf16)
            if first < min(low, last):
                out[first : min(low, last), :] = source[0, : min(low, last) - first, :]
            if max(high, first) < last:
                out[max(high, first) : last, :] = source[0, max(high, first) - first :, :]


def ring_add(right, left, own_right, own_left, rows):
    width = right.shape[1]
    total = sum(rows)
    firsts = [sum(rows[:i]) for i in range(len(rows))]
    full = lambda *shape: pl.BlockSpec(shape, lambda i: (0,) * len(shape))
    part = lambda spot, count: pl.BlockSpec((1, count, width), lambda i: (spot[1], spot[2], 0))
    shape = jax.ShapeDtypeStruct((total, width), bf16)
    return pl.pallas_call(
        functools.partial(ring_add_kernel, right.shape[0], firsts),
        out_shape=(shape, shape),
        grid=(1,),
        in_specs=[full(*right.shape)] * 2
        + [part(spot, count) for spot, count in zip(own_right, rows)]
        + [part(spot, count) for spot, count in zip(own_left, rows)],
        out_specs=(full(total, width),) * 2,
        compiler_params=pltpu.CompilerParams(vmem_limit_bytes=14 * 2**20),
        cost_estimate=pl.CostEstimate(
            flops=2 * total * width, bytes_accessed=1000, transcendentals=0
        ),
        name="ring_add",
    )(right, left, *[spot[0] for spot in own_right], *[spot[0] for spot in own_left])


class Sum:
    def __init__(self, sources, count):
        self.sources, self.count, self.step = sources, count, count // 2
        self.rows = [rows for array, block, rows in sources]
        self.right = self.left = None
        self.done = False

    def chunk(self, distance):
        return jnp.concatenate(
            [array[distance, block * rows : (block + 1) * rows] for array, block, rows in self.sources],
            axis=0,
        )

    def hop(self, *waits):
        if self.right is None:
            right, left = halve(self.chunk(self.step))
        else:
            spots = [
                [(array, distance, block) for array, block, rows in self.sources]
                for distance in (self.step, self.count - self.step)
            ]
            right, left = ring_add(self.right, self.left, *spots, self.rows)
        right, left = after((right, left), *waits)
        self.right = ring_send(right, 1, self.count)
        self.left = ring_send(left, -1, self.count)
        self.step -= 1
        self.done = self.step == 0

    def last(self):
        return (self.right, self.left)


def total_of(ring):
    total = ring.chunk(0).astype(f32)
    return total + ring.right.astype(f32) + ring.left.astype(f32)


def fire(rings, *waits):
    rings = [ring for ring in rings if not ring.done]
    waits = waits + tuple(ring.last() for ring in rings if ring.last()[0] is not None)
    for ring in rings:
        ring.hop(*waits)


def lasts(rings):
    return tuple(ring.last() for ring in rings)


def swap(value, axis, count, bit):
    return lax.ppermute(value, axis, [(i, i ^ bit) for i in range(count)])


def bits_of(count):
    return [1 << i for i in range(count.bit_length() - 1)]


def rep_scatter(value, count, me, *waits):
    for bit in bits_of(count):
        value = value.reshape((value.shape[0] // 2, 2) + value.shape[1:])
        side = (me // bit) % 2
        sent = lax.dynamic_index_in_dim(value, 1 - side, 1, keepdims=False)
        kept = lax.dynamic_index_in_dim(value, side, 1, keepdims=False)
        if bit > 1:
            sent = after(sent, *waits)
        value = add_low(kept, swap(sent, "rep", count, bit))
    return value[0]


def rep_parts(value, count, me):
    parts, tags = [value], [0]
    for bit in bits_of(count)[::-1]:
        parts = parts + [swap(part, "rep", count, bit) for part in parts]
        tags = tags + [tag ^ bit for tag in tags]
    return parts, (me ^ jnp.array(tags, jnp.int32))


def rep_order(count):
    tags = [0]
    for bit in bits_of(count)[::-1]:
        tags = tags + [tag ^ bit for tag in tags]
    return [tags.index(tag) for tag in range(count)]


def weave_kernel(count, spots, *refs):
    parts, out, sems = refs[:count], refs[count], refs[count + 1]
    copies = [
        pltpu.make_async_copy(part, out.at[:, spots[i]], sems.at[i])
        for i, part in enumerate(parts)
    ]
    for copy in copies:
        copy.start()
    for copy in copies:
        copy.wait()


def weave(parts, spots):
    first, rows, columns = parts[0].shape
    anywhere = pl.BlockSpec(memory_space=pl.ANY)
    out = pl.pallas_call(
        functools.partial(weave_kernel, len(parts)),
        out_shape=jax.ShapeDtypeStruct((first, len(parts), rows, columns), parts[0].dtype),
        in_specs=[pl.BlockSpec(memory_space=pltpu.SMEM)] + [anywhere] * len(parts),
        out_specs=anywhere,
        scratch_shapes=[pltpu.SemaphoreType.DMA((len(parts),))],
        compiler_params=pltpu.CompilerParams(vmem_limit_bytes=2**20),
        name="weave",
    )(spots, *parts)
    return out.reshape(first * len(parts) * rows, columns)


def widen_kernel(parts, meta, kept, got, kept_other, got_other, out, *scratch):
    held, wide, in_sems, out_sems = scratch
    half = kept.shape[0]
    rows = half // parts
    sources = (kept, got, kept_other, got_other)
    ins = [
        [
            pltpu.make_async_copy(
                source.at[pl.ds(part * rows, rows), :],
                held.at[number, pl.ds(part * rows, rows), :],
                in_sems.at[number * parts + part],
            )
            for number, source in enumerate(sources)
        ]
        for part in range(parts)
    ]
    for part in range(parts):
        for copy in ins[part]:
            copy.start()
    outs = []
    for part in range(parts):
        for copy in ins[part]:
            copy.wait()
        at = slice(part * rows, (part + 1) * rows)
        for pair in range(2):
            total = held[2 * pair, at, :].astype(f32) + held[2 * pair + 1, at, :].astype(f32)
            wide[pair, at, :] = total
            side = meta[0] if pair == 0 else 1 - meta[0]
            start = pl.multiple_of(side * half + part * rows, 8)
            outs.append(
                pltpu.make_async_copy(
                    wide.at[pair, pl.ds(part * rows, rows), :],
                    out.at[pl.ds(start, rows), :],
                    out_sems.at[pair * parts + part],
                )
            )
            outs[-1].start()
    for copy in outs:
        copy.wait()


def widen(side, kept, got, kept_other, got_other):
    half, width = kept.shape
    parts = 4 if half % 64 == 0 else 2 if half % 32 == 0 else 1
    anywhere = pl.BlockSpec(memory_space=pl.ANY)
    return pl.pallas_call(
        functools.partial(widen_kernel, parts),
        out_shape=jax.ShapeDtypeStruct((2 * half, width), f32),
        in_specs=[pl.BlockSpec(memory_space=pltpu.SMEM)] + [anywhere] * 4,
        out_specs=anywhere,
        scratch_shapes=[
            pltpu.VMEM((4, half, width), bf16),
            pltpu.VMEM((2, half, width), f32),
            pltpu.SemaphoreType.DMA((4 * parts,)),
            pltpu.SemaphoreType.DMA((2 * parts,)),
        ],
        compiler_params=pltpu.CompilerParams(vmem_limit_bytes=16 * 2**20),
        name="widen",
    )(side, kept, got, kept_other, got_other)


class RepTotal:
    def __init__(self, value, count, me):
        self.count, self.side = count, me % 2
        value = value.reshape((2, value.shape[0] // 2) + value.shape[1:])
        sent = lax.dynamic_index_in_dim(value, 1 - self.side, 0, keepdims=False)
        self.kept = lax.dynamic_index_in_dim(value, self.side, 0, keepdims=False)
        self.got = swap(sent, "rep", count, 1)

    def cross(self, *waits):
        kept = add_low(self.kept, self.got)
        for bit in bits_of(self.count)[1:-1]:
            kept = add_low(kept, swap(kept, "rep", self.count, bit))
        self.kept = after(kept, *waits)
        self.got = swap(self.kept, "rep", self.count, self.count // 2)
        self.kept_other = swap(self.kept, "rep", self.count, 1)

    def finish(self):
        got_other = swap(self.got, "rep", self.count, 1)
        side = self.side.reshape(1).astype(jnp.int32)
        return widen(side, self.kept, self.got, self.kept_other, got_other)


def bias_kernel(vec, table, turned):
    heads, _, width = table.shape
    for head in range(heads):
        line = jnp.broadcast_to(vec[head : head + 1, :], (128, vec.shape[1]))
        line = pltpu.roll(line, vec.shape[1] - 127, 1, stride=1, stride_axis=0)
        table[head] = line[:, :width]
        for first in range(0, width, 128):
            turned[head, first : first + 128, :] = line[:, first : first + 128].T


def bias_tables(vec):
    heads, length = vec.shape
    width = length - 128
    return pl.pallas_call(
        bias_kernel,
        out_shape=(
            jax.ShapeDtypeStruct((heads, 128, width), f32),
            jax.ShapeDtypeStruct((heads, width, 128), f32),
        ),
        in_specs=[whole_ref],
        out_specs=[whole_ref] * 2,
        compiler_params=pltpu.CompilerParams(vmem_limit_bytes=24 * 2**20),
        name="bias_tables",
    )(vec)


def attend_kernel(seq, seqs, places, heads, head_size, riders, meta, *refs):
    pieces = refs[: len(places)]
    cotangent, weight, bias, tokens_out, qkv_out, mixed_out, *more = refs[len(places) :]
    sems = more[-1]
    length = meta[seq]
    span = cotangent.shape[0]
    seq_len = tokens_out.shape[0]
    each = heads * head_size
    blocks = seq_len // 128
    copies = []
    for number, ((distance, first), piece) in enumerate(zip(places, pieces)):
        start = pl.multiple_of(meta[seqs + distance] * span, 16)
        copies.append(
            pltpu.make_async_copy(
                piece.at[pl.ds(first, span), :],
                tokens_out.at[pl.ds(start, span), :],
                sems.at[number],
            )
        )
        copies[-1].start()
    for number, (distance, first) in enumerate(riders):
        copies.append(
            pltpu.make_async_copy(
                pieces[number].at[pl.ds(first, more[0].shape[1]), :],
                more[0].at[distance],
                sems.at[len(places) + number],
            )
        )
        copies[-1].start()
    mixed_out[0:span, :] = cotangent[...]
    for copy in copies:
        copy.wait()
    for first in range(0, seq_len, 256):
        rows = slice(first, first + 256)
        low = tokens_out[rows, :]
        wide = low.astype(f32)
        factor = lax.rsqrt(jnp.mean(wide * wide, axis=-1, keepdims=True) + epsilon)
        made = dot_nn(low, weight[...]) * factor
        for part in range(3 * heads):
            cut = made[:, part * head_size : (part + 1) * head_size]
            if part < heads:
                cut = cut.astype(bf16).astype(f32) * head_size ** (-0.5)
            qkv_out[part, rows, :] = cut.astype(bf16)
    for head in range(heads):
        keys = qkv_out[heads + head]
        values = qkv_out[2 * heads + head]
        for block in range(0, blocks, 2):
            queries = qkv_out[head, block * 128 : block * 128 + 256, :]
            scores = dot_nt(queries, keys)
            first_col = (blocks - 1 - block) * 128
            added = jnp.concatenate(
                [
                    bias[head, :, first_col : first_col + seq_len],
                    bias[head, :, first_col - 128 : first_col - 128 + seq_len],
                ],
                axis=0,
            )
            column = lax.broadcasted_iota(jnp.int32, scores.shape, 1)
            scores = jnp.where(column < length, scores + added, -1e30)
            top = jnp.max(scores, axis=-1, keepdims=True)
            weights = jnp.exp(scores - top)
            total = jnp.sum(weights, axis=-1, keepdims=True)
            mixed = dot_nn(weights.astype(bf16), values) / total
            mixed = mixed.astype(bf16)
            for part in range(256 // span):
                lane = (block * 128 // span + part) * each + head * head_size
                mixed_out[span : 2 * span, lane : lane + head_size] = mixed[
                    part * span : (part + 1) * span, :
                ]


def attend(meta, seq, seqs, pieces, cotangent, weight, bias, heads, head_size):
    width = weight.shape[0]
    span = cotangent.shape[0]
    pieces = [(d, half, piece) for d, half, piece in pieces if half is None or half == seq]
    places = [(d, seq * span if half is None else 0) for d, half, piece in pieces]
    seq_len = span * len(pieces)
    full = lambda *shape: pl.BlockSpec(shape, lambda i, meta: (0,) * len(shape))
    shapes = [(seq_len, width), (3 * heads, seq_len, head_size), (2 * span, width)]
    riders = []
    if seq == 0:
        extra = pieces[0][2].shape[0] - seqs * span
        riders = [(d, seqs * span if half is None else span) for d, half, piece in pieces]
        shapes.append((len(pieces), extra, width))
    return pl.pallas_call(
        functools.partial(attend_kernel, seq, seqs, places, heads, head_size, riders),
        out_shape=tuple(jax.ShapeDtypeStruct(shape, bf16) for shape in shapes),
        grid_spec=pltpu.PrefetchScalarGridSpec(
            num_scalar_prefetch=1,
            grid=(1,),
            in_specs=[pl.BlockSpec(memory_space=pl.ANY)] * len(pieces)
            + [full(*cotangent.shape), full(*weight.shape), full(*bias.shape)],
            out_specs=[full(*shape) for shape in shapes],
            scratch_shapes=[pltpu.SemaphoreType.DMA((2 * len(pieces),))],
        ),
        compiler_params=pltpu.CompilerParams(vmem_limit_bytes=28 * 2**20),
        cost_estimate=pl.CostEstimate(
            flops=8 * 10**9, bytes_accessed=1000, transcendentals=heads * seq_len * seq_len
        ),
        name="attend",
    )(meta, *[piece for d, half, piece in pieces], cotangent, weight, bias)


def experts_kernel(static, meta, *refs):
    count, span, seqs, expert_count, capacity, seq, blocks, kinds, alias_count = static
    tokens_hbm, *pieces = refs[: 1 + len(kinds)]
    refs = refs[1 + len(kinds) :]
    gain, router_weight, ids, gain_in, out_weight, gate_weight, up_weight, down_weight = refs[:8]
    refs = refs[8 + alias_count :]
    buffers, sums_out, gain_out, refs = refs[:8], refs[8], refs[9], refs[10:]
    staged, refs = refs[:8], refs[8:]
    heads_all, mix_all, tokens_all, context_all, sems_all, in_sems_all = refs
    _, rows, width = tokens_all.shape
    each = width // count
    seq_len = span * count
    members = rows // span
    length, me = meta[seq], meta[meta.shape[0] - 1]


    def bring(number_of_block, block):
        tokens, context = tokens_all.at[number_of_block], context_all.at[number_of_block]
        cotangent, in_sems = staged[2].at[number_of_block], in_sems_all.at[number_of_block]
        tokens_copy = pltpu.make_async_copy(
            tokens_hbm.at[pl.ds(block * rows, rows), :], tokens, in_sems.at[0]
        )
        tokens_copy.start()
        lanes = pl.ds(block * members * each, members * each)
        context_copies, cotangent_copies = [], []
        for number, ((distance, half), piece) in enumerate(zip(kinds, pieces)):
            if half != 0:
                first = span if half is None else 0
                context_copies.append(
                    pltpu.make_async_copy(
                        piece.at[pl.ds(first, span), lanes],
                        context.at[distance],
                        in_sems.at[1 + 2 * number],
                    )
                )
                context_copies[-1].start()
        for number, ((distance, half), piece) in enumerate(zip(kinds, pieces)):
            if half != 1:
                owner = meta[seqs + distance]
                inside = owner // members == block
                start = pl.multiple_of(
                    jnp.where(inside, owner - block * members, 0) * span, 16
                )
                copy = pltpu.make_async_copy(
                    piece.at[pl.ds(0, span), :],
                    cotangent.at[pl.ds(start, span), :],
                    in_sems.at[2 + 2 * number],
                )
                pl.when(inside)(copy.start)
                cotangent_copies.append((inside, copy))
        return tokens_copy, context_copies, cotangent_copies

    def work(number_of_block, block, brought, staged):
        tokens_copy, context_copies, cotangent_copies = brought
        staged = [ref.at[number_of_block] for ref in staged]
        heads_out, mix_out, tokens, context = (
            ref.at[number_of_block] for ref in (heads_all, mix_all, tokens_all, context_all)
        )
        sems = sems_all.at[number_of_block]
        at_row = seq * seq_len + block * rows
        lanes = pl.ds(block * members * each, members * each)
        (
            context_out,
            normed_out,
            cotangent,
            hidden_out,
            grad_gate_out,
            grad_up_out,
            grad_out,
            logits_out,
        ) = staged
        copies = [
            pltpu.make_async_copy(source, target.at[pl.ds(at_row, rows), :], sems.at[number])
            for number, (source, target) in enumerate(zip(staged, buffers))
        ]
        heads_copy = pltpu.make_async_copy(
            heads_out, sums_out.at[:, pl.ds(0, span), lanes], sems.at[8]
        )
        mix_copies = [
            pltpu.make_async_copy(
                mix_out.at[pl.ds(part * span, span), :],
                sums_out.at[meta[seqs + count + block * members + part], pl.ds(span, span), :],
                sems.at[9 + part],
            )
            for part in range(members)
        ]

        group = seqs * span
        before = (
            lax.broadcasted_iota(jnp.int32, (group, group), 0)
            < lax.broadcasted_iota(jnp.int32, (group, group), 1)
        ).astype(bf16)
        expert_row = lax.broadcasted_iota(jnp.int32, (8, group), 0).astype(f32)
        member_lane = lax.broadcasted_iota(jnp.int32, (1, group), 1)
        codes = []
        for part in range(members):
            owner = block * members + part
            line = ids[pl.ds(meta[seqs + count + owner], 1), :]
            alive = jnp.zeros((1, group), f32)
            for other in range(seqs):
                inside = jnp.logical_and(
                    member_lane >= other * span, member_lane < (other + 1) * span
                )
                inside = jnp.logical_and(
                    inside, member_lane - other * span + owner * span < meta[other]
                )
                alive = jnp.where(inside, 1.0, alive)
            taken = jnp.logical_or(
                line[:, :group] == expert_row, line[:, group : 2 * group] == expert_row
            ).astype(f32)
            earlier = dot_nn((taken * alive).astype(bf16), before)
            code = taken * (1.0 + jnp.where(earlier < capacity, alive, 0.0))
            code = code[:, seq * span : (seq + 1) * span]
            code = jnp.concatenate([code, jnp.zeros((120, span), f32)], axis=0)
            codes.append(code.T)
        code = jnp.concatenate(codes, axis=0)

        total_units = gate_weight.shape[0]
        units = total_units // expert_count
        cuts = [slice(i, min(i + 256, total_units)) for i in range(0, total_units, 256)]
        row = block * rows + lax.broadcasted_iota(jnp.int32, (rows, 1), 0)
        own = jnp.logical_and(row >= me * span, row < (me + 1) * span)
        for copy in context_copies:
            copy.wait()
        joined = jnp.concatenate(
            [
                jnp.concatenate(
                    [context[d, :, part * each : (part + 1) * each] for d in range(count)], axis=1
                )
                for part in range(members)
            ],
            axis=0,
        )
        context_out[...] = joined
        copies[0].start()
        tokens_copy.wait()
        hidden = tokens[...].astype(f32) + dot_nn(joined, out_weight[...])
        factor = lax.rsqrt(jnp.mean(hidden * hidden, axis=-1, keepdims=True) + epsilon)
        normed = (hidden * factor * gain[...]).astype(bf16)
        normed_out[...] = normed
        copies[1].start()
        logits = dot_nn(normed, router_weight[...])
        lane = lax.broadcasted_iota(jnp.int32, logits.shape, 1)
        logits = jnp.where(lane < expert_count, logits, -1e30)
        router = jnp.exp(logits - jnp.max(logits, axis=-1, keepdims=True))
        router = router / jnp.sum(router, axis=-1, keepdims=True)
        chosen = (code > 0.5).astype(f32)
        kept = (code > 1.5).astype(f32)
        pair_total = jnp.sum(router * chosen, axis=-1, keepdims=True)
        share = router * chosen / pair_total
        scale = share * kept
        for inside, copy in cotangent_copies:
            pl.when(inside)(copy.wait)
        copies[2].start()
        upstream = jnp.where(row < length, cotangent[...].astype(f32), 0.0)
        upstream_low = upstream.astype(bf16)
        root = 0.7978845608028654
        pair_grads = jnp.zeros(logits.shape, f32)
        scale_of = [jnp.broadcast_to(scale[:, e : e + 1], (rows, 128)) for e in range(expert_count)]
        part_sums = [jnp.zeros((rows, 128), f32) for e in range(expert_count)]
        lanes = lax.broadcasted_iota(jnp.int32, (rows, 128), 1)

        def front(number):
            cut = cuts[number]
            return (
                dot_nt(normed, gate_weight[cut, :]),
                dot_nt(normed, up_weight[cut, :]),
                dot_nt(upstream_low, down_weight[cut, :]),
            )

        ready = front(0)
        for number, cut in enumerate(cuts):
            now = ready
            if number + 1 < len(cuts):
                ready = front(number + 1)
            for first in range(cut.start, cut.stop, 128):
                wide = min(128, cut.stop - first)
                inside = slice(first - cut.start, first - cut.start + wide)
                gate_in, up_in, grad_hidden = (value[:, inside] for value in now)
                square = gate_in * gate_in
                bent = gate_in * (root + (root * 0.044715) * square)
                rise = 0.5 + 0.5 * jnp.tanh(bent)
                gelu = gate_in * rise
                slope = rise + (rise - rise * rise) * (6.0 * bent - (4.0 * root) * gate_in)
                hidden_unit = gelu * up_in
                product = hidden_unit * grad_hidden
                low_expert, high_expert = first // units, (first + wide - 1) // units
                scales = scale_of[low_expert][:, :wide]
                if low_expert == high_expert:
                    if wide < 128:
                        product = jnp.pad(product, ((0, 0), (0, 128 - wide)))
                    part_sums[low_expert] = part_sums[low_expert] + product
                else:
                    under = lanes[:, :wide] < high_expert * units - first
                    scales = jnp.where(under, scales, scale_of[high_expert][:, :wide])
                    part_sums[low_expert] = part_sums[low_expert] + jnp.where(under, product, 0.0)
                    part_sums[high_expert] = part_sums[high_expert] + jnp.where(under, 0.0, product)
                scaled_grad = scales * grad_hidden
                at = slice(first, first + wide)
                hidden_out[:, at] = (scales * hidden_unit).astype(bf16)
                grad_gate_out[:, at] = (scaled_grad * up_in * slope).astype(bf16)
                grad_up_out[:, at] = (scaled_grad * gelu).astype(bf16)
        for expert in range(expert_count):
            pair_sum = jnp.sum(part_sums[expert], axis=-1, keepdims=True)
            pair_grads = jnp.where(lane == expert, pair_sum, pair_grads)
        for copy in copies[3:6]:
            copy.start()
        mix = dot_nn(hidden_out[...], down_weight[...])
        grad = dot_nn(grad_gate_out[...], gate_weight[...]) + dot_nn(grad_up_out[...], up_weight[...])
        mix_out[...] = (mix + jnp.where(own, hidden, 0.0)).astype(bf16)
        for copy in mix_copies:
            copy.start()
        pair_grads = pair_grads * kept
        weighted = jnp.sum(pair_grads * share, axis=-1, keepdims=True)
        grad_router = chosen * (pair_grads - weighted) / pair_total
        grad_logits = router * (grad_router - jnp.sum(router * grad_router, axis=-1, keepdims=True))
        grad_logits = grad_logits.astype(bf16)
        logits_out[...] = grad_logits
        copies[7].start()
        grad = grad + dot_nt(grad_logits, router_weight[...])
        spread = hidden * factor
        gain_part = jnp.sum(grad * spread, axis=0, keepdims=True)
        if number_of_block == 0:
            gain_out[...] = gain_in[...]
        gain_out[0:1, :] += gain_part
        grad = grad * gain[...]
        middle = jnp.mean(grad * hidden, axis=-1, keepdims=True) * (factor * factor)
        back = factor * grad - spread * middle + jnp.where(own, upstream, 0.0)
        back = back.astype(bf16)
        grad_out[...] = back
        copies[6].start()
        grad_heads = dot_nt(back, out_weight[...]).astype(bf16)
        for d in range(count):
            for part in range(members):
                heads_out[d, :, part * each : (part + 1) * each] = grad_heads[
                    part * span : (part + 1) * span, d * each : (d + 1) * each
                ]
        heads_copy.start()
        return [*copies, *mix_copies, heads_copy]

    brought = [bring(number, block) for number, block in enumerate(blocks)]
    started = []
    for number, block in enumerate(blocks):
        started += work(number, block, brought[number], staged)
    for copy in started:
        copy.wait()


def experts(
    meta,
    where,
    tokens,
    pieces,
    gain,
    router_weight,
    ids,
    gain_in,
    weights,
    buffers,
    sums,
    sizes,
):
    seq, blocks = where
    count, span, seqs, expert_count, capacity = sizes
    seq_len, width = tokens.shape
    units = weights[1].shape[0]
    rows = 256
    each = width // count
    members = rows // span
    many = len(blocks)
    kinds = [(d, half) for d, half, piece in pieces]
    anywhere = pl.BlockSpec(memory_space=pl.ANY)
    low = lambda *shape: jax.ShapeDtypeStruct(shape, bf16)
    columns = [width] * 3 + [units] * 3 + [width, 128]
    aliased = list(buffers or []) + ([sums] if sums is not None else [])
    first = 2 + len(pieces) + 8
    targets = ([*range(8)] if buffers else []) + ([8] if sums is not None else [])
    static = (count, span, seqs, expert_count, capacity, seq, blocks, kinds, len(aliased))
    return pl.pallas_call(
        functools.partial(experts_kernel, static),
        out_shape=[low(seqs * seq_len, cols) for cols in columns]
        + [low(count, 2 * span, width), jax.ShapeDtypeStruct((8, width), f32)],
        in_specs=[pl.BlockSpec(memory_space=pltpu.SMEM)]
        + [anywhere] * (1 + len(pieces))
        + [whole_ref] * 8
        + [anywhere] * len(aliased),
        out_specs=[anywhere] * 9 + [whole_ref],
        scratch_shapes=[pltpu.VMEM((many, rows, cols), bf16) for cols in columns]
        + [
            pltpu.VMEM((many, count, span, members * each), bf16),
            pltpu.VMEM((many, rows, width), bf16),
            pltpu.VMEM((many, rows, width), bf16),
            pltpu.VMEM((many, count, span, members * each), bf16),
            pltpu.SemaphoreType.DMA((many, 9 + members)),
            pltpu.SemaphoreType.DMA((many, 1 + 2 * len(pieces))),
        ],
        input_output_aliases={first + i: target for i, target in enumerate(targets)},
        compiler_params=pltpu.CompilerParams(vmem_limit_bytes=36 * 2**20),
        cost_estimate=pl.CostEstimate(
            flops=2 * many * rows * width * (6 * units + 2 * width),
            bytes_accessed=1000,
            transcendentals=many * rows * units,
        ),
        name="experts",
    )(
        meta,
        tokens,
        *[piece for d, half, piece in pieces],
        gain,
        router_weight,
        ids,
        gain_in,
        *weights,
        *aliased,
    )


def block_sets(blocks, seq):
    step = 1 if seq == 0 else 2
    return [list(range(i, min(i + step, blocks))) for i in range(0, blocks, step)]


def attend_back_kernel(seq, head, heads, meta, queries_in, keys_in, values_in, *refs):
    own, right, left, bias, parts_out, sums_out = refs[:6]
    table, key_sum, value_sum, summed = refs[6:]
    length = meta[seq]
    _, seq_len, head_size = keys_in.shape
    span = right.shape[0]
    each = heads * head_size
    blocks = seq_len // 128
    summed[...] = (own[0].astype(f32) + right[...].astype(f32) + left[...].astype(f32)).astype(bf16)
    table[...] = jnp.zeros_like(table)
    keys = keys_in[0]
    values = values_in[0]
    for block in range(0, blocks, 2):
        rows = slice(block * 128, block * 128 + 256)
        queries = queries_in[0, rows, :]
        firsts = [
            part * each + head * head_size
            for part in range(block * 128 // span, (block * 128 + 256) // span)
        ]
        grads = jnp.concatenate(
            [summed[:, lane : lane + head_size] for lane in firsts], axis=0
        )
        first_row = (blocks - 1 - block) * 128
        added = jnp.concatenate(
            [
                bias[0, first_row : first_row + seq_len, :],
                bias[0, first_row - 128 : first_row - 128 + seq_len, :],
            ],
            axis=1,
        )
        scores = dot_nt(keys, queries)
        row = lax.broadcasted_iota(jnp.int32, scores.shape, 0)
        scores = jnp.where(row < length, scores + added, -1e30)
        top = jnp.max(scores, axis=0, keepdims=True)
        probs = jnp.exp(scores - top)
        probs = probs * (1.0 / jnp.sum(probs, axis=0, keepdims=True))
        product = probs * dot_nt(values, grads)
        delta = jnp.sum(product, axis=0, keepdims=True)
        grad_scores = product - probs * delta
        table[first_row : first_row + seq_len, :] += grad_scores[:, :128]
        table[first_row - 128 : first_row - 128 + seq_len, :] += grad_scores[:, 128:]
        scores_low = grad_scores.astype(bf16)
        key_part = dot_nn(scores_low, queries)
        value_part = dot_nn(probs.astype(bf16), grads)
        if block == 0:
            key_sum[...] = key_part
            value_sum[...] = value_part
        else:
            key_sum[...] += key_part
            value_sum[...] += value_part
        query_grad = dot_tn(keys, scores_low) * head_size ** (-0.5)
        parts_out[0, rows, :] = query_grad.T.astype(bf16)
    parts_out[1] = key_sum[...].astype(bf16)
    parts_out[2] = value_sum[...].astype(bf16)
    width = table.shape[0] + 128
    lines = jnp.concatenate(
        [table[first : first + 128, :].T for first in range(0, width - 128, 128)]
        + [jnp.zeros((128, 128), f32)],
        axis=1,
    )
    rows = 128
    while rows > 1:
        rows //= 2
        lines = lines[:rows] + pltpu.roll(lines[rows : 2 * rows], width - rows, 1)
    sums_out[...] = jnp.broadcast_to(pltpu.roll(lines, 127, 1), sums_out.shape)


def attend_back(meta, seq, head, heads, qkv, own, right, left, span, bias):
    _, seq_len, head_size = qkv.shape
    width = right.shape[1]
    part = lambda at: pl.BlockSpec((1, seq_len, head_size), lambda i, meta: (at, 0, 0))
    full = lambda *shape: pl.BlockSpec(shape, lambda i, meta: (0,) * len(shape))
    low = jax.ShapeDtypeStruct((3, seq_len, head_size), bf16)
    return pl.pallas_call(
        functools.partial(attend_back_kernel, seq, head, heads),
        out_shape=(low, jax.ShapeDtypeStruct((8, 2 * seq_len), f32)),
        grid_spec=pltpu.PrefetchScalarGridSpec(
            num_scalar_prefetch=1,
            grid=(1,),
            in_specs=[part(head), part(heads + head), part(2 * heads + head)]
            + [full(1, span, width), full(span, width), full(span, width)]
            + [pl.BlockSpec((1,) + bias.shape[1:], lambda i, meta: (head, 0, 0))],
            out_specs=[full(3, seq_len, head_size), full(8, 2 * seq_len)],
            scratch_shapes=[
                pltpu.VMEM(bias.shape[1:], f32),
                pltpu.VMEM((seq_len, head_size), f32),
                pltpu.VMEM((seq_len, head_size), f32),
                pltpu.VMEM((span, width), bf16),
            ],
        ),
        compiler_params=pltpu.CompilerParams(vmem_limit_bytes=28 * 2**20),
        cost_estimate=pl.CostEstimate(
            flops=6 * 10**9, bytes_accessed=1000, transcendentals=seq_len * seq_len
        ),
        name="attend_back",
    )(meta, qkv, qkv, qkv, own, right, left, bias)


def norm_back_kernel(heads, first, meta, *refs):
    parts, (tokens, weight, grad_in, grad_out, parts_out, gain_out) = refs[:heads], refs[heads:]

    @pl.when(pl.program_id(0) == 0)
    def _():
        gain_out[...] = jnp.zeros_like(gain_out)

    low = jnp.concatenate([part[kind] for kind in range(3) for part in parts], axis=1)
    wide = tokens[...].astype(f32)
    factor = lax.rsqrt(jnp.mean(wide * wide, axis=-1, keepdims=True) + epsilon)
    upstream = dot_nt(low, weight[...])
    spread = wide * factor
    gain_out[0:1, :] += jnp.sum(upstream * spread, axis=0, keepdims=True)
    middle = jnp.mean(upstream * wide, axis=-1, keepdims=True) * (factor * factor)
    back = factor * upstream - spread * middle + grad_in[...].astype(f32)
    back = back.astype(bf16)
    span = grad_out.shape[1]
    members = back.shape[0] // span
    for part in range(members):
        distance = meta[first + pl.program_id(0) * members + part]
        grad_out[distance] = back[part * span : (part + 1) * span, :]
    parts_out[...] = (low.astype(f32) * factor).astype(bf16)


def norm_back(meta, seq, seqs, parts, tokens, weight, grad_in, count):
    seq_len, width = tokens.shape
    head_size = parts[0].shape[2]
    rows, span = 256, seq_len // count
    by_row = lambda cols, at=0: pl.BlockSpec((rows, cols), lambda i, meta: (at + i, 0))
    columns = 3 * head_size * len(parts)
    return pl.pallas_call(
        functools.partial(norm_back_kernel, len(parts), seqs + count),
        out_shape=(
            jax.ShapeDtypeStruct((count, span, width), bf16),
            jax.ShapeDtypeStruct((seq_len, columns), bf16),
            jax.ShapeDtypeStruct((8, width), f32),
        ),
        grid_spec=pltpu.PrefetchScalarGridSpec(
            num_scalar_prefetch=1,
            grid=(seq_len // rows,),
            in_specs=[pl.BlockSpec((3, rows, head_size), lambda i, meta: (0, i, 0))] * len(parts)
            + [
                by_row(width),
                pl.BlockSpec(weight.shape, lambda i, meta: (0, 0)),
                by_row(width, seq * (seq_len // rows)),
            ],
            out_specs=(
                pl.BlockSpec((count, span, width), lambda i, meta: (0, 0, 0)),
                by_row(columns),
                pl.BlockSpec((8, width), lambda i, meta: (0, 0)),
            ),
        ),
        compiler_params=pltpu.CompilerParams(vmem_limit_bytes=24 * 2**20),
        cost_estimate=pl.CostEstimate(
            flops=2 * seq_len * width * columns, bytes_accessed=1000, transcendentals=0
        ),
        name="norm_back",
    )(meta, *parts, tokens, weight, grad_in)


def spread_kernel(reps, spots, *refs):
    parts, gain, outs = refs[:reps], refs[reps], refs[reps + 1 :]
    count, _, columns = parts[0].shape
    cut = gain.shape[0] // reps
    each = columns // 3
    for number, part in enumerate(parts):
        rows = pl.ds(pl.multiple_of(spots[number] * cut, cut), cut)
        scale = gain[rows, :]
        for owner in range(count):
            block = part[owner, :cut, :].astype(f32) * scale
            for kind, out in enumerate(outs):
                out[rows, owner * each : (owner + 1) * each] = block[:, kind * each : (kind + 1) * each]


def spread(parts, spots, found, gain):
    count, _, columns = parts[0].shape
    cut, each = gain.shape[0] // len(parts), columns // 3
    if cut % 8:
        whole = jnp.take(jnp.stack(parts), found, axis=0)[:, :, :cut].astype(f32)
        whole = whole.reshape(len(parts), count, cut, 3, each).transpose(3, 0, 2, 1, 4)
        whole = whole.reshape(3, gain.shape[0], count * each) * gain[None, :, None]
        return whole[0], whole[1], whole[2]
    shape = jax.ShapeDtypeStruct((gain.shape[0], count * each), f32)
    return pl.pallas_call(
        functools.partial(spread_kernel, len(parts)),
        out_shape=(shape,) * 3,
        in_specs=[pl.BlockSpec(memory_space=pltpu.SMEM)] + [whole_ref] * (len(parts) + 1),
        out_specs=[whole_ref] * 3,
        compiler_params=pltpu.CompilerParams(vmem_limit_bytes=12 * 2**20),
        name="spread",
    )(spots, *parts, gain.reshape(-1, 1))


def body(
    tokens,
    lengths,
    expert_ids,
    buckets,
    norm1_gain,
    w_query,
    w_key,
    w_value,
    w_out,
    rel_bias,
    norm2_gain,
    w_router,
    w_gate,
    w_up,
    w_down,
    cotangent,
):
    seqs, span, width = tokens.shape
    count = lax.axis_size("shard")
    reps = lax.axis_size("rep")
    me = lax.axis_index("shard")
    rep = lax.axis_index("rep")
    seq_len = span * count
    expert_count, unit_count, _ = w_gate.shape
    heads = rel_bias.shape[1]
    head_size = w_query.shape[1] // (count * heads)
    each = heads * head_size
    feats = w_query.shape[0]
    cut = feats // reps
    row_count = seqs * span
    capacity = 10 * row_count // (4 * expert_count)
    place = ring_place(me, count)
    distances = jnp.arange(count, dtype=jnp.int32)
    owners = ring_index((place + distances) % count, count)
    distance_of = (ring_place(distances, count) - place) % count
    meta = jnp.concatenate([lengths, owners, distance_of, me[None]]).astype(jnp.int32)

    def line(values):
        flat = values.reshape(-1).astype(bf16)
        return jnp.pad(flat, (0, width - flat.shape[0]))[None]

    packed = jnp.concatenate(
        [
            tokens.reshape(row_count, width),
            lax.dynamic_slice_in_dim(w_out, rep * cut, cut, 0),
            line(expert_ids.reshape(row_count, 2).T),
            line(jnp.concatenate([norm2_gain, w_router.reshape(-1)])),
            jnp.zeros((14, width), bf16),
        ],
        axis=0,
    )
    extra = row_count
    token_ring = Gather(
        packed,
        count,
        lambda value: (
            jnp.concatenate([value[:span], value[extra:]], axis=0),
            value[span:extra],
        ),
    )
    hops = []
    while not token_ring.done:
        fire([token_ring])
        hops.append(token_ring.last())

    gain_one = norm1_gain.astype(f32)
    own_qkv = jnp.stack([w_query, w_key, w_value], axis=1)
    own_cut = lax.dynamic_slice_in_dim(own_qkv, rep * cut, cut, 0).astype(f32)
    own_cut = own_cut * lax.dynamic_slice_in_dim(gain_one, rep * cut, cut, 0)[:, None, None]
    own_cut = own_cut.astype(bf16).reshape(cut, 3, count, each).transpose(2, 0, 1, 3)
    qkv_weight = lax.all_to_all(
        own_cut.reshape(count, cut, 3 * each), "shard", split_axis=0, concat_axis=0, tiled=True
    )
    qkv_weight = weave(*rep_parts(after(qkv_weight, hops[1]), reps, rep))

    bucket_count = rel_bias.shape[0]
    bucket_hot = (
        buckets[:, None] == jnp.arange(bucket_count, dtype=jnp.int32)[None, :]
    ).astype(f32)
    bucket_hot = jnp.pad(bucket_hot, ((0, 1), (0, 0)))
    bias_vec = jnp.einsum("rb,bh->hr", bucket_hot, rel_bias.astype(f32), precision=highest)
    bias, bias_turned = bias_tables(bias_vec)

    def sent(rings):
        return tuple(ring.last() for ring in rings if ring.last()[0] is not None)

    attended, mixed_rings, rings = [], [], []
    waits = token_ring.last()
    for s in range(seqs):
        fire(rings, waits)
        attended.append(
            attend(
                after(meta, waits),
                s,
                seqs,
                token_ring.pieces,
                cotangent[s],
                qkv_weight,
                bias,
                heads,
                head_size,
            )
        )
        waits = (attended[s][2], sent(rings))
        if s == 0:
            riders = attended[s][3]
            out_parts = rep_parts(riders[:, :cut], reps, rep)
        mixed_rings.append(Gather(attended[s][2], count))
        rings = [mixed_rings[0]]
    while not rings[0].done:
        fire(rings, waits)
        waits = lasts(rings)

    out_weight = weave(*out_parts)
    ids = riders[:, cut].astype(f32)
    small = jnp.take(riders[:, cut + 1], distance_of, axis=0)
    gain_two = small[:, :feats].astype(f32).reshape(1, width)
    router_weight = small[:, feats : feats * (1 + expert_count)].reshape(width, expert_count)
    router_weight = jnp.pad(router_weight, ((0, 0), (0, 128 - expert_count)))
    expert_weights = [out_weight] + [
        weight.reshape(expert_count * unit_count, width) for weight in (w_gate, w_up, w_down)
    ]

    sizes = (count, span, seqs, expert_count, capacity)
    buffers = None
    gain_part = jnp.zeros((8, width), f32)
    sums_all, sum_rings = [], []
    rings = [mixed_rings[1]]
    for s in range(seqs):
        if s > 0:
            while not rings[0].done:
                fire(rings, waits)
                waits = lasts(rings)
            sum_rings.append(Sum([(sums_all[s - 1], 0, 2 * span)], count))
            rings = [sum_rings[s - 1]]
        sums = None
        for blocks in block_sets(seq_len // 256, s):
            if not rings[0].done:
                fire(rings, waits)
            *buffers, sums, gain_part = experts(
                after(meta, waits),
                (s, blocks),
                attended[s][0],
                mixed_rings[s].pieces,
                gain_two,
                router_weight,
                ids,
                gain_part,
                expert_weights,
                buffers,
                sums,
                sizes,
            )
            waits = (gain_part, sent(rings))
        sums_all.append(sums)
    context_rows, normed, cot_rows, hidden, grad_gate, grad_up, grad_rows, grad_logits = buffers

    offset_sums, totals, finished, scaled_all, gain_one_part = [], [], [], [], []

    def total_grad(left_side, right_side, waits):
        grads = dot_tn(after(left_side, waits), right_side).astype(bf16)
        totals.append(RepTotal(grads, reps, rep))
        return grads

    def step(rings, waits):
        live = [ring for ring in rings if not ring.done]
        if live:
            fire(live, waits)

    def back_head(s, head, waits):
        made = attend_back(
            after(meta, waits),
            s,
            head,
            heads,
            attended[s][1],
            sums_all[s],
            *sum_rings[s].last(),
            span,
            bias_turned,
        )
        offset_sums.append((head, made[1]))
        return made[0]

    def back_norm(s, parts, waits):
        grads, scaled, gain_rows = norm_back(
            after(meta, waits), s, seqs, parts, attended[s][0], qkv_weight, grad_rows, count
        )
        scaled_all.append(scaled)
        gain_one_part.append(gain_rows)
        return grads

    sum_rings.append(Sum([(sums_all[1], 0, 2 * span)], count))
    first, second = sum_rings
    rings = [first]
    step(rings, waits)
    done = total_grad(hidden, cot_rows, waits)
    rings = [first, second]
    waits = (done, sent(rings))
    step(rings, waits)
    out_grad = dot_tn(after(context_rows, waits), grad_rows).astype(bf16)
    router_grad = dot_tn(normed, grad_logits)[:, :expert_count]
    flat = jnp.concatenate(
        [gain_part[0].reshape(count, feats), router_grad.reshape(count, feats * expert_count)], axis=1
    ).astype(bf16)
    flat = jnp.take(flat, owners, axis=0)
    small_size = flat.shape[1] // 2
    flat = jnp.pad(flat.reshape(count, 2, 1, small_size), ((0, 0), (0, 0), (0, 15), (0, width - small_size)))
    out_whole = jnp.concatenate([out_grad.reshape(count, 2, each // 2, width), flat], axis=2)
    side = rep % 2
    out_kept = lax.dynamic_index_in_dim(out_whole, side, 1, keepdims=False)
    out_got = swap(lax.dynamic_index_in_dim(out_whole, 1 - side, 1, keepdims=False), "rep", reps, 1)
    done = total_grad(grad_gate, normed, (waits, out_grad))
    waits = (done, sent(rings))
    while not first.done:
        step(rings, waits)
        waits = lasts(rings)
    rings = [second]
    parts = []
    for head in range(heads):
        step(rings, waits)
        parts.append(back_head(0, head, waits))
        waits = (parts[-1], sent(rings))
        if head == 0:
            totals[0].cross()
            out_grad = add_low(out_kept, out_got)
            waits = waits + (totals[0].kept, out_grad)
    totals[1].cross()
    waits = waits + (totals[1].kept,)
    grads_first = back_norm(0, parts, waits)
    waits = (grads_first, waits)
    final = [Sum([(grads_first, 0, span), (out_grad, 0, out_grad.shape[1])], count)]
    rings = [second, final[0]]
    step(rings, waits)
    done = total_grad(grad_up, normed, (waits, totals[0].got))
    wide = totals[0].finish()
    waits = (done, wide, sent(rings))
    while not second.done:
        step(rings, waits)
        waits = lasts(rings)
    rings = [final[0]]
    parts = []
    for head in range(heads):
        step(rings, waits)
        parts.append(back_head(1, head, waits))
        waits = (parts[-1], sent(rings))
        if head == 0:
            totals[2].cross()
            waits = waits + (totals[2].kept,)
    step(rings, waits)
    grads_last = back_norm(1, parts, (waits, totals[1].got))
    final.append(Sum([(grads_last, 0, span)], count))
    waits = (grads_last, sent(rings))
    rings = final
    wider = None
    while not all(ring.done for ring in rings):
        step(rings, waits)
        waits = lasts(rings)
        if wider is None:
            wider = totals[1].finish()
            waits = (waits, wider)

    mix_first, mix_last, final_first, final_last = (
        total_of(ring) for ring in (*sum_rings, *final)
    )
    grad_tokens = jnp.stack([final_first[:span], final_last])
    positions = me * span + jnp.arange(span, dtype=jnp.int32)
    live_mask = (positions[None, :] < lengths[:, None]).astype(f32)[:, :, None]
    block_out = (live_mask * jnp.stack([mix_first[span:], mix_last[span:]])).astype(bf16)
    out_own = final_first[span:].astype(bf16)
    for bit in bits_of(reps)[1:]:
        out_own = add_low(out_own, swap(out_own, "rep", reps, bit))
    out_other = swap(out_own, "rep", reps, 1)
    out_both = jnp.where(
        side == 0, jnp.stack([out_own, out_other]), jnp.stack([out_other, out_own])
    ).astype(f32)
    total_out = out_both[:, : each // 2].reshape(feats, width)
    flat = out_both[:, each // 2, :small_size].reshape(-1)
    total_gain_two = flat[:feats]
    total_router = flat[feats:].reshape(feats, expert_count)

    qkv_grad = sum(dot_tn(attended[s][0], scaled_all[s]) for s in range(seqs)).astype(bf16)
    offsets = jnp.stack(
        [sum(part[0] for h, part in offset_sums if h == head) for head in range(heads)]
    )
    bias_grad = jnp.einsum("hr,rb->hb", offsets, bucket_hot, precision=highest)
    gain_rows = sum(part[0] for part in gain_one_part).reshape(count, reps, 1, cut)
    bias_rows = jnp.broadcast_to(
        bias_grad.reshape(1, reps, 1, -1), (count, reps, 1, bias_grad.size // reps)
    )
    flat = jnp.concatenate([gain_rows, bias_rows], axis=3).astype(bf16)
    flat = jnp.pad(flat, ((0, 0), (0, 0), (0, 15), (0, 3 * each - flat.shape[3])))
    qkv_grad = jnp.concatenate([qkv_grad.reshape(count, reps, cut, 3 * each), flat], axis=2)
    qkv_grad = rep_scatter(qkv_grad.transpose(1, 0, 2, 3), reps, rep, totals[2].got)
    qkv_grad = lax.all_to_all(qkv_grad, "shard", split_axis=0, concat_axis=0, tiled=True)
    bias_size = bias_grad.size // reps
    parts, spots = rep_parts(qkv_grad, reps, rep)
    found = jnp.take(jnp.array(rep_order(reps), jnp.int32), rep ^ jnp.arange(reps))
    qkv_grad = spread(parts, spots, found, gain_one)
    tail = jnp.take(jnp.stack([part[:, cut] for part in parts]), found, axis=0).astype(f32)
    total_gain_one = jnp.sum(tail[:, :, :cut], axis=1).reshape(feats) / gain_one
    total_bias = lax.dynamic_index_in_dim(tail, me, 1, keepdims=False)[:, cut : cut + bias_size]
    total_bias = total_bias.reshape(heads, bucket_count).T

    total_down, total_gate, total_up = (
        total.reshape(expert_count, unit_count, width)
        for total in (wide, wider, totals[2].finish())
    )
    return (
        block_out,
        grad_tokens,
        total_gain_one,
        qkv_grad[0],
        qkv_grad[1],
        qkv_grad[2],
        total_out,
        total_bias,
        total_gain_two,
        total_router,
        total_gate,
        total_up,
        total_down,
    )


def solution(mesh):
    rows = P("rep", "shard", None)
    first = P("shard")
    weight = P("shard", None)
    expert = P(None, "shard", None)
    return jax.shard_map(
        body,
        mesh=mesh,
        in_specs=(rows, P("rep"), rows, P(), first, weight, weight, weight, weight)
        + (P(None, "shard"), first, weight, expert, expert, expert, rows),
        out_specs=(rows, rows, first, weight, weight, weight, weight)
        + (P(None, "shard"), first, weight, expert, expert, expert),
        check_vma=False,
    )
```
